32 devices in a mesh: dp: 8 (over z, y), fsdp: 4 (over x, core).
Axes of the slice: x: 2, y: 2, z: 4, core: 2. Of those that a mesh axis runs over, the one named last changes fastest.
Arguments:
- tokens: bfloat16 [2, 32, 512, 768], P(None, ('dp', 'fsdp')), may hold values from -6 to 6
- lengths: int32 [2, 32], P(None, ('dp', 'fsdp')), may hold values from 1 to 512, 10240 in all within a row
- cotangent: bfloat16 [2, 32, 512, 768], P(None, ('dp', 'fsdp')), may hold values from -6 to 6
- query_weight: bfloat16 [768, 768], P('dp', 'fsdp'), may hold values from -0.21875 to 0.21875
- key_weight: bfloat16 [768, 768], P('dp', 'fsdp'), may hold values from -0.21875 to 0.21875
- value_weight: bfloat16 [768, 768], P('dp', 'fsdp'), may hold values from -0.21875 to 0.21875
- output_weight: bfloat16 [768, 768], P('dp', 'fsdp'), may hold values from -1.75 to 1.75
- inner_weight: bfloat16 [768, 3072], P('dp', 'fsdp'), may hold values from -0.21875 to 0.21875
- outer_weight: bfloat16 [3072, 768], P('dp', 'fsdp'), may hold values from -0.109375 to 0.109375
- bias_vectors: bfloat16 [4, 768], P(None, 'dp'), may hold values from -3 to 3
- bias_hidden: bfloat16 [3072], P('dp'), may hold values from -3 to 3
- norm_gains: bfloat16 [2, 768], P(None, 'dp'), may hold values from 0.099609375 to 1.8984375
- norm_shifts: bfloat16 [2, 768], P(None, 'dp'), may hold values from -3 to 3
Outputs:
- activations: bfloat16 [2, 32, 512, 768], P(None, ('dp', 'fsdp'))
- input_grad: bfloat16 [2, 32, 512, 768], P(None, ('dp', 'fsdp'))
- query_grad: float32 [768, 768], P('dp', 'fsdp')
- key_grad: float32 [768, 768], P('dp', 'fsdp')
- value_grad: float32 [768, 768], P('dp', 'fsdp')
- output_grad: float32 [768, 768], P('dp', 'fsdp')
- inner_grad: float32 [768, 3072], P('dp', 'fsdp')
- outer_grad: float32 [3072, 768], P('dp', 'fsdp')
- bias_grads: float32 [4, 768], P(None, 'dp')
- hidden_grad: float32 [3072], P('dp')
- gains_grad: float32 [2, 768], P(None, 'dp')
- shifts_grad: float32 [2, 768], P(None, 'dp')
The draws below stay inside these ranges and needn't reach their ends.
Inputs may be any that keep to these rules, and one draw needn't show every extreme that they name: In each micro-batch the lengths sum to 10240 and the largest is exactly 512.
All inputs are finite; a program needn't handle non-finite values. No bound on the sum of `lengths` on one device may be relied on, other than what follows from the above.
Results may differ from the reference program's by a relative error of at most 0.015.
Values may be sent and summed in bfloat16 or wider, within the bound.
No kernel may reach another device: no remote copies, remote signals or barrier semaphores. Data moves between devices by JAX's collectives and lax.ppermute only.
A program may use at most 192 MiB of HBM per device.

```python
import math
import jax
import jax.numpy as jnp
import numpy as np
from jax import lax

D = 768
HEADS = 12
HEAD_DIM = 64
FF = 3072
SEQ_LEN = 512
MICRO = 2
NSEQ = 32


def spiked(array, key, source, target, shards_of, factor):
    def block_of(axis_at):
        return (jnp.arange(array.shape[axis_at]) // (array.shape[axis_at] // shards_of)).reshape((-1,) + (1,) * (array.ndim - 1 - axis_at))

    near = jax.random.permutation(key, shards_of)[block_of(target)]
    far = (block_of(target) + shards_of // 2) % shards_of
    return jnp.where((block_of(source) == near) | (block_of(source) == far), factor * array, array)


def levels(own_key, dims, pieces, low, top_value):
    def one(axis_at, blocks):
        steps = jax.random.uniform(jax.random.fold_in(jax.random.fold_in(own_key, 6), axis_at), (blocks,), jnp.float32, low / len(pieces), top_value / len(pieces))
        return jnp.repeat(jnp.exp(steps), dims[axis_at] // blocks).reshape((-1,) + (1,) * (len(dims) - axis_at - 1))

    loudness = one(*pieces[0])
    for cut in pieces[1:]:
        loudness = loudness * one(*cut)
    return loudness


def split_up(amount, total, most, lean):
    weights = [(1 << 20) // math.isqrt(grade ** lean) + 1 for grade in range(2, amount + 1)]
    surplus, given = total - most - (amount - 1), [1] * (amount - 1)
    while surplus > 0:
        candidates = [i for i in range(amount - 1) if given[i] < most]
        pool, remaining = sum([weights[i] for i in candidates]), surplus
        for i in candidates:
            more = min(most - given[i], max(1, remaining * weights[i] // pool), surplus)
            given[i] = given[i] + more
            surplus = surplus - more
    return np.array([most] + given)


def ragged(rng, amount, total, reach, lean):
    if amount == 2:
        one = jax.random.randint(rng, (), max(1, total - reach), min(reach, total - 1) + 1)
        return jnp.stack([one, total - one])
    sizes = jnp.asarray(split_up(amount, total, reach, lean), jnp.int32)
    pairs = (amount - 1) // 2
    source_of, receiver = sizes[1:1 + 2 * pairs:2], sizes[2:2 + 2 * pairs:2]
    slack = jnp.minimum(source_of - 1, reach - receiver)
    passed = jax.random.randint(jax.random.fold_in(rng, 1), (pairs,), 0, 1 << 20) % (slack + 1)
    sizes = sizes.at[1:1 + 2 * pairs:2].set(source_of - passed).at[2:2 + 2 * pairs:2].set(receiver + passed)
    return sizes[jax.random.permutation(jax.random.fold_in(rng, 2), amount)]


def gaussian(stream_key, extent, spread, limit, split=(), kind=jnp.bfloat16):
    values = spread * jax.random.normal(stream_key, extent, jnp.float32)
    if split:
        values = values * levels(stream_key, extent, split, -0.22, 0.18)
    return jnp.clip(values, -limit, limit).astype(kind)


def noise_with(stream_key, extent, spread, bound, pieces, heavy, held_as=jnp.bfloat16):
    values = spread * jax.random.normal(stream_key, extent, jnp.float32)
    if pieces:
        values = values * levels(stream_key, extent, pieces, -0.22, 0.18)
    return jnp.clip(spiked(values, jax.random.fold_in(stream_key, 3), *heavy), -bound, bound).astype(held_as)


def setup_inputs(seed: int = 0) -> dict:
    splits = jax.random.split(jax.random.key(seed), 14)
    return {
        "tokens": noise_with(splits[0], (MICRO, NSEQ, SEQ_LEN, D), 1.0, 6.0, ((1, 32),), (1, 3, 32, 2.75)),
        "lengths": jax.vmap(lambda own: ragged(own, NSEQ, NSEQ * SEQ_LEN * 5 // 8, SEQ_LEN, 1))(jax.random.split(splits[1], MICRO)).reshape((MICRO, NSEQ)).astype(jnp.int32),
        "cotangent": gaussian(splits[2], (MICRO, NSEQ, SEQ_LEN, D), 1.0, 6.0, ((1, 32),)),
        "query_weight": gaussian(splits[3], (D, D), D ** -0.5, 0.21875, ((0, 8), (1, 4))),
        "key_weight": gaussian(splits[4], (D, D), D ** -0.5, 0.21875, ((0, 8), (1, 4))),
        "value_weight": gaussian(splits[5], (D, D), D ** -0.5, 0.21875, ((0, 8), (1, 4))),
        "output_weight": gaussian(splits[6], (D, D), (max(D // 64, 4)) ** -0.5, 1.75, ((0, 8), (1, 4))),
        "inner_weight": gaussian(splits[7], (D, FF), D ** -0.5, 0.21875, ((0, 8), (1, 4))),
        "outer_weight": gaussian(splits[8], (FF, D), FF ** -0.5, 0.109375, ((0, 8), (1, 4))),
        "bias_vectors": gaussian(splits[9], (4, D), 0.5, 3.0, ((1, 8),)),
        "bias_hidden": gaussian(splits[10], (FF,), 0.5, 3.0, ((0, 8),)),
        "norm_gains": jnp.clip(1.0 + 0.18 * jax.random.normal(splits[11], (2, D), jnp.float32), 0.099609375, 1.8984375).astype(jnp.bfloat16),
        "norm_shifts": gaussian(splits[12], (2, D), 0.5, 3.0, ((1, 8),)),
    }


@jax.custom_vjp
def low(v):
    return lax.optimization_barrier(v.astype(jnp.bfloat16)).astype(jnp.float32)

@jax.custom_vjp
def low_back(v):
    return v

def low_keep(v):
    return (low(v), None)

def low_pass(kept, grad):
    return (grad,)

def back_keep(v):
    return (v, None)

def back_low(kept, grad):
    return (low(grad),)
low.defvjp(low_keep, low_pass)
low_back.defvjp(back_keep, back_low)
EPSILON = 1e-12
MASKED = -1000000000.0

def matmul_high(left, right):
    return jnp.matmul(left, right, precision=lax.Precision.HIGHEST)

def normalize_rows(values):
    centered = values - lax.optimization_barrier(jnp.mean(values, axis=-1, keepdims=True))
    variance = lax.optimization_barrier(jnp.mean(centered * centered, axis=-1, keepdims=True))
    return centered * lax.rsqrt(variance + EPSILON)

def group_forward(params, inputs, lengths_group):
    query_weight, key_weight, value_weight, output_weight, inner_weight, outer_weight, bias_vectors, bias_hidden, norm_gains, norm_shifts = params
    seq_count = inputs.shape[0]
    visible = jnp.arange(SEQ_LEN, dtype=jnp.int32)[None, :] < lengths_group[:, None]
    shape_heads = (seq_count, SEQ_LEN, HEADS, HEAD_DIM)
    queries = low(low_back(matmul_high(inputs, query_weight) + bias_vectors[0])).reshape(shape_heads)
    keys_all = low(low_back(matmul_high(inputs, key_weight))).reshape(shape_heads)
    values_all = low(low_back(matmul_high(inputs, value_weight) + bias_vectors[1])).reshape(shape_heads)
    factor = HEAD_DIM ** (-0.5)
    scores = low_back(factor * jnp.einsum('gqhd,gkhd->ghqk', queries, keys_all, precision=lax.Precision.HIGHEST))
    scores = jnp.where(visible[:, None, None, :], scores, MASKED)
    weights_soft = low(jax.nn.softmax(scores, axis=-1))
    blended = jnp.einsum('ghqk,gkhd->gqhd', weights_soft, values_all, precision=lax.Precision.HIGHEST)
    attended = low(low_back(blended.reshape(inputs.shape)))
    branch = low_back(matmul_high(attended, output_weight) + bias_vectors[2])
    middle = normalize_rows(inputs + branch) * norm_gains[0] + norm_shifts[0]
    hidden_pre = low_back(matmul_high(low(middle), inner_weight) + bias_hidden)
    activated = low(jax.nn.gelu(hidden_pre, approximate=False))
    second = low_back(matmul_high(activated, outer_weight) + bias_vectors[3])
    result = normalize_rows(middle + second) * norm_gains[1] + norm_shifts[1]
    return result * visible[:, :, None].astype(jnp.float32)

def reference(tokens, lengths, cotangent, query_weight, key_weight, value_weight, output_weight, inner_weight, outer_weight, bias_vectors, bias_hidden, norm_gains, norm_shifts):
    params = tuple((source.astype(jnp.float32) for source in (query_weight, key_weight, value_weight, output_weight, inner_weight, outer_weight, bias_vectors, bias_hidden, norm_gains, norm_shifts)))
    seq_total = MICRO * NSEQ
    group_size = math.gcd(seq_total, max(1, 4096 // SEQ_LEN))
    group_shape = (seq_total // group_size, group_size, SEQ_LEN, D)
    grouped_tokens = tokens.astype(jnp.float32).reshape(group_shape)
    grouped_lengths = lengths.reshape(seq_total // group_size, group_size)

    def forward(weights, inputs):

        def one_group(group_pair):
            return group_forward(weights, group_pair[0], group_pair[1])
        return lax.map(jax.checkpoint(one_group), (inputs, grouped_lengths))
    outputs, pullback = jax.vjp(forward, params, grouped_tokens)
    weight_grads, input_grads = pullback(cotangent.astype(jnp.float32).reshape(group_shape))
    activations = outputs.reshape(tokens.shape).astype(jnp.bfloat16)
    input_grad = input_grads.reshape(tokens.shape).astype(jnp.bfloat16)
    return (activations, input_grad, weight_grads[0], weight_grads[1], weight_grads[2], weight_grads[3], weight_grads[4], weight_grads[5], weight_grads[6], weight_grads[7], weight_grads[8], weight_grads[9])
```

```python
import functools
import jax
import jax.numpy as jnp
from jax import lax
from jax.experimental import pallas as pl
from jax.experimental.pallas import tpu as pltpu
from jax.sharding import PartitionSpec as P

HEADS = 12


EPSILON = 1e-12
MASKED = -1000000000.0
SMALL_ROWS = 16


def swap(value, axis, bit):
    size = lax.axis_size(axis)
    return lax.ppermute(value, axis, [(i, i ^ (1 << bit)) for i in range(size)])


def stage_orders(mesh):
    dp_bits = mesh.shape["dp"].bit_length() - 1
    fsdp_bits = mesh.shape["fsdp"].bit_length() - 1
    far = [("dp", b) for b in range(dp_bits - 1, 0, -1)]
    across = [("fsdp", b) for b in range(fsdp_bits - 1, 0, -1)]
    return (far + across + [("dp", 0)], far + [("dp", 0)] + across)


def fits(mesh, row_counts, width):
    sizes = (mesh.shape["dp"], mesh.shape["fsdp"])
    powers = all(s >= 2 and s & (s - 1) == 0 for s in sizes)
    return powers and all(r % 32 == 0 for r in row_counts) and width % 64 == 0


def true_index(stages, place, mine, pair_flip):
    index = {"dp": mine["dp"], "fsdp": mine["fsdp"] ^ pair_flip}
    for s, (axis, bit) in enumerate(stages):
        index[axis] = index[axis] ^ (((place >> s) & 1) << bit)
    return index["dp"], index["fsdp"]


def gather_part(piece, stages):
    current = piece[None]
    for axis, bit in stages:
        current = jnp.concatenate([current, swap(current, axis, bit)], axis=0)
    return current, swap(current, "fsdp", 0)


def copy_list(stages, rows, mine, with_small, blocks):
    copies = []
    for flip in range(2):
        for place in range(1 << len(stages)):
            dp, fsdp = true_index(stages, place, mine, flip)
            at = 0
            for w, half in enumerate(rows):
                row = pl.multiple_of((dp * 2 + (fsdp & 1)) * half, 16)
                copies.append((flip, place, at, half, w, row, fsdp >> 1))
                at += half
            if with_small and (flip == 0 or blocks):
                copies.append((flip, place, at, SMALL_ROWS, len(rows), dp, None))
    return copies


def place_kernel(stages, rows, width, with_small, me_ref, *refs):
    sources, outs, sems = refs[:2], refs[2:-1], refs[-1]
    mine = {"dp": me_ref[0], "fsdp": me_ref[1]}
    seen, started = set(), []
    for flip, place, at, count, w, row, column in copy_list(stages, rows, mine, with_small, False):
        source = sources[flip].at[place, pl.ds(at, count), :]
        if column is None:
            across = any((place >> s) & 1 for s, (axis, _) in enumerate(stages) if axis == "fsdp")
            if across:
                continue
            target = outs[w].at[row]
        else:
            target = outs[w].at[pl.ds(row, count), pl.ds(pl.multiple_of(column * width, 128), width)]
        copy = pltpu.make_async_copy(source, target, sems.at[len(started)])
        copy.start()
        started.append(copy)
    for copy in started:
        copy.wait()


def place_part(mesh, own, other, me, stages, rows, with_small):
    width = own.shape[-1]
    dp, across = mesh.shape["dp"], mesh.shape["fsdp"] // 2
    shapes = [jax.ShapeDtypeStruct((dp * 2 * h, across * width), own.dtype) for h in rows]
    if with_small:
        shapes.append(jax.ShapeDtypeStruct((dp, SMALL_ROWS, width), own.dtype))
    anywhere = pl.BlockSpec(memory_space=pl.ANY)
    return pl.pallas_call(
        functools.partial(place_kernel, stages, rows, width, with_small),
        out_shape=tuple(shapes),
        in_specs=[pl.BlockSpec(memory_space=pltpu.SMEM), anywhere, anywhere],
        out_specs=(anywhere,) * len(shapes),
        scratch_shapes=[pltpu.SemaphoreType.DMA((2 * (1 << len(stages)) * (len(rows) + 1),))],
        name="place",
    )(me, own, other)


def cut_kernel(stages, rows, width, with_small, me_ref, *refs):
    count_in = len(rows) + with_small
    sources, outs, sems = refs[:count_in], refs[count_in:-1], refs[-1]
    mine = {"dp": me_ref[0], "fsdp": me_ref[1]}
    started = []
    for flip, place, at, count, w, row, column in copy_list(stages, rows, mine, with_small, True):
        target = outs[flip].at[place, pl.ds(at, count), :]
        if column is None:
            source = sources[w].at[row]
        else:
            source = sources[w].at[pl.ds(row, count), pl.ds(pl.multiple_of(column * width, 128), width)]
        copy = pltpu.make_async_copy(source, target, sems.at[len(started)])
        copy.start()
        started.append(copy)
    for copy in started:
        copy.wait()


def cut_part(mesh, arrays, small, me, stages, rows, width):
    total = sum(rows) + (SMALL_ROWS if small is not None else 0)
    places = 1 << len(stages)
    shape = jax.ShapeDtypeStruct((places, total, width), jnp.bfloat16)
    anywhere = pl.BlockSpec(memory_space=pl.ANY)
    operands = list(arrays) + ([small] if small is not None else [])
    return pl.pallas_call(
        functools.partial(cut_kernel, stages, rows, width, small is not None),
        out_shape=(shape, shape),
        in_specs=[pl.BlockSpec(memory_space=pltpu.SMEM)] + [anywhere] * len(operands),
        out_specs=(anywhere, anywhere),
        scratch_shapes=[pltpu.SemaphoreType.DMA((2 * places * (len(rows) + 1),))],
        name="cut",
    )(me, *operands)


def total_of(left, right, kind):
    return (left.astype(jnp.float32) + right.astype(jnp.float32)).astype(kind)


def scatter_part(keep, send, stages):
    received = swap(send, "fsdp", 0)
    for axis, bit in reversed(stages):
        half = keep.shape[0] // 2
        send = total_of(keep[half:], received[half:], jnp.bfloat16)
        arriving = swap(send, axis, bit)
        keep = total_of(keep[:half], received[:half], jnp.bfloat16)
        received = arriving
    return total_of(keep, received, jnp.float32)[0]


def settle(total, rows):
    width = total.shape[-1] // 2
    count = sum(rows)
    second = lax.axis_index("fsdp") & 1
    own = jnp.where(second == 0, total[:count, :width], total[:count, width:])
    away = jnp.where(second == 0, total[:count, width:], total[:count, :width])
    came = swap(away.astype(jnp.bfloat16), "fsdp", 0).astype(jnp.float32)
    first, last = jnp.where(second == 0, own, came), jnp.where(second == 0, came, own)
    outs, at = [], 0
    for half in rows:
        outs.append(jnp.concatenate([first[at : at + half], last[at : at + half]], axis=0))
        at += half
    return outs


def pair_up(shards):
    second = lax.axis_index("fsdp") & 1
    outs = []
    for shard in shards:
        half = shard.shape[0] // 2
        mine = jnp.where(second == 0, shard[:half], shard[half:])
        away = jnp.where(second == 0, shard[half:], shard[:half])
        came = swap(away, "fsdp", 0)
        outs.append(
            jnp.where(
                second == 0,
                jnp.concatenate([mine, came], axis=1),
                jnp.concatenate([came, mine], axis=1),
            )
        )
    return outs


def split_up(value, dim, size):
    before, after = (value.shape[:dim], value.shape[dim + 1 :])
    return jnp.moveaxis(value.reshape(*before, size, -1, *after), dim, 0)


def sum_at_owner(value, axis, dim):
    size = lax.axis_size(axis)
    parts = lax.all_to_all(split_up(value, dim, size), axis, 0, 0, tiled=True)
    return jnp.sum(parts.astype(jnp.float32), axis=0)


def side_by_side(arrays, axis, dim, along):
    ends, at = ([], 0)
    for a in arrays[:-1]:
        at += a.shape[along]
        ends.append(at)
    both = jnp.concatenate(arrays, axis=along)
    return tuple(jnp.split(sum_at_owner(both, axis, dim), ends, axis=along))


def normalize(values):
    centered = values - jnp.mean(values, axis=-1, keepdims=True)
    variance = jnp.mean(centered * centered, axis=-1, keepdims=True)
    factor = lax.rsqrt(variance + EPSILON)
    return (centered * factor, factor)


def norm_back(upward, normed, factor):
    return factor * (
        upward
        - jnp.mean(upward, axis=-1, keepdims=True)
        - normed * jnp.mean(upward * normed, axis=-1, keepdims=True)
    )


def gelu_slope(hidden_pre):
    cumulative = 0.5 * (1.0 + lax.erf(hidden_pre * 0.7071067811865476))
    return cumulative + hidden_pre * jnp.exp(-0.5 * hidden_pre * hidden_pre) * 0.3989422804014327


def outer_sum(left, right):
    return lax.dot_general(
        left, right, (((0,), (0,)), ((), ())), preferred_element_type=jnp.float32
    )


def back_product(upward, weight):
    return lax.dot_general(
        upward, weight, (((1,), (1,)), ((), ())), preferred_element_type=jnp.float32
    )


def column_sums(values):
    return jnp.sum(values.astype(jnp.float32), axis=0)


def masked_scores(queries, keys_seq, length):
    factor = queries.shape[-1] ** (-0.5)
    scores = (
        jnp.einsum("qhd,khd->hqk", queries, keys_seq, preferred_element_type=jnp.float32) * factor
    )
    visible = lax.broadcasted_iota(jnp.int32, scores.shape, 2) < length
    return (jnp.where(visible, scores, MASKED), factor)


def attend_forward(inputs):
    queries, keys_seq, values_seq, length = inputs
    scores, factor = masked_scores(queries, keys_seq, length)
    highest = jnp.max(scores, axis=-1, keepdims=True)
    exponent = jnp.exp(scores - highest)
    row_total = jnp.sum(exponent, axis=-1, keepdims=True)
    soft_low = (exponent / row_total).astype(jnp.bfloat16)
    blended = jnp.einsum("hqk,khd->qhd", soft_low, values_seq, preferred_element_type=jnp.float32)
    return (blended.reshape(blended.shape[0], -1), (highest + jnp.log(row_total))[..., 0])


def attend_backward(inputs):
    queries, keys_seq, values_seq, upward, logsum, length = inputs
    scores, factor = masked_scores(queries, keys_seq, length)
    soft = jnp.exp(scores - logsum[..., None])
    soft_low = soft.astype(jnp.bfloat16)
    upward_heads = upward.reshape(queries.shape)
    grad_soft = jnp.einsum(
        "qhd,khd->hqk", upward_heads, values_seq, preferred_element_type=jnp.float32
    )
    grad_values = jnp.einsum(
        "hqk,qhd->khd", soft_low, upward_heads, preferred_element_type=jnp.float32
    )
    inner = jnp.sum(soft * grad_soft, axis=-1, keepdims=True)
    scores_low = (soft * (grad_soft - inner)).astype(jnp.bfloat16)
    grad_queries = (
        jnp.einsum("hqk,khd->qhd", scores_low, keys_seq, preferred_element_type=jnp.float32)
        * factor
    )
    grad_keys = (
        jnp.einsum("hqk,qhd->khd", scores_low, queries, preferred_element_type=jnp.float32) * factor
    )
    row_count = queries.shape[0]
    return (
        grad_queries.reshape(row_count, -1),
        grad_keys.reshape(row_count, -1),
        grad_values.reshape(row_count, -1),
    )


def gather_forward(shards):
    (
        query_part,
        key_part,
        value_part,
        output_part,
        inner_part,
        outer_part,
        bias_part,
        hidden_part,
        gain_part,
        shift_part,
    ) = shards
    column_full = (
        lax.all_gather(query_part, "fsdp", axis=1, tiled=True),
        lax.all_gather(key_part, "fsdp", axis=1, tiled=True),
        lax.all_gather(value_part, "fsdp", axis=1, tiled=True),
        lax.all_gather(output_part, "fsdp", axis=1, tiled=True),
        lax.all_gather(inner_part, "fsdp", axis=1, tiled=True),
        lax.all_gather(outer_part, "fsdp", axis=1, tiled=True),
    )
    return (
        lax.all_gather(column_full[0], "dp", axis=0, tiled=True),
        lax.all_gather(column_full[1], "dp", axis=0, tiled=True),
        lax.all_gather(column_full[2], "dp", axis=0, tiled=True),
        lax.all_gather(column_full[3], "dp", axis=0, tiled=True),
        lax.all_gather(column_full[4], "dp", axis=0, tiled=True),
        lax.all_gather(column_full[5], "dp", axis=0, tiled=True),
        lax.all_gather(bias_part, "dp", axis=1, tiled=True),
        lax.all_gather(hidden_part, "dp", axis=0, tiled=True),
        lax.all_gather(gain_part, "dp", axis=1, tiled=True),
        lax.all_gather(shift_part, "dp", axis=1, tiled=True),
    )


def reduce_grads(grads):
    (
        query_grad,
        key_grad,
        value_grad,
        output_grad,
        inner_grad,
        outer_grad,
        bias_grad,
        hidden_grad,
        gain_grad,
        shift_grad,
    ) = grads
    bias_grad, hidden_grad, gain_grad, shift_grad = (
        lax.psum(bias_grad.astype(jnp.bfloat16), "fsdp").astype(jnp.float32),
        lax.psum(hidden_grad.astype(jnp.bfloat16), "fsdp").astype(jnp.float32),
        lax.psum(gain_grad.astype(jnp.bfloat16), "fsdp").astype(jnp.float32),
        lax.psum(shift_grad.astype(jnp.bfloat16), "fsdp").astype(jnp.float32),
    )
    narrow = (
        lax.psum_scatter(
            query_grad.astype(jnp.bfloat16), "fsdp", scatter_dimension=1, tiled=True
        ).astype(jnp.float32),
        lax.psum_scatter(
            key_grad.astype(jnp.bfloat16), "fsdp", scatter_dimension=1, tiled=True
        ).astype(jnp.float32),
        lax.psum_scatter(
            value_grad.astype(jnp.bfloat16), "fsdp", scatter_dimension=1, tiled=True
        ).astype(jnp.float32),
        lax.psum_scatter(
            output_grad.astype(jnp.bfloat16), "fsdp", scatter_dimension=1, tiled=True
        ).astype(jnp.float32),
        lax.psum_scatter(
            inner_grad.astype(jnp.bfloat16), "fsdp", scatter_dimension=1, tiled=True
        ).astype(jnp.float32),
        lax.psum_scatter(
            outer_grad.astype(jnp.bfloat16), "fsdp", scatter_dimension=1, tiled=True
        ).astype(jnp.float32),
    )
    return (
        *side_by_side(
            (
                narrow[0].astype(jnp.bfloat16),
                narrow[1].astype(jnp.bfloat16),
                narrow[2].astype(jnp.bfloat16),
                narrow[3].astype(jnp.bfloat16),
                narrow[4].astype(jnp.bfloat16),
            ),
            "dp",
            0,
            1,
        ),
        sum_at_owner(narrow[5].astype(jnp.bfloat16), "dp", 0),
        sum_at_owner(bias_grad.astype(jnp.bfloat16), "dp", 1),
        sum_at_owner(hidden_grad.astype(jnp.bfloat16), "dp", 0),
        *side_by_side(
            (gain_grad.astype(jnp.bfloat16), shift_grad.astype(jnp.bfloat16)), "dp", 1, 0
        ),
    )


def layer_step(inputs, length_row, upstream, forward_weights):
    (
        query_full,
        key_full,
        value_full,
        output_full,
        inner_full,
        outer_full,
        bias_full,
        hidden_full,
        gain_full,
        shift_full,
    ) = forward_weights
    query_back, key_back, value_back, output_back, inner_back, outer_back = forward_weights[:6]
    seq_count, seq_len, model_width = inputs.shape
    row_count = seq_count * seq_len
    flat_rows = inputs.reshape(row_count, model_width)
    row_mask = lax.broadcasted_iota(jnp.int32, (seq_count, seq_len), 1) < length_row[:, None]
    row_mask = row_mask.astype(jnp.float32).reshape(row_count, 1)
    bias_rows = bias_full.astype(jnp.float32)
    gain_rows = gain_full.astype(jnp.float32)
    shift_rows = shift_full.astype(jnp.float32)
    hidden_bias = hidden_full.astype(jnp.float32)
    shape_heads = (seq_count, seq_len, HEADS, model_width // HEADS)
    queries = (
        jnp.dot(flat_rows, query_full, preferred_element_type=jnp.float32) + bias_rows[0]
    ).astype(jnp.bfloat16)
    keys_all = jnp.dot(flat_rows, key_full, preferred_element_type=jnp.float32).astype(jnp.bfloat16)
    values_all = (
        jnp.dot(flat_rows, value_full, preferred_element_type=jnp.float32) + bias_rows[1]
    ).astype(jnp.bfloat16)
    query_heads = queries.reshape(shape_heads)
    key_heads = keys_all.reshape(shape_heads)
    value_heads = values_all.reshape(shape_heads)
    blended, logsum = lax.map(attend_forward, (query_heads, key_heads, value_heads, length_row))
    attended = blended.reshape(row_count, model_width).astype(jnp.bfloat16)
    first_sum = (
        flat_rows.astype(jnp.float32)
        + jnp.dot(attended, output_full, preferred_element_type=jnp.float32)
        + bias_rows[2]
    )
    normed_one, factor_one = normalize(first_sum)
    middle = normed_one * gain_rows[0] + shift_rows[0]
    middle_low = middle.astype(jnp.bfloat16)
    hidden_pre = jnp.dot(middle_low, inner_full, preferred_element_type=jnp.float32) + hidden_bias
    activated = jax.nn.gelu(hidden_pre, approximate=False).astype(jnp.bfloat16)
    second = (
        middle + jnp.dot(activated, outer_full, preferred_element_type=jnp.float32) + bias_rows[3]
    )
    normed_two, factor_two = normalize(second)
    outputs = ((normed_two * gain_rows[1] + shift_rows[1]) * row_mask).astype(jnp.bfloat16)
    upward = upstream.reshape(row_count, model_width).astype(jnp.float32) * row_mask
    gain_two = jnp.sum(upward * normed_two, axis=0)
    shift_two = jnp.sum(upward, axis=0)
    grad_second = norm_back(upward * gain_rows[1], normed_two, factor_two)
    second_low = grad_second.astype(jnp.bfloat16)
    outer_grad = outer_sum(activated, second_low)
    hidden_low = (back_product(second_low, outer_back) * gelu_slope(hidden_pre)).astype(
        jnp.bfloat16
    )
    inner_grad = outer_sum(middle_low, hidden_low)
    grad_middle = grad_second + back_product(hidden_low, inner_back)
    gain_one = jnp.sum(grad_middle * normed_one, axis=0)
    shift_one = jnp.sum(grad_middle, axis=0)
    grad_first = norm_back(grad_middle * gain_rows[0], normed_one, factor_one)
    branch_low = grad_first.astype(jnp.bfloat16)
    output_grad = outer_sum(attended, branch_low)
    attended_low = back_product(branch_low, output_back).astype(jnp.bfloat16)
    grad_queries, grad_keys, grad_values = lax.map(
        attend_backward,
        (
            query_heads,
            key_heads,
            value_heads,
            attended_low.reshape(seq_count, seq_len, model_width),
            logsum,
            length_row,
        ),
    )
    queries_low = grad_queries.reshape(row_count, model_width).astype(jnp.bfloat16)
    keys_low = grad_keys.reshape(row_count, model_width).astype(jnp.bfloat16)
    values_low = grad_values.reshape(row_count, model_width).astype(jnp.bfloat16)
    query_grad = outer_sum(flat_rows, queries_low)
    key_grad = outer_sum(flat_rows, keys_low)
    value_grad = outer_sum(flat_rows, values_low)
    grad_inputs = (
        grad_first
        + back_product(queries_low, query_back)
        + back_product(keys_low, key_back)
        + back_product(values_low, value_back)
    )
    bias_grad = jnp.stack(
        [
            column_sums(queries_low),
            column_sums(values_low),
            column_sums(branch_low),
            column_sums(second_low),
        ]
    )
    grads = (
        query_grad,
        key_grad,
        value_grad,
        output_grad,
        inner_grad,
        outer_grad,
        bias_grad,
        column_sums(hidden_low),
        jnp.stack([gain_one, gain_two]),
        jnp.stack([shift_one, shift_two]),
    )
    return (
        outputs.reshape(inputs.shape),
        grad_inputs.astype(jnp.bfloat16).reshape(inputs.shape),
        grads,
    )


def pack_small(bias, hidden, gains, shifts, width):
    columns = bias.shape[-1]
    rows = jnp.concatenate([bias, hidden.reshape(-1, columns), gains, shifts], axis=0)
    return jnp.pad(rows, ((0, SMALL_ROWS - rows.shape[0]), (0, width - columns)))


def unpack_small(packed, columns, hidden_count):
    split = 4 + hidden_count // columns
    lined = packed[:, :, :columns]
    whole = jnp.moveaxis(lined, 0, 1).reshape(packed.shape[1], -1)
    hidden = lined[:, 4:split].reshape(-1)
    return whole[:4], hidden, whole[split : split + 2], whole[split + 2 : split + 4]


def spread_small(bias, hidden, gains, shifts, parts, width):
    columns = bias.shape[-1] // parts

    def cut(v):
        return jnp.moveaxis(v.reshape(v.shape[0], parts, columns), 1, 0)

    rows = jnp.concatenate(
        [cut(bias), hidden.reshape(parts, -1, columns), cut(gains), cut(shifts)], axis=1
    )
    rows = rows.astype(jnp.bfloat16)
    return jnp.pad(rows, ((0, 0), (0, SMALL_ROWS - rows.shape[1]), (0, width - columns)))


def exchange_gather(mesh, shards, me):
    query, key, value, output, inner, outer, bias, hidden, gains, shifts = shards
    order_one, order_two = stage_orders(mesh)
    half, half_outer = query.shape[0] // 2, outer.shape[0] // 2
    width = 2 * query.shape[1]
    count = query.shape[0]
    small = pack_small(bias, hidden, gains, shifts, width)
    (first,) = pair_up((jnp.stack([query, key]).reshape(2, 2, half, -1).swapaxes(0, 1).reshape(4 * half, -1),))
    (second,) = pair_up((jnp.stack([value, output]).reshape(2, 2, half, -1).swapaxes(0, 1).reshape(4 * half, -1),))
    (third,) = pair_up((inner,))
    (fourth,) = pair_up((outer,))
    first = jnp.concatenate([first, small], axis=0)
    own, other = gather_part(first, order_one)
    query_full, key_full, small_full = place_part(mesh, own, other, me, order_one, (half, half), True)
    own, other = gather_part(second, order_two)
    value_full, output_full = place_part(mesh, own, other, me, order_two, (half, half), False)
    own, other = gather_part(third, order_one)
    (inner_full,) = place_part(mesh, own, other, me, order_one, (half,), False)
    own, other = gather_part(fourth, order_two)
    (outer_full,) = place_part(mesh, own, other, me, order_two, (half_outer,), False)
    vectors = unpack_small(small_full, bias.shape[1], hidden.shape[0])
    return (query_full, key_full, value_full, output_full, inner_full, outer_full, *vectors)


def exchange_scatter(mesh, grads, me, shards):
    query, key, value, output, inner, outer, bias, hidden, gains, shifts = grads
    order_one, order_two = stage_orders(mesh)
    half, half_outer = shards[0].shape[0] // 2, shards[5].shape[0] // 2
    width = 2 * shards[0].shape[1]
    columns = shards[6].shape[1]
    low = jnp.bfloat16
    keep, send = cut_part(mesh, (outer.astype(low),), None, me, order_two, (half_outer,), width)
    outer_sum_ = settle(scatter_part(keep, send, order_two), (half_outer,))[0]
    keep, send = cut_part(mesh, (inner.astype(low),), None, me, order_one, (half,), 2 * shards[4].shape[1])
    inner_sum = settle(scatter_part(keep, send, order_one), (half,))[0]
    keep, send = cut_part(
        mesh, (value.astype(low), output.astype(low)), None, me, order_two, (half, half), width
    )
    value_sum, output_sum = settle(scatter_part(keep, send, order_two), (half, half))
    small = spread_small(bias, hidden, gains, shifts, mesh.shape["dp"], width)
    keep, send = cut_part(
        mesh, (query.astype(low), key.astype(low)), small, me, order_one, (half, half), width
    )
    total = scatter_part(keep, send, order_one)
    query_sum, key_sum = settle(total, (half, half))
    rows = total[2 * half :, :columns]
    split = 4 + shards[7].shape[0] // columns
    return (
        query_sum,
        key_sum,
        value_sum,
        output_sum,
        inner_sum,
        outer_sum_,
        rows[:4],
        rows[4:split].reshape(-1),
        rows[split : split + 2],
        rows[split + 2 : split + 4],
    )


def on_device(
    mesh,
    tokens,
    lengths,
    cotangent,
    *shards,
):
    me = jnp.stack([lax.axis_index("dp"), lax.axis_index("fsdp")]).astype(jnp.int32)
    rows = (shards[0].shape[0], shards[5].shape[0])
    direct = fits(mesh, rows, shards[0].shape[1])
    weights = exchange_gather(mesh, shards, me) if direct else gather_forward(shards)
    shape = (-1, *tokens.shape[2:])
    outputs, grad_inputs, grads = layer_step(
        tokens.reshape(shape), lengths.reshape(-1), cotangent.reshape(shape), weights
    )
    totals = exchange_scatter(mesh, grads, me, shards) if direct else reduce_grads(grads)
    return (outputs.reshape(tokens.shape), grad_inputs.reshape(tokens.shape), *totals)


def solution(mesh):
    placed = (
        P(None, ("dp", "fsdp"), None, None),
        P(None, ("dp", "fsdp")),
        P(None, ("dp", "fsdp"), None, None),
        P("dp", "fsdp"),
        P("dp", "fsdp"),
        P("dp", "fsdp"),
        P("dp", "fsdp"),
        P("dp", "fsdp"),
        P("dp", "fsdp"),
        P(None, "dp"),
        P("dp"),
        P(None, "dp"),
        P(None, "dp"),
    )
    return jax.shard_map(
        functools.partial(on_device, mesh),
        mesh=mesh,
        in_specs=placed,
        out_specs=(
            P(None, ("dp", "fsdp"), None, None),
            P(None, ("dp", "fsdp"), None, None),
            P("dp", "fsdp"),
            P("dp", "fsdp"),
            P("dp", "fsdp"),
            P("dp", "fsdp"),
            P("dp", "fsdp"),
            P("dp", "fsdp"),
            P(None, "dp"),
            P("dp"),
            P(None, "dp"),
            P(None, "dp"),
        ),
        check_vma=False,
    )
```

```python
import functools
import jax
import jax.numpy as jnp
from jax import lax
from jax.experimental import pallas as pl
from jax.experimental.pallas import tpu as pltpu
from jax.sharding import PartitionSpec as P

HEADS = 12


EPSILON = 1e-12
MASKED = -1000000000.0
SMALL_ROWS = 16


def swap(value, axis, bit):
    size = lax.axis_size(axis)
    return lax.ppermute(value, axis, [(i, i ^ (1 << bit)) for i in range(size)])


def stage_orders(mesh):
    dp_bits = mesh.shape["dp"].bit_length() - 1
    fsdp_bits = mesh.shape["fsdp"].bit_length() - 1
    far = [("dp", b) for b in range(dp_bits - 1, 0, -1)]
    across = [("fsdp", b) for b in range(fsdp_bits - 1, 0, -1)]
    return (far + across + [("dp", 0)], far + [("dp", 0)] + across)


def fits(mesh, row_counts, width):
    sizes = (mesh.shape["dp"], mesh.shape["fsdp"])
    powers = all(s >= 2 and s & (s - 1) == 0 for s in sizes)
    return powers and all(r % 32 == 0 for r in row_counts) and width % 64 == 0


def true_index(stages, place, mine, pair_flip):
    index = {"dp": mine["dp"], "fsdp": mine["fsdp"] ^ pair_flip}
    for s, (axis, bit) in enumerate(stages):
        index[axis] = index[axis] ^ (((place >> s) & 1) << bit)
    return index["dp"], index["fsdp"]


def gather_part(piece, stages):
    current = piece[None]
    for axis, bit in stages:
        current = jnp.concatenate([current, swap(current, axis, bit)], axis=0)
    return current, swap(current, "fsdp", 0)


def copy_list(stages, rows, mine, with_small, blocks):
    copies = []
    for flip in range(2):
        for place in range(1 << len(stages)):
            dp, fsdp = true_index(stages, place, mine, flip)
            at = 0
            for w, half in enumerate(rows):
                row = pl.multiple_of((dp * 2 + (fsdp & 1)) * half, 16)
                copies.append((flip, place, at, half, w, row, fsdp >> 1))
                at += half
            if with_small and (flip == 0 or blocks):
                copies.append((flip, place, at, SMALL_ROWS, len(rows), dp, None))
    return copies


def place_kernel(stages, rows, width, with_small, me_ref, *refs):
    sources, outs, sems = refs[:2], refs[2:-1], refs[-1]
    mine = {"dp": me_ref[0], "fsdp": me_ref[1]}
    started = []
    for flip, place, at, count, w, row, column in copy_list(stages, rows, mine, with_small, False):
        source = sources[flip].at[place, pl.ds(at, count), :]
        if column is None:
            across = any((place >> s) & 1 for s, (axis, _) in enumerate(stages) if axis == "fsdp")
            if across:
                continue
            target = outs[w].at[row]
        else:
            target = outs[w].at[pl.ds(row, count), pl.ds(pl.multiple_of(column * width, 128), width)]
        copy = pltpu.make_async_copy(source, target, sems.at[len(started)])
        copy.start()
        started.append(copy)
    for copy in started:
        copy.wait()


def place_part(mesh, own, other, me, stages, rows, with_small):
    width = own.shape[-1]
    dp, across = mesh.shape["dp"], mesh.shape["fsdp"] // 2
    shapes = [jax.ShapeDtypeStruct((dp * 2 * h, across * width), own.dtype) for h in rows]
    if with_small:
        shapes.append(jax.ShapeDtypeStruct((dp, SMALL_ROWS, width), own.dtype))
    anywhere = pl.BlockSpec(memory_space=pl.ANY)
    return pl.pallas_call(
        functools.partial(place_kernel, stages, rows, width, with_small),
        out_shape=tuple(shapes),
        in_specs=[pl.BlockSpec(memory_space=pltpu.SMEM), anywhere, anywhere],
        out_specs=(pl.BlockSpec(memory_space=pltpu.VMEM),) * len(shapes),
        compiler_params=pltpu.CompilerParams(vmem_limit_bytes=VMEM_BYTES),
        scratch_shapes=[pltpu.SemaphoreType.DMA((2 * (1 << len(stages)) * (len(rows) + 1),))],
        name="place",
    )(me, own, other)


def cut_kernel(stages, rows, width, with_small, me_ref, *refs):
    count_in = len(rows) + with_small
    sources, outs, sems = refs[:count_in], refs[count_in:-1], refs[-1]
    mine = {"dp": me_ref[0], "fsdp": me_ref[1]}
    started = []
    for flip, place, at, count, w, row, column in copy_list(stages, rows, mine, with_small, True):
        target = outs[flip].at[place, pl.ds(at, count), :]
        if column is None:
            source = sources[w].at[row]
        else:
            source = sources[w].at[pl.ds(row, count), pl.ds(pl.multiple_of(column * width, 128), width)]
        copy = pltpu.make_async_copy(source, target, sems.at[len(started)])
        copy.start()
        started.append(copy)
    for copy in started:
        copy.wait()


def cut_part(mesh, arrays, small, me, stages, rows, width):
    total = sum(rows) + (SMALL_ROWS if small is not None else 0)
    places = 1 << len(stages)
    shape = jax.ShapeDtypeStruct((places, total, width), jnp.bfloat16)
    anywhere = pl.BlockSpec(memory_space=pl.ANY)
    operands = list(arrays) + ([small] if small is not None else [])
    return pl.pallas_call(
        functools.partial(cut_kernel, stages, rows, width, small is not None),
        out_shape=(shape, shape),
        in_specs=[pl.BlockSpec(memory_space=pltpu.SMEM)]
        + [pl.BlockSpec(memory_space=pltpu.VMEM)] * len(operands),
        out_specs=(anywhere, anywhere),
        compiler_params=pltpu.CompilerParams(vmem_limit_bytes=VMEM_BYTES),
        scratch_shapes=[pltpu.SemaphoreType.DMA((2 * places * (len(rows) + 1),))],
        name="cut",
    )(me, *operands)


def total_of(left, right, kind):
    return (left.astype(jnp.float32) + right.astype(jnp.float32)).astype(kind)


def scatter_part(keep, send, stages):
    received = swap(send, "fsdp", 0)
    for axis, bit in reversed(stages):
        half = keep.shape[0] // 2
        send = total_of(keep[half:], received[half:], jnp.bfloat16)
        arriving = swap(send, axis, bit)
        keep = total_of(keep[:half], received[:half], jnp.bfloat16)
        received = arriving
    return total_of(keep, received, jnp.float32)[0]


def settle(total, rows):
    width = total.shape[-1] // 2
    count = sum(rows)
    second = lax.axis_index("fsdp") & 1
    own = jnp.where(second == 0, total[:count, :width], total[:count, width:])
    away = jnp.where(second == 0, total[:count, width:], total[:count, :width])
    came = swap(away.astype(jnp.bfloat16), "fsdp", 0).astype(jnp.float32)
    first, last = jnp.where(second == 0, own, came), jnp.where(second == 0, came, own)
    outs, at = [], 0
    for half in rows:
        outs.append(jnp.concatenate([first[at : at + half], last[at : at + half]], axis=0))
        at += half
    return outs


def pair_up(shards):
    second = lax.axis_index("fsdp") & 1
    outs = []
    for shard in shards:
        half = shard.shape[0] // 2
        mine = jnp.where(second == 0, shard[:half], shard[half:])
        away = jnp.where(second == 0, shard[half:], shard[:half])
        came = swap(away, "fsdp", 0)
        outs.append(
            jnp.where(
                second == 0,
                jnp.concatenate([mine, came], axis=1),
                jnp.concatenate([came, mine], axis=1),
            )
        )
    return outs


VMEM_BYTES = 56 << 20


def dot(left, right):
    return jnp.dot(left, right, preferred_element_type=jnp.float32)


def dot_last(left, right):
    return lax.dot_general(
        left, right, (((1,), (1,)), ((), ())), preferred_element_type=jnp.float32
    )


def dot_first(left, right):
    return lax.dot_general(
        left, right, (((0,), (0,)), ((), ())), preferred_element_type=jnp.float32
    )


def normalize(values):
    centered = values - jnp.mean(values, axis=-1, keepdims=True)
    variance = jnp.mean(centered * centered, axis=-1, keepdims=True)
    factor = lax.rsqrt(variance + EPSILON)
    return (centered * factor, factor)


def norm_back(upward, normed, factor):
    return factor * (
        upward
        - jnp.mean(upward, axis=-1, keepdims=True)
        - normed * jnp.mean(upward * normed, axis=-1, keepdims=True)
    )


def gelu_pair(v):
    size = jnp.abs(v) * 0.7071067811865476
    t = 1.0 / (1.0 + 0.3275911 * size)
    bell = jnp.exp(-size * size)
    poly = t * (
        0.254829592
        + t * (-0.284496736 + t * (1.421413741 + t * (-1.453152027 + t * 1.061405429)))
    )
    tail = 0.5 * poly * bell
    cdf = jnp.where(v >= 0.0, 1.0 - tail, tail)
    return v * cdf, cdf + v * bell * 0.3989422804014327


def three_parts(value):
    high = value.astype(jnp.bfloat16).astype(jnp.float32)
    rest = value - high
    middle = rest.astype(jnp.bfloat16).astype(jnp.float32)
    return high, middle, rest - middle


def head_keys(pair, head, length, with_stats):
    rows, lanes = pair.shape
    lane = lax.broadcasted_iota(jnp.int32, (rows, lanes), 1)
    row = lax.broadcasted_iota(jnp.int32, (rows, lanes), 0)
    start = lanes // 2 if head == 0 else 0
    own = lane < lanes // 2 if head == 0 else lane >= lanes // 2
    hidden = jnp.where((lane == start) & (row >= length), MASKED, 0.0)
    if with_stats:
        hidden = jnp.where((lane > start) & (lane < start + 4), 1.0, hidden)
    return jnp.where(own, pair.astype(jnp.float32), hidden).astype(jnp.bfloat16)


def head_values(pair, head):
    rows, lanes = pair.shape
    lane = lax.broadcasted_iota(jnp.int32, (rows, lanes), 1)
    start = lanes // 2 if head == 0 else 0
    own = lane < lanes // 2 if head == 0 else lane >= lanes // 2
    ones = jnp.where((lane >= start) & (lane < start + 3), 1.0, 0.0)
    return jnp.where(own, pair.astype(jnp.float32), ones).astype(jnp.bfloat16)


def only_head(pair, head):
    lane = lax.broadcasted_iota(jnp.int32, pair.shape, 1)
    own = lane < pair.shape[1] // 2 if head == 0 else lane >= pair.shape[1] // 2
    return jnp.where(own, pair.astype(jnp.float32), 0.0).astype(jnp.bfloat16)


def with_rows(part, head, rows):
    count, width = part.shape
    row = lax.broadcasted_iota(jnp.int32, (count, width), 0)
    extra = jnp.zeros((count, width), jnp.float32)
    for i, value in enumerate(rows):
        extra = jnp.where(row == i, value, extra)
    extra = extra.astype(jnp.bfloat16)
    return jnp.concatenate([part, extra] if head == 0 else [extra, part], axis=0)


def forward_kernel(
    lengths, x_ref, wq_ref, wk_ref, wv_ref, wo_ref, vec_ref,
    q_ref, k_ref, v_ref, att_ref, lse_ref, first_ref, qt, vt, ot,
):
    length = lengths[pl.program_id(0)]
    x = x_ref[...]
    head_size = x.shape[1] // HEADS
    scale = head_size**-0.5
    queries = (dot(x, wq_ref[...]) + vec_ref[0:1, :]).astype(jnp.bfloat16)
    queries = (queries.astype(jnp.float32) * scale).astype(jnp.bfloat16)
    q_ref[...] = queries
    qt[...] = queries.T
    k_ref[...] = dot(x, wk_ref[...]).astype(jnp.bfloat16)
    values = (dot(x, wv_ref[...]) + vec_ref[1:2, :]).astype(jnp.bfloat16)
    v_ref[...] = values
    vt[...] = values.T

    def one_pair(p, carry):
        base = pl.multiple_of(p * 2 * head_size, 2 * head_size)
        pair = k_ref[:, pl.ds(base, 2 * head_size)]
        for head in range(2):
            at = pl.multiple_of(base + head * head_size, head_size)
            keys = head_keys(pair, head, length, False)
            scores = dot(keys, with_rows(qt[pl.ds(at, head_size), :], head, [1.0]))
            highest = jnp.max(scores, axis=0, keepdims=True)
            exponent = jnp.exp(scores - highest)
            total = jnp.sum(exponent, axis=0, keepdims=True)
            blended = dot(vt[pl.ds(at, head_size), :], exponent.astype(jnp.bfloat16))
            ot[pl.ds(at, head_size), :] = (blended / total).astype(jnp.bfloat16)
            lse_ref[p, head : head + 1, :] = highest + jnp.log(total)
        return carry

    lax.fori_loop(0, HEADS // 2, one_pair, 0)
    attended = ot[...].T
    att_ref[...] = attended
    first_ref[...] = x.astype(jnp.float32) + dot(attended, wo_ref[...]) + vec_ref[2:3, :]


def whole(shape):
    return pl.BlockSpec(shape, lambda *_: (0,) * len(shape))


def attend_forward(x, lengths, wq, wk, wv, wo, vectors):
    seqs, slots, width = x.shape
    rows = pl.BlockSpec((None, slots, width), lambda i, *_: (i, 0, 0))
    low = jax.ShapeDtypeStruct(x.shape, jnp.bfloat16)
    return pl.pallas_call(
        forward_kernel,
        grid_spec=pltpu.PrefetchScalarGridSpec(
            num_scalar_prefetch=1,
            grid=(seqs,),
            in_specs=[rows] + [whole((width, width))] * 4 + [whole(vectors.shape)],
            out_specs=[rows] * 4
            + [pl.BlockSpec((None, HEADS // 2, 2, slots), lambda i, *_: (i, 0, 0, 0)), rows],
            scratch_shapes=[pltpu.VMEM((width, slots), jnp.bfloat16)] * 3,
        ),
        out_shape=[low] * 4
        + [
            jax.ShapeDtypeStruct((seqs, HEADS // 2, 2, slots), jnp.float32),
            jax.ShapeDtypeStruct(x.shape, jnp.float32),
        ],
        compiler_params=pltpu.CompilerParams(vmem_limit_bytes=VMEM_BYTES),
        name="attend_forward",
    )(lengths, x, wq, wk, wv, wo, vectors)


def feed_kernel(
    tiles, chunk, lengths, first_ref, cot_ref, wi_ref, wo_ref, hb_ref, vec_ref,
    out_ref, act_ref, slope_ref, mid_ref, gs_ref, low_ref, sums_ref,
):
    step = pl.program_id(0)
    count = first_ref.shape[0]
    normed, _ = normalize(first_ref[...])
    middle = normed * vec_ref[4:5, :] + vec_ref[6:7, :]
    middle_low = middle.astype(jnp.bfloat16)
    mid_ref[...] = middle_low
    second = middle + vec_ref[3:4, :]
    for at in range(0, wi_ref.shape[1], chunk):
        here = slice(at, at + chunk)
        hidden = dot(middle_low, wi_ref[:, here]) + hb_ref[:, here]
        active, slope = gelu_pair(hidden)
        active = active.astype(jnp.bfloat16)
        act_ref[:, here] = active
        slope_ref[:, here] = slope.astype(jnp.bfloat16)
        second = second + dot(active, wo_ref[here, :])
    normed, factor = normalize(second)
    slot = (step % tiles) * count + lax.broadcasted_iota(jnp.int32, (count, 1), 0)
    mask = (slot < lengths[step // tiles]).astype(jnp.float32)
    out_ref[...] = ((normed * vec_ref[5:6, :] + vec_ref[7:8, :]) * mask).astype(jnp.bfloat16)
    upward = cot_ref[...].astype(jnp.float32) * mask
    grad = norm_back(upward * vec_ref[5:6, :], normed, factor)
    gs_ref[...] = grad
    low = grad.astype(jnp.bfloat16)
    low_ref[...] = low

    @pl.when(step == 0)
    def _():
        sums_ref[...] = jnp.zeros_like(sums_ref)

    sums_ref[0:1, :] += jnp.sum(upward * normed, axis=0, keepdims=True)
    sums_ref[1:2, :] += jnp.sum(upward, axis=0, keepdims=True)
    sums_ref[2:3, :] += jnp.sum(low.astype(jnp.float32), axis=0, keepdims=True)


def feed_forward(first, cotangent, lengths, wi, wo, hidden_bias, vectors):
    seqs, slots, width = first.shape
    inner = wi.shape[1]
    count = min(256, slots)
    tiles = slots // count
    total = seqs * slots
    rows = pl.BlockSpec((count, width), lambda i, *_: (i, 0))
    wide = pl.BlockSpec((count, inner), lambda i, *_: (i, 0))

    def shape(columns, kind):
        return jax.ShapeDtypeStruct((total, columns), kind)

    return pl.pallas_call(
        functools.partial(feed_kernel, tiles, min(512, inner)),
        grid_spec=pltpu.PrefetchScalarGridSpec(
            num_scalar_prefetch=1,
            grid=(seqs * tiles,),
            in_specs=[rows, rows, whole(wi.shape), whole(wo.shape), whole((1, inner)), whole(vectors.shape)],
            out_specs=[rows, wide, wide, rows, rows, rows, whole((8, width))],
        ),
        out_shape=[
            shape(width, jnp.bfloat16),
            shape(inner, jnp.bfloat16),
            shape(inner, jnp.bfloat16),
            shape(width, jnp.bfloat16),
            shape(width, jnp.float32),
            shape(width, jnp.bfloat16),
            jax.ShapeDtypeStruct((8, width), jnp.float32),
        ],
        compiler_params=pltpu.CompilerParams(vmem_limit_bytes=VMEM_BYTES),
        name="feed_forward",
    )(lengths, first.reshape(total, width), cotangent.reshape(total, width), wi, wo, hidden_bias, vectors)


def feed_back_outer_kernel(low_ref, act_ref, slope_ref, wo_ref, hid_ref, grad_ref, sum_ref):
    low = low_ref[...]
    up = dot_last(low, wo_ref[...]) * slope_ref[...].astype(jnp.float32)
    hidden = up.astype(jnp.bfloat16)
    hid_ref[...] = hidden
    sum_ref[...] = jnp.sum(hidden.astype(jnp.float32), axis=0, keepdims=True)
    grad_ref[...] = dot_first(act_ref[...], low).astype(jnp.bfloat16)


def feed_back_outer(low, act, slope, wo):
    total, width = low.shape
    inner = act.shape[1]
    chunk = min(512, inner)
    wide = pl.BlockSpec((total, chunk), lambda i: (0, i))
    tall = pl.BlockSpec((chunk, width), lambda i: (i, 0))
    return pl.pallas_call(
        feed_back_outer_kernel,
        grid=(inner // chunk,),
        in_specs=[whole((total, width)), wide, wide, tall],
        out_specs=[wide, tall, pl.BlockSpec((1, chunk), lambda i: (0, i))],
        out_shape=[
            jax.ShapeDtypeStruct((total, inner), jnp.bfloat16),
            jax.ShapeDtypeStruct((inner, width), jnp.bfloat16),
            jax.ShapeDtypeStruct((1, inner), jnp.float32),
        ],
        compiler_params=pltpu.CompilerParams(vmem_limit_bytes=VMEM_BYTES),
        name="feed_back_outer",
    )(low, act, slope, wo)


def feed_back_inner_kernel(gs_ref, mid_ref, hid_ref, wi_ref, gm_ref, grad_ref, mid_t):
    step = pl.program_id(0)

    @pl.when(step == 0)
    def _():
        gm_ref[...] = gs_ref[...]
        mid_t[...] = mid_ref[...].T

    hidden = hid_ref[...]
    grad_ref[...] = dot(mid_t[...], hidden).astype(jnp.bfloat16)
    gm_ref[...] += dot_last(hidden, wi_ref[...])


def feed_back_inner(gs, mid, hid, wi):
    total, width = mid.shape
    inner = hid.shape[1]
    chunk = min(512, inner)
    wide = pl.BlockSpec((total, chunk), lambda i: (0, i))
    flat = pl.BlockSpec((width, chunk), lambda i: (0, i))
    return pl.pallas_call(
        feed_back_inner_kernel,
        grid=(inner // chunk,),
        in_specs=[whole((total, width)), whole((total, width)), wide, flat],
        out_specs=[whole((total, width)), flat],
        out_shape=[
            jax.ShapeDtypeStruct((total, width), jnp.float32),
            jax.ShapeDtypeStruct((width, inner), jnp.bfloat16),
        ],
        scratch_shapes=[pltpu.VMEM((width, total), jnp.bfloat16)],
        compiler_params=pltpu.CompilerParams(vmem_limit_bytes=VMEM_BYTES),
        name="feed_back_inner",
    )(gs, mid, hid, wi)


def backward_kernel(
    lengths, gm_ref, first_ref, q_ref, k_ref, v_ref, att_ref, lse_ref, wo_ref, vec_ref,
    gf_ref, dq_ref, dk_ref, dv_ref, og_ref, sums_ref,
    qt, kt, at_t, do_s, do_t, dq_t, total_s,
):
    step = pl.program_id(0)
    length = lengths[step]
    slots, width = gm_ref.shape
    head_size = width // HEADS
    scale = head_size**-0.5
    grad_middle = gm_ref[...]
    normed, factor = normalize(first_ref[...])

    @pl.when(step == 0)
    def _():
        sums_ref[...] = jnp.zeros_like(sums_ref)
        total_s[...] = jnp.zeros_like(total_s)

    sums_ref[0:1, :] += jnp.sum(grad_middle * normed, axis=0, keepdims=True)
    sums_ref[1:2, :] += jnp.sum(grad_middle, axis=0, keepdims=True)
    grad_first = norm_back(grad_middle * vec_ref[4:5, :], normed, factor)
    gf_ref[...] = grad_first
    branch = grad_first.astype(jnp.bfloat16)
    sums_ref[2:3, :] += jnp.sum(branch.astype(jnp.float32), axis=0, keepdims=True)
    at_t[...] = att_ref[...].T
    total_s[...] += dot(at_t[...], branch)

    @pl.when(step == pl.num_programs(0) - 1)
    def _():
        og_ref[...] = total_s[...].astype(jnp.bfloat16)

    upward = dot_last(branch, wo_ref[...]).astype(jnp.bfloat16)
    do_s[...] = upward
    do_t[...] = upward.T
    qt[...] = q_ref[...].T
    kt[...] = k_ref[...].T

    def one_pair(p, carry):
        base = pl.multiple_of(p * 2 * head_size, 2 * head_size)
        here = pl.ds(base, 2 * head_size)
        key_pair, value_pair = k_ref[:, here], v_ref[:, here]
        query_pair, up_pair = q_ref[:, here], do_s[:, here]
        grad_keys = grad_values = None
        for head in range(2):
            at = pl.multiple_of(base + head * head_size, head_size)
            mine = pl.ds(at, head_size)
            logs = [-part for part in three_parts(lse_ref[p, head : head + 1, :])]
            keys = head_keys(key_pair, head, length, True)
            soft = jnp.exp(dot(keys, with_rows(qt[mine, :], head, [1.0] + logs)))
            up = do_t[mine, :]
            delta = jnp.sum(
                up.astype(jnp.float32) * at_t[mine, :].astype(jnp.float32), axis=0, keepdims=True
            )
            deltas = [-part for part in three_parts(delta)]
            grad_soft = dot(head_values(value_pair, head), with_rows(up, head, deltas))
            scores = (soft * grad_soft).astype(jnp.bfloat16)
            from_values = dot(soft.astype(jnp.bfloat16), only_head(up_pair, head))
            from_keys = dot(scores, only_head(query_pair, head))
            grad_values = from_values if head == 0 else grad_values + from_values
            grad_keys = from_keys if head == 0 else grad_keys + from_keys
            dq_t[mine, :] = (dot(kt[mine, :], scores) * scale).astype(jnp.bfloat16)
        dk_ref[:, here] = grad_keys.astype(jnp.bfloat16)
        dv_ref[:, here] = grad_values.astype(jnp.bfloat16)
        return carry

    lax.fori_loop(0, HEADS // 2, one_pair, 0)
    dq_ref[...] = dq_t[...].T


def attend_backward(gm, first, q, k, v, att, lse, lengths, wo, vectors):
    seqs, slots, width = q.shape
    rows = pl.BlockSpec((None, slots, width), lambda i, *_: (i, 0, 0))
    low = jax.ShapeDtypeStruct(q.shape, jnp.bfloat16)
    turned = pltpu.VMEM((width, slots), jnp.bfloat16)
    return pl.pallas_call(
        backward_kernel,
        grid_spec=pltpu.PrefetchScalarGridSpec(
            num_scalar_prefetch=1,
            grid=(seqs,),
            in_specs=[rows] * 6
            + [
                pl.BlockSpec((None, HEADS // 2, 2, slots), lambda i, *_: (i, 0, 0, 0)),
                whole((width, width)),
                whole(vectors.shape),
            ],
            out_specs=[rows] * 4 + [whole((width, width)), whole((8, width))],
            scratch_shapes=[
                turned, turned, turned, pltpu.VMEM((slots, width), jnp.bfloat16), turned, turned,
                pltpu.VMEM((width, width), jnp.float32),
            ],
        ),
        out_shape=[
            jax.ShapeDtypeStruct(q.shape, jnp.float32), low, low, low,
            jax.ShapeDtypeStruct((width, width), jnp.bfloat16),
            jax.ShapeDtypeStruct((8, width), jnp.float32),
        ],
        compiler_params=pltpu.CompilerParams(vmem_limit_bytes=VMEM_BYTES),
        name="attend_backward",
    )(lengths, gm, first, q, k, v, att, lse, wo, vectors)


def project_grads_kernel(x_ref, dq_ref, dk_ref, dv_ref, gq_ref, gk_ref, gv_ref, sums_ref, xt):
    xt[...] = x_ref[...].T
    gq_ref[...] = dot(xt[...], dq_ref[...]).astype(jnp.bfloat16)
    gk_ref[...] = dot(xt[...], dk_ref[...]).astype(jnp.bfloat16)
    gv_ref[...] = dot(xt[...], dv_ref[...]).astype(jnp.bfloat16)
    sums_ref[...] = jnp.zeros_like(sums_ref)
    sums_ref[0:1, :] = jnp.sum(dq_ref[...].astype(jnp.float32), axis=0, keepdims=True)
    sums_ref[1:2, :] = jnp.sum(dv_ref[...].astype(jnp.float32), axis=0, keepdims=True)


def project_grads(x, dq, dk, dv):
    total, width = x.shape
    grad = jax.ShapeDtypeStruct((width, width), jnp.bfloat16)
    return pl.pallas_call(
        project_grads_kernel,
        out_shape=[grad, grad, grad, jax.ShapeDtypeStruct((8, width), jnp.float32)],
        scratch_shapes=[pltpu.VMEM((width, total), jnp.bfloat16)],
        compiler_params=pltpu.CompilerParams(vmem_limit_bytes=VMEM_BYTES),
        name="project_grads",
    )(x, dq, dk, dv)


def input_grad_kernel(gf_ref, dq_ref, dk_ref, dv_ref, wq_ref, wk_ref, wv_ref, out_ref):
    grad = gf_ref[...] + dot_last(dq_ref[...], wq_ref[...])
    grad = grad + dot_last(dk_ref[...], wk_ref[...])
    grad = grad + dot_last(dv_ref[...], wv_ref[...])
    out_ref[...] = grad.astype(jnp.bfloat16)


def input_grads(gf, dq, dk, dv, wq, wk, wv):
    total, width = dq.shape
    count = min(256, total)
    rows = pl.BlockSpec((count, width), lambda i: (i, 0))
    return pl.pallas_call(
        input_grad_kernel,
        grid=(total // count,),
        in_specs=[rows] * 4 + [whole((width, width))] * 3,
        out_specs=rows,
        out_shape=jax.ShapeDtypeStruct((total, width), jnp.bfloat16),
        compiler_params=pltpu.CompilerParams(vmem_limit_bytes=VMEM_BYTES),
        name="input_grads",
    )(gf, dq, dk, dv, wq, wk, wv)


def layer_step(inputs, lengths, upstream, weights):
    wq, wk, wv, wo, wi, wf, bias, hidden, gains, shifts = weights
    shape = inputs.shape
    flat = (shape[0] * shape[1], shape[2])
    vectors = jnp.concatenate([bias, gains, shifts], axis=0).astype(jnp.float32)
    hidden_bias = hidden.astype(jnp.float32)[None]
    q, k, v, att, lse, first = attend_forward(inputs, lengths, wq, wk, wv, wo, vectors)
    outputs, act, slope, mid, gs, low, sums_two = feed_forward(
        first, upstream, lengths, wi, wf, hidden_bias, vectors
    )
    hid, outer_grad, hidden_sum = feed_back_outer(low, act, slope, wf)
    gm, inner_grad = feed_back_inner(gs, mid, hid, wi)
    gf, dq, dk, dv, output_grad, sums_one = attend_backward(
        gm.reshape(shape), first, q, k, v, att, lse, lengths, wo, vectors
    )
    dq, dk, dv = dq.reshape(flat), dk.reshape(flat), dv.reshape(flat)
    query_grad, key_grad, value_grad, sums_in = project_grads(inputs.reshape(flat), dq, dk, dv)
    input_grad = input_grads(gf.reshape(flat), dq, dk, dv, wq, wk, wv)
    bias_grad = jnp.concatenate([sums_in[:2], sums_one[2:3], sums_two[2:3]], axis=0)
    gain_grad = jnp.concatenate([sums_one[:1], sums_two[:1]], axis=0)
    shift_grad = jnp.concatenate([sums_one[1:2], sums_two[1:2]], axis=0)
    grads = (
        query_grad, key_grad, value_grad, output_grad, inner_grad, outer_grad,
        bias_grad, hidden_sum[0], gain_grad, shift_grad,
    )
    return outputs.reshape(shape), input_grad.reshape(shape), grads


def split_up(value, dim, size):
    before, after = (value.shape[:dim], value.shape[dim + 1 :])
    return jnp.moveaxis(value.reshape(*before, size, -1, *after), dim, 0)


def sum_at_owner(value, axis, dim):
    size = lax.axis_size(axis)
    parts = lax.all_to_all(split_up(value, dim, size), axis, 0, 0, tiled=True)
    return jnp.sum(parts.astype(jnp.float32), axis=0)


def side_by_side(arrays, axis, dim, along):
    ends, at = ([], 0)
    for a in arrays[:-1]:
        at += a.shape[along]
        ends.append(at)
    both = jnp.concatenate(arrays, axis=along)
    return tuple(jnp.split(sum_at_owner(both, axis, dim), ends, axis=along))


def gather_forward(shards):
    (
        query_part,
        key_part,
        value_part,
        output_part,
        inner_part,
        outer_part,
        bias_part,
        hidden_part,
        gain_part,
        shift_part,
    ) = shards
    column_full = (
        lax.all_gather(query_part, "fsdp", axis=1, tiled=True),
        lax.all_gather(key_part, "fsdp", axis=1, tiled=True),
        lax.all_gather(value_part, "fsdp", axis=1, tiled=True),
        lax.all_gather(output_part, "fsdp", axis=1, tiled=True),
        lax.all_gather(inner_part, "fsdp", axis=1, tiled=True),
        lax.all_gather(outer_part, "fsdp", axis=1, tiled=True),
    )
    return (
        lax.all_gather(column_full[0], "dp", axis=0, tiled=True),
        lax.all_gather(column_full[1], "dp", axis=0, tiled=True),
        lax.all_gather(column_full[2], "dp", axis=0, tiled=True),
        lax.all_gather(column_full[3], "dp", axis=0, tiled=True),
        lax.all_gather(column_full[4], "dp", axis=0, tiled=True),
        lax.all_gather(column_full[5], "dp", axis=0, tiled=True),
        lax.all_gather(bias_part, "dp", axis=1, tiled=True),
        lax.all_gather(hidden_part, "dp", axis=0, tiled=True),
        lax.all_gather(gain_part, "dp", axis=1, tiled=True),
        lax.all_gather(shift_part, "dp", axis=1, tiled=True),
    )


def reduce_grads(grads):
    (
        query_grad,
        key_grad,
        value_grad,
        output_grad,
        inner_grad,
        outer_grad,
        bias_grad,
        hidden_grad,
        gain_grad,
        shift_grad,
    ) = grads
    bias_grad, hidden_grad, gain_grad, shift_grad = (
        lax.psum(bias_grad.astype(jnp.bfloat16), "fsdp").astype(jnp.float32),
        lax.psum(hidden_grad.astype(jnp.bfloat16), "fsdp").astype(jnp.float32),
        lax.psum(gain_grad.astype(jnp.bfloat16), "fsdp").astype(jnp.float32),
        lax.psum(shift_grad.astype(jnp.bfloat16), "fsdp").astype(jnp.float32),
    )
    narrow = (
        lax.psum_scatter(
            query_grad.astype(jnp.bfloat16), "fsdp", scatter_dimension=1, tiled=True
        ).astype(jnp.float32),
        lax.psum_scatter(
            key_grad.astype(jnp.bfloat16), "fsdp", scatter_dimension=1, tiled=True
        ).astype(jnp.float32),
        lax.psum_scatter(
            value_grad.astype(jnp.bfloat16), "fsdp", scatter_dimension=1, tiled=True
        ).astype(jnp.float32),
        lax.psum_scatter(
            output_grad.astype(jnp.bfloat16), "fsdp", scatter_dimension=1, tiled=True
        ).astype(jnp.float32),
        lax.psum_scatter(
            inner_grad.astype(jnp.bfloat16), "fsdp", scatter_dimension=1, tiled=True
        ).astype(jnp.float32),
        lax.psum_scatter(
            outer_grad.astype(jnp.bfloat16), "fsdp", scatter_dimension=1, tiled=True
        ).astype(jnp.float32),
    )
    return (
        *side_by_side(
            (
                narrow[0].astype(jnp.bfloat16),
                narrow[1].astype(jnp.bfloat16),
                narrow[2].astype(jnp.bfloat16),
                narrow[3].astype(jnp.bfloat16),
                narrow[4].astype(jnp.bfloat16),
            ),
            "dp",
            0,
            1,
        ),
        sum_at_owner(narrow[5].astype(jnp.bfloat16), "dp", 0),
        sum_at_owner(bias_grad.astype(jnp.bfloat16), "dp", 1),
        sum_at_owner(hidden_grad.astype(jnp.bfloat16), "dp", 0),
        *side_by_side(
            (gain_grad.astype(jnp.bfloat16), shift_grad.astype(jnp.bfloat16)), "dp", 1, 0
        ),
    )


def pack_small(bias, hidden, gains, shifts, width):
    columns = bias.shape[-1]
    rows = jnp.concatenate([bias, hidden.reshape(-1, columns), gains, shifts], axis=0)
    return jnp.pad(rows, ((0, SMALL_ROWS - rows.shape[0]), (0, width - columns)))


def unpack_small(packed, columns, hidden_count):
    split = 4 + hidden_count // columns
    lined = packed[:, :, :columns]
    whole = jnp.moveaxis(lined, 0, 1).reshape(packed.shape[1], -1)
    hidden = lined[:, 4:split].reshape(-1)
    return whole[:4], hidden, whole[split : split + 2], whole[split + 2 : split + 4]


def spread_small(bias, hidden, gains, shifts, parts, width):
    columns = bias.shape[-1] // parts

    def cut(v):
        return jnp.moveaxis(v.reshape(v.shape[0], parts, columns), 1, 0)

    rows = jnp.concatenate(
        [cut(bias), hidden.reshape(parts, -1, columns), cut(gains), cut(shifts)], axis=1
    )
    rows = rows.astype(jnp.bfloat16)
    return jnp.pad(rows, ((0, 0), (0, SMALL_ROWS - rows.shape[1]), (0, width - columns)))


def exchange_gather(mesh, shards, me):
    query, key, value, output, inner, outer, bias, hidden, gains, shifts = shards
    order_one, order_two = stage_orders(mesh)
    half, half_outer = query.shape[0] // 2, outer.shape[0] // 2
    width = 2 * query.shape[1]
    count = query.shape[0]
    small = pack_small(bias, hidden, gains, shifts, width)
    (first,) = pair_up((jnp.stack([query, key]).reshape(2, 2, half, -1).swapaxes(0, 1).reshape(4 * half, -1),))
    (second,) = pair_up((jnp.stack([value, output]).reshape(2, 2, half, -1).swapaxes(0, 1).reshape(4 * half, -1),))
    (third,) = pair_up((inner,))
    (fourth,) = pair_up((outer,))
    first = jnp.concatenate([first, small], axis=0)
    own, other = gather_part(first, order_one)
    query_full, key_full, small_full = place_part(mesh, own, other, me, order_one, (half, half), True)
    own, other = gather_part(second, order_two)
    value_full, output_full = place_part(mesh, own, other, me, order_two, (half, half), False)
    own, other = gather_part(third, order_one)
    (inner_full,) = place_part(mesh, own, other, me, order_one, (half,), False)
    own, other = gather_part(fourth, order_two)
    (outer_full,) = place_part(mesh, own, other, me, order_two, (half_outer,), False)
    vectors = unpack_small(small_full, bias.shape[1], hidden.shape[0])
    return (query_full, key_full, value_full, output_full, inner_full, outer_full, *vectors)


def exchange_scatter(mesh, grads, me, shards):
    query, key, value, output, inner, outer, bias, hidden, gains, shifts = grads
    order_one, order_two = stage_orders(mesh)
    half, half_outer = shards[0].shape[0] // 2, shards[5].shape[0] // 2
    width = 2 * shards[0].shape[1]
    columns = shards[6].shape[1]
    low = jnp.bfloat16
    keep, send = cut_part(mesh, (outer.astype(low),), None, me, order_two, (half_outer,), width)
    outer_sum_ = settle(scatter_part(keep, send, order_two), (half_outer,))[0]
    keep, send = cut_part(mesh, (inner.astype(low),), None, me, order_one, (half,), 2 * shards[4].shape[1])
    inner_sum = settle(scatter_part(keep, send, order_one), (half,))[0]
    keep, send = cut_part(
        mesh, (value.astype(low), output.astype(low)), None, me, order_two, (half, half), width
    )
    value_sum, output_sum = settle(scatter_part(keep, send, order_two), (half, half))
    small = spread_small(bias, hidden, gains, shifts, mesh.shape["dp"], width)
    keep, send = cut_part(
        mesh, (query.astype(low), key.astype(low)), small, me, order_one, (half, half), width
    )
    total = scatter_part(keep, send, order_one)
    query_sum, key_sum = settle(total, (half, half))
    rows = total[2 * half :, :columns]
    split = 4 + shards[7].shape[0] // columns
    return (
        query_sum,
        key_sum,
        value_sum,
        output_sum,
        inner_sum,
        outer_sum_,
        rows[:4],
        rows[4:split].reshape(-1),
        rows[split : split + 2],
        rows[split + 2 : split + 4],
    )


def on_device(
    mesh,
    tokens,
    lengths,
    cotangent,
    *shards,
):
    me = jnp.stack([lax.axis_index("dp"), lax.axis_index("fsdp")]).astype(jnp.int32)
    rows = (shards[0].shape[0], shards[5].shape[0])
    direct = fits(mesh, rows, shards[0].shape[1])
    weights = exchange_gather(mesh, shards, me) if direct else gather_forward(shards)
    shape = (-1, *tokens.shape[2:])
    outputs, grad_inputs, grads = layer_step(
        tokens.reshape(shape), lengths.reshape(-1), cotangent.reshape(shape), weights
    )
    totals = exchange_scatter(mesh, grads, me, shards) if direct else reduce_grads(grads)
    return (outputs.reshape(tokens.shape), grad_inputs.reshape(tokens.shape), *totals)


def solution(mesh):
    placed = (
        P(None, ("dp", "fsdp"), None, None),
        P(None, ("dp", "fsdp")),
        P(None, ("dp", "fsdp"), None, None),
        P("dp", "fsdp"),
        P("dp", "fsdp"),
        P("dp", "fsdp"),
        P("dp", "fsdp"),
        P("dp", "fsdp"),
        P("dp", "fsdp"),
        P(None, "dp"),
        P("dp"),
        P(None, "dp"),
        P(None, "dp"),
    )
    return jax.shard_map(
        functools.partial(on_device, mesh),
        mesh=mesh,
        in_specs=placed,
        out_specs=(
            P(None, ("dp", "fsdp"), None, None),
            P(None, ("dp", "fsdp"), None, None),
            P("dp", "fsdp"),
            P("dp", "fsdp"),
            P("dp", "fsdp"),
            P("dp", "fsdp"),
            P("dp", "fsdp"),
            P("dp", "fsdp"),
            P(None, "dp"),
            P("dp"),
            P(None, "dp"),
            P(None, "dp"),
        ),
        check_vma=False,
    )
```

```python
import functools
import jax
import jax.numpy as jnp
from jax import lax
from jax.experimental import pallas as pl
from jax.experimental.pallas import tpu as pltpu
from jax.sharding import PartitionSpec as P

HEADS = 12


EPSILON = 1e-12
MASKED = -1000000000.0
SMALL_ROWS = 16


def swap(value, axis, bit):
    size = lax.axis_size(axis)
    return lax.ppermute(value, axis, [(i, i ^ (1 << bit)) for i in range(size)])


def stage_orders(mesh):
    dp_bits = mesh.shape["dp"].bit_length() - 1
    fsdp_bits = mesh.shape["fsdp"].bit_length() - 1
    far = [("dp", b) for b in range(dp_bits - 1, 0, -1)]
    across = [("fsdp", b) for b in range(fsdp_bits - 1, 0, -1)]
    return (far + across + [("dp", 0)], far + [("dp", 0)] + across)


def fits(mesh, row_counts, width):
    sizes = (mesh.shape["dp"], mesh.shape["fsdp"])
    powers = all(s >= 2 and s & (s - 1) == 0 for s in sizes)
    return powers and all(r % 32 == 0 for r in row_counts) and width % 64 == 0


def true_index(stages, place, mine, pair_flip):
    index = {"dp": mine["dp"], "fsdp": mine["fsdp"] ^ pair_flip}
    for s, (axis, bit) in enumerate(stages):
        index[axis] = index[axis] ^ (((place >> s) & 1) << bit)
    return index["dp"], index["fsdp"]


def copy_list(stages, rows, mine, with_small, blocks):
    copies = []
    for flip in range(2):
        for place in range(1 << len(stages)):
            dp, fsdp = true_index(stages, place, mine, flip)
            at = 0
            for w, half in enumerate(rows):
                row = pl.multiple_of((dp * 2 + (fsdp & 1)) * half, 16)
                copies.append((flip, place, at, half, w, row, fsdp >> 1))
                at += half
            if with_small and (flip == 0 or blocks):
                copies.append((flip, place, at, SMALL_ROWS, len(rows), dp, None))
    return copies


def place_kernel(stages, rows, width, with_small, me_ref, *refs):
    sources, outs, sems = refs[:2], refs[2:-1], refs[-1]
    mine = {"dp": me_ref[0], "fsdp": me_ref[1]}
    started = []
    for flip, place, at, count, w, row, column in copy_list(stages, rows, mine, with_small, False):
        source = sources[flip].at[place, pl.ds(at, count), :]
        if column is None:
            across = any((place >> s) & 1 for s, (axis, _) in enumerate(stages) if axis == "fsdp")
            if across:
                continue
            target = outs[w].at[row]
        else:
            target = outs[w].at[pl.ds(row, count), pl.ds(pl.multiple_of(column * width, 128), width)]
        copy = pltpu.make_async_copy(source, target, sems.at[len(started)])
        copy.start()
        started.append(copy)
    for copy in started:
        copy.wait()


def place_part(mesh, own, other, me, stages, rows, with_small):
    width = own.shape[-1]
    dp, across = mesh.shape["dp"], mesh.shape["fsdp"] // 2
    shapes = [jax.ShapeDtypeStruct((dp * 2 * h, across * width), own.dtype) for h in rows]
    if with_small:
        shapes.append(jax.ShapeDtypeStruct((dp, SMALL_ROWS, width), own.dtype))
    anywhere = pl.BlockSpec(memory_space=pl.ANY)
    return pl.pallas_call(
        functools.partial(place_kernel, stages, rows, width, with_small),
        out_shape=tuple(shapes),
        in_specs=[pl.BlockSpec(memory_space=pltpu.SMEM), anywhere, anywhere],
        out_specs=(pl.BlockSpec(memory_space=pltpu.VMEM),) * len(shapes),
        compiler_params=pltpu.CompilerParams(vmem_limit_bytes=VMEM_BYTES),
        scratch_shapes=[pltpu.SemaphoreType.DMA((2 * (1 << len(stages)) * (len(rows) + 1),))],
        cost_estimate=estimate(5),
        name="place",
    )(me, own, other)


def place_of(stages, dp, fsdp, me_ref):
    index = {"dp": dp ^ me_ref[0], "fsdp": fsdp ^ me_ref[1]}
    place = 0
    for s, (axis, bit) in enumerate(stages):
        place = place + (((index[axis] >> bit) & 1) << s)
    return place


def piece_copies(source, outs, sems, me_ref, stages, first_dp, count_dp, half, at, columns, width):
    copies = []
    for i in range(count_dp):
        dp = first_dp + i
        for flip in range(2):
            fsdp = (me_ref[1] & 1) ^ flip
            row = pl.multiple_of((2 * i + fsdp) * half, 16)
            for start, pair, into, count in columns:
                place = place_of(stages, dp, 2 * pair + fsdp, me_ref)
                copies.append(
                    pltpu.make_async_copy(
                        source.at[pl.ds(row, half), pl.ds(start, count)],
                        outs[flip].at[place, pl.ds(at, half), pl.ds(into, count)],
                        sems.at[len(copies)],
                    )
                )
    return copies


def small_copies(source, outs, sems, me_ref, stages, at, dp_size, pairs):
    copies = []
    for dp in range(dp_size):
        for flip in range(2):
            fsdp = (me_ref[1] & 1) ^ flip
            for pair in range(pairs):
                place = place_of(stages, dp, 2 * pair + fsdp, me_ref)
                copies.append(
                    pltpu.make_async_copy(
                        source.at[dp],
                        outs[flip].at[place, pl.ds(at, SMALL_ROWS), :],
                        sems.at[len(copies)],
                    )
                )
    return copies


def run_all(copies):
    for copy in copies:
        copy.start()
    return copies


def wait_all(copies):
    for copy in copies:
        copy.wait()


def total_of(left, right, kind):
    return (left.astype(jnp.float32) + right.astype(jnp.float32)).astype(kind)


def settle(total, rows):
    width = total.shape[-1] // 2
    count = sum(rows)
    second = lax.axis_index("fsdp") & 1
    own = jnp.where(second == 0, total[:count, :width], total[:count, width:])
    away = jnp.where(second == 0, total[:count, width:], total[:count, :width])
    came = swap(away.astype(jnp.bfloat16), "fsdp", 0).astype(jnp.float32)
    first, last = jnp.where(second == 0, own, came), jnp.where(second == 0, came, own)
    outs, at = [], 0
    for half in rows:
        outs.append(jnp.concatenate([first[at : at + half], last[at : at + half]], axis=0))
        at += half
    return outs


def pair_up(shards):
    second = lax.axis_index("fsdp") & 1
    outs = []
    for shard in shards:
        half = shard.shape[0] // 2
        mine = jnp.where(second == 0, shard[:half], shard[half:])
        away = jnp.where(second == 0, shard[half:], shard[:half])
        came = swap(away, "fsdp", 0)
        outs.append(
            jnp.where(
                second == 0,
                jnp.concatenate([mine, came], axis=1),
                jnp.concatenate([came, mine], axis=1),
            )
        )
    return outs


VMEM_BYTES = 56 << 20


def estimate(micros):
    return pl.CostEstimate(flops=micros * 1000000000, bytes_accessed=micros * 1000000, transcendentals=0)


def dot(left, right):
    return jnp.dot(left, right, preferred_element_type=jnp.float32)


def dot_last(left, right):
    return lax.dot_general(
        left, right, (((1,), (1,)), ((), ())), preferred_element_type=jnp.float32
    )


def dot_first(left, right):
    return lax.dot_general(
        left, right, (((0,), (0,)), ((), ())), preferred_element_type=jnp.float32
    )


def normalize(values):
    centered = values - jnp.mean(values, axis=-1, keepdims=True)
    variance = jnp.mean(centered * centered, axis=-1, keepdims=True)
    factor = lax.rsqrt(variance + EPSILON)
    return (centered * factor, factor)


def norm_back(upward, normed, factor):
    return factor * (
        upward
        - jnp.mean(upward, axis=-1, keepdims=True)
        - normed * jnp.mean(upward * normed, axis=-1, keepdims=True)
    )


def gelu_pair(v):
    size = jnp.abs(v) * 0.7071067811865476
    t = 1.0 / (1.0 + 0.3275911 * size)
    bell = jnp.exp(-size * size)
    poly = t * (
        0.254829592
        + t * (-0.284496736 + t * (1.421413741 + t * (-1.453152027 + t * 1.061405429)))
    )
    tail = 0.5 * poly * bell
    cdf = jnp.where(v >= 0.0, 1.0 - tail, tail)
    return v * cdf, cdf + v * bell * 0.3989422804014327


def three_parts(value):
    high = value.astype(jnp.bfloat16).astype(jnp.float32)
    rest = value - high
    middle = rest.astype(jnp.bfloat16).astype(jnp.float32)
    return high, middle, rest - middle


def head_keys(pair, head, length, with_stats):
    rows, lanes = pair.shape
    lane = lax.broadcasted_iota(jnp.int32, (rows, lanes), 1)
    row = lax.broadcasted_iota(jnp.int32, (rows, lanes), 0)
    start = lanes // 2 if head == 0 else 0
    own = lane < lanes // 2 if head == 0 else lane >= lanes // 2
    hidden = jnp.where((lane == start) & (row >= length), MASKED, 0.0)
    if with_stats:
        hidden = jnp.where((lane > start) & (lane < start + 4), 1.0, hidden)
    return jnp.where(own, pair.astype(jnp.float32), hidden).astype(jnp.bfloat16)


def head_values(pair, head):
    rows, lanes = pair.shape
    lane = lax.broadcasted_iota(jnp.int32, (rows, lanes), 1)
    start = lanes // 2 if head == 0 else 0
    own = lane < lanes // 2 if head == 0 else lane >= lanes // 2
    ones = jnp.where((lane >= start) & (lane < start + 3), 1.0, 0.0)
    return jnp.where(own, pair.astype(jnp.float32), ones).astype(jnp.bfloat16)


def only_head(pair, head):
    lane = lax.broadcasted_iota(jnp.int32, pair.shape, 1)
    own = lane < pair.shape[1] // 2 if head == 0 else lane >= pair.shape[1] // 2
    return jnp.where(own, pair.astype(jnp.float32), 0.0).astype(jnp.bfloat16)


def with_rows(part, head, rows):
    count, width = part.shape
    row = lax.broadcasted_iota(jnp.int32, (count, width), 0)
    extra = jnp.zeros((count, width), jnp.float32)
    for i, value in enumerate(rows):
        extra = jnp.where(row == i, value, extra)
    extra = extra.astype(jnp.bfloat16)
    return jnp.concatenate([part, extra] if head == 0 else [extra, part], axis=0)


def forward_kernel(
    seq, lengths, x_ref, wq_ref, wk_ref, wv_ref, wo_ref, vec_ref,
    q_ref, k_ref, v_ref, att_ref, lse_ref, first_ref, qt, vt, ot,
):
    length = lengths[seq]
    x = x_ref[...]
    head_size = x.shape[1] // HEADS
    scale = head_size**-0.5
    queries = (dot(x, wq_ref[...]) + vec_ref[0:1, :]).astype(jnp.bfloat16)
    queries = (queries.astype(jnp.float32) * scale).astype(jnp.bfloat16)
    q_ref[...] = queries
    qt[...] = queries.T
    k_ref[...] = dot(x, wk_ref[...]).astype(jnp.bfloat16)
    values = (dot(x, wv_ref[...]) + vec_ref[1:2, :]).astype(jnp.bfloat16)
    v_ref[...] = values
    vt[...] = values.T

    def one_pair(p, carry):
        base = pl.multiple_of(p * 2 * head_size, 2 * head_size)
        pair = k_ref[:, pl.ds(base, 2 * head_size)]
        for head in range(2):
            at = pl.multiple_of(base + head * head_size, head_size)
            keys = head_keys(pair, head, length, False)
            scores = dot(keys, with_rows(qt[pl.ds(at, head_size), :], head, [1.0]))
            highest = jnp.max(scores, axis=0, keepdims=True)
            exponent = jnp.exp(scores - highest)
            total = jnp.sum(exponent, axis=0, keepdims=True)
            blended = dot(vt[pl.ds(at, head_size), :], exponent.astype(jnp.bfloat16))
            ot[pl.ds(at, head_size), :] = (blended / total).astype(jnp.bfloat16)
            lse_ref[p, head : head + 1, :] = highest + jnp.log(total)
        return carry

    lax.fori_loop(0, HEADS // 2, one_pair, 0)
    attended = ot[...].T
    att_ref[...] = attended
    first_ref[...] = x.astype(jnp.float32) + dot(attended, wo_ref[...]) + vec_ref[2:3, :]


def whole(shape):
    return pl.BlockSpec(shape, lambda *_: (0,) * len(shape))


def skip_refs(kernel, first, count, *refs):
    kernel(*refs[:first], *refs[first + count :])


def attend_forward(seq, x, lengths, wq, wk, wv, wo, vectors, before):
    seqs, slots, width = x.shape
    rows = pl.BlockSpec((None, slots, width), lambda i, *_: (seq, 0, 0))
    low = jax.ShapeDtypeStruct(x.shape, jnp.bfloat16)
    inputs = (lengths, x, wq, wk, wv, wo, vectors)
    return pl.pallas_call(
        functools.partial(skip_refs, functools.partial(forward_kernel, seq), len(inputs), len(before)),
        grid_spec=pltpu.PrefetchScalarGridSpec(
            num_scalar_prefetch=1,
            grid=(1,),
            in_specs=[rows]
            + [whole((width, width))] * 4
            + [whole(vectors.shape)]
            + [pl.BlockSpec(memory_space=pl.ANY)] * len(before),
            out_specs=[rows] * 4
            + [pl.BlockSpec((None, HEADS // 2, 2, slots), lambda i, *_: (seq, 0, 0, 0)), rows],
            scratch_shapes=[pltpu.VMEM((width, slots), jnp.bfloat16)] * 3,
        ),
        out_shape=[low] * 4
        + [
            jax.ShapeDtypeStruct((seqs, HEADS // 2, 2, slots), jnp.float32),
            jax.ShapeDtypeStruct(x.shape, jnp.float32),
        ],
        input_output_aliases={len(inputs) + i: i for i in range(len(before))},
        compiler_params=pltpu.CompilerParams(vmem_limit_bytes=VMEM_BYTES),
        cost_estimate=estimate(12),
        name="attend_forward",
    )(*inputs, *before)


def feed_kernel(
    tiles, chunk, lengths, first_ref, cot_ref, wi_ref, wo_ref, hb_ref, vec_ref,
    out_ref, act_ref, slope_ref, mid_ref, gs_ref, low_ref, sums_ref,
):
    step = pl.program_id(0)
    count = first_ref.shape[0]
    normed, _ = normalize(first_ref[...])
    middle = normed * vec_ref[4:5, :] + vec_ref[6:7, :]
    middle_low = middle.astype(jnp.bfloat16)
    mid_ref[...] = middle_low
    second = middle + vec_ref[3:4, :]
    for at in range(0, wi_ref.shape[1], chunk):
        here = slice(at, at + chunk)
        hidden = dot(middle_low, wi_ref[:, here]) + hb_ref[:, here]
        active, slope = gelu_pair(hidden)
        active = active.astype(jnp.bfloat16)
        act_ref[:, here] = active
        slope_ref[:, here] = slope.astype(jnp.bfloat16)
        second = second + dot(active, wo_ref[here, :])
    normed, factor = normalize(second)
    slot = (step % tiles) * count + lax.broadcasted_iota(jnp.int32, (count, 1), 0)
    mask = (slot < lengths[step // tiles]).astype(jnp.float32)
    out_ref[...] = ((normed * vec_ref[5:6, :] + vec_ref[7:8, :]) * mask).astype(jnp.bfloat16)
    upward = cot_ref[...].astype(jnp.float32) * mask
    grad = norm_back(upward * vec_ref[5:6, :], normed, factor)
    gs_ref[...] = grad
    low = grad.astype(jnp.bfloat16)
    low_ref[...] = low

    @pl.when(step == 0)
    def _():
        sums_ref[...] = jnp.zeros_like(sums_ref)

    sums_ref[0:1, :] += jnp.sum(upward * normed, axis=0, keepdims=True)
    sums_ref[1:2, :] += jnp.sum(upward, axis=0, keepdims=True)
    sums_ref[2:3, :] += jnp.sum(low.astype(jnp.float32), axis=0, keepdims=True)


def feed_forward(first, cotangent, lengths, wi, wo, hidden_bias, vectors):
    seqs, slots, width = first.shape
    inner = wi.shape[1]
    count = min(256, slots)
    tiles = slots // count
    total = seqs * slots
    rows = pl.BlockSpec((count, width), lambda i, *_: (i, 0))
    wide = pl.BlockSpec((count, inner), lambda i, *_: (i, 0))

    def shape(columns, kind):
        return jax.ShapeDtypeStruct((total, columns), kind)

    return pl.pallas_call(
        functools.partial(feed_kernel, tiles, min(512, inner)),
        grid_spec=pltpu.PrefetchScalarGridSpec(
            num_scalar_prefetch=1,
            grid=(seqs * tiles,),
            in_specs=[rows, rows, whole(wi.shape), whole(wo.shape), whole((1, inner)), whole(vectors.shape)],
            out_specs=[rows, wide, wide, rows, rows, rows, whole((8, width))],
        ),
        out_shape=[
            shape(width, jnp.bfloat16),
            shape(inner, jnp.bfloat16),
            shape(inner, jnp.bfloat16),
            shape(width, jnp.bfloat16),
            shape(width, jnp.float32),
            shape(width, jnp.bfloat16),
            jax.ShapeDtypeStruct((8, width), jnp.float32),
        ],
        compiler_params=pltpu.CompilerParams(vmem_limit_bytes=VMEM_BYTES),
        cost_estimate=estimate(32),
        name="feed_forward",
    )(lengths, first.reshape(total, width), cotangent.reshape(total, width), wi, wo, hidden_bias, vectors)


def feed_back_outer_kernel(cut, me_ref, low_ref, act_ref, slope_ref, wo_ref, hid_ref, sum_ref, *rest):
    low = low_ref[...]
    up = dot_last(low, wo_ref[...]) * slope_ref[...].astype(jnp.float32)
    hidden = up.astype(jnp.bfloat16)
    hid_ref[...] = hidden
    sum_ref[...] = jnp.sum(hidden.astype(jnp.float32), axis=0, keepdims=True)
    grad = dot_first(act_ref[...], low).astype(jnp.bfloat16)
    if cut is None:
        rest[0][...] = grad
        return
    outs, held, sems = rest[:2], rest[2], rest[3]
    step = pl.program_id(0)
    slot = step % 2
    chunk = grad.shape[0]
    blocks = chunk // (2 * cut.half)
    width = outs[0].shape[2]
    columns = [(p * width, p, 0, width) for p in range(grad.shape[1] // width)]

    def copies(at_step):
        return piece_copies(
            held.at[at_step % 2], outs, sems.at[at_step % 2], me_ref, cut.stages,
            at_step * blocks, blocks, cut.half, 0, columns, width,
        )

    @pl.when(step >= 2)
    def _():
        wait_all(copies(step - 2))

    held[slot] = grad
    run_all(copies(step))

    @pl.when(step == pl.num_programs(0) - 1)
    def _():
        if pl.num_programs(0) > 1:
            wait_all(copies(step - 1))
        wait_all(copies(step))


class Cut:
    def __init__(self, stages, half, rows, width):
        self.stages, self.half, self.rows, self.width = tuple(stages), half, rows, width
        self.places = 1 << len(stages)

    def shapes(self):
        return [jax.ShapeDtypeStruct((self.places, self.rows, self.width), jnp.bfloat16)] * 2


ANYWHERE = pl.BlockSpec(memory_space=pl.ANY)
SCALARS = pl.BlockSpec(memory_space=pltpu.SMEM)


def feed_back_outer(me, low, act, slope, wo, cut):
    total, width = low.shape
    inner = act.shape[1]
    chunk = min(768, inner)
    wide = pl.BlockSpec((total, chunk), lambda i: (0, i))
    tall = pl.BlockSpec((chunk, width), lambda i: (i, 0))
    direct = cut is not None
    grads = cut.shapes() if direct else [jax.ShapeDtypeStruct((inner, width), jnp.bfloat16)]
    copies = 2 * (chunk // (2 * cut.half)) * (width // cut.width) if direct else 1
    scratch = [pltpu.VMEM((2, chunk, width), jnp.bfloat16), pltpu.SemaphoreType.DMA((2, copies))]
    return pl.pallas_call(
        functools.partial(feed_back_outer_kernel, cut),
        grid=(inner // chunk,),
        in_specs=[SCALARS, whole((total, width)), wide, wide, tall],
        out_specs=[wide, pl.BlockSpec((1, chunk), lambda i: (0, i))]
        + ([ANYWHERE] * 2 if direct else [tall]),
        out_shape=[
            jax.ShapeDtypeStruct((total, inner), jnp.bfloat16),
            jax.ShapeDtypeStruct((1, inner), jnp.float32),
            *grads,
        ],
        scratch_shapes=scratch if direct else [],
        compiler_params=pltpu.CompilerParams(vmem_limit_bytes=VMEM_BYTES),
        cost_estimate=estimate(15),
        name="feed_back_outer",
    )(me, low, act, slope, wo)


def feed_back_inner_kernel(cut, me_ref, gs_ref, mid_ref, hid_ref, wi_ref, gm_ref, *rest):
    step = pl.program_id(0)
    mid_t = rest[-1]

    @pl.when(step == 0)
    def _():
        gm_ref[...] = gs_ref[...]
        mid_t[...] = mid_ref[...].T

    hidden = hid_ref[...]
    grad = dot(mid_t[...], hidden).astype(jnp.bfloat16)
    if cut is None:
        rest[0][...] = grad
        gm_ref[...] += dot_last(hidden, wi_ref[...])
        return
    outs, held, sems = rest[:2], rest[2], rest[3]
    rows, chunk = grad.shape
    parts = cut.width // chunk
    blocks = rows // (2 * cut.half)

    def copies(at_step):
        columns = [(0, at_step // parts, pl.multiple_of(at_step % parts * chunk, 128), chunk)]
        return piece_copies(
            held.at[at_step % 2], outs, sems.at[at_step % 2], me_ref, cut.stages,
            0, blocks, cut.half, 0, columns, chunk,
        )

    @pl.when(step >= 2)
    def _():
        wait_all(copies(step - 2))

    held[step % 2] = grad
    run_all(copies(step))
    gm_ref[...] += dot_last(hidden, wi_ref[...])

    @pl.when(step == pl.num_programs(0) - 1)
    def _():
        if pl.num_programs(0) > 1:
            wait_all(copies(step - 1))
        wait_all(copies(step))


def feed_back_inner(me, gs, mid, hid, wi, cut):
    total, width = mid.shape
    inner = hid.shape[1]
    chunk = min(768, inner)
    wide = pl.BlockSpec((total, chunk), lambda i: (0, i))
    flat = pl.BlockSpec((width, chunk), lambda i: (0, i))
    direct = cut is not None
    grads = cut.shapes() if direct else [jax.ShapeDtypeStruct((width, inner), jnp.bfloat16)]
    scratch = [
        pltpu.VMEM((2, width, chunk), jnp.bfloat16),
        pltpu.SemaphoreType.DMA((2, width // cut.half if direct else 1)),
    ]
    return pl.pallas_call(
        functools.partial(feed_back_inner_kernel, cut),
        grid=(inner // chunk,),
        in_specs=[SCALARS, whole((total, width)), whole((total, width)), wide, flat],
        out_specs=[whole((total, width))] + ([ANYWHERE] * 2 if direct else [flat]),
        out_shape=[jax.ShapeDtypeStruct((total, width), jnp.float32), *grads],
        scratch_shapes=(scratch if direct else []) + [pltpu.VMEM((width, total), jnp.bfloat16)],
        compiler_params=pltpu.CompilerParams(vmem_limit_bytes=VMEM_BYTES),
        cost_estimate=estimate(16),
        name="feed_back_inner",
    )(me, gs, mid, hid, wi)


def backward_kernel(
    seq, lengths, gm_ref, first_ref, q_ref, k_ref, v_ref, att_ref, lse_ref, wo_ref, vec_ref,
    *rest,
):
    gf_ref, dq_ref, dk_ref, dv_ref, og_ref, sums_ref, qt, kt, at_t, do_s, do_t, dq_t = rest[-12:]
    totals_before = rest[:-12]
    length = lengths[seq]
    slots, width = gm_ref.shape
    head_size = width // HEADS
    scale = head_size**-0.5
    grad_middle = gm_ref[...]
    normed, factor = normalize(first_ref[...])

    sums_ref[...] = totals_before[1][...] if totals_before else jnp.zeros_like(sums_ref)
    sums_ref[0:1, :] += jnp.sum(grad_middle * normed, axis=0, keepdims=True)
    sums_ref[1:2, :] += jnp.sum(grad_middle, axis=0, keepdims=True)
    grad_first = norm_back(grad_middle * vec_ref[4:5, :], normed, factor)
    gf_ref[...] = grad_first
    branch = grad_first.astype(jnp.bfloat16)
    sums_ref[2:3, :] += jnp.sum(branch.astype(jnp.float32), axis=0, keepdims=True)
    at_t[...] = att_ref[...].T
    output_grad = dot(at_t[...], branch)
    og_ref[...] = totals_before[0][...] + output_grad if totals_before else output_grad
    upward = dot_last(branch, wo_ref[...]).astype(jnp.bfloat16)
    do_s[...] = upward
    do_t[...] = upward.T
    qt[...] = q_ref[...].T
    kt[...] = k_ref[...].T

    def one_pair(p, carry):
        base = pl.multiple_of(p * 2 * head_size, 2 * head_size)
        here = pl.ds(base, 2 * head_size)
        key_pair, value_pair = k_ref[:, here], v_ref[:, here]
        query_pair, up_pair = q_ref[:, here], do_s[:, here]
        grad_keys = grad_values = None
        for head in range(2):
            at = pl.multiple_of(base + head * head_size, head_size)
            mine = pl.ds(at, head_size)
            logs = [-part for part in three_parts(lse_ref[p, head : head + 1, :])]
            keys = head_keys(key_pair, head, length, True)
            soft = jnp.exp(dot(keys, with_rows(qt[mine, :], head, [1.0] + logs)))
            up = do_t[mine, :]
            delta = jnp.sum(
                up.astype(jnp.float32) * at_t[mine, :].astype(jnp.float32), axis=0, keepdims=True
            )
            deltas = [-part for part in three_parts(delta)]
            grad_soft = dot(head_values(value_pair, head), with_rows(up, head, deltas))
            scores = (soft * grad_soft).astype(jnp.bfloat16)
            from_values = dot(soft.astype(jnp.bfloat16), only_head(up_pair, head))
            from_keys = dot(scores, only_head(query_pair, head))
            grad_values = from_values if head == 0 else grad_values + from_values
            grad_keys = from_keys if head == 0 else grad_keys + from_keys
            dq_t[mine, :] = (dot(kt[mine, :], scores) * scale).astype(jnp.bfloat16)
        dk_ref[:, here] = grad_keys.astype(jnp.bfloat16)
        dv_ref[:, here] = grad_values.astype(jnp.bfloat16)
        return carry

    lax.fori_loop(0, HEADS // 2, one_pair, 0)
    dq_ref[...] = dq_t[...].T
    sums_ref[3:4, :] += jnp.sum(dq_ref[...].astype(jnp.float32), axis=0, keepdims=True)
    sums_ref[4:5, :] += jnp.sum(dv_ref[...].astype(jnp.float32), axis=0, keepdims=True)


def attend_backward(seq, gm, first, q, k, v, att, lse, lengths, wo, vectors, totals, before):
    seqs, slots, width = q.shape
    rows = pl.BlockSpec((None, slots, width), lambda i, *_: (seq, 0, 0))
    low = jax.ShapeDtypeStruct(q.shape, jnp.bfloat16)
    turned = pltpu.VMEM((width, slots), jnp.bfloat16)
    inputs = (lengths, gm, first, q, k, v, att, lse, wo, vectors, *totals)
    return pl.pallas_call(
        functools.partial(skip_refs, functools.partial(backward_kernel, seq), len(inputs), len(before)),
        grid_spec=pltpu.PrefetchScalarGridSpec(
            num_scalar_prefetch=1,
            grid=(1,),
            in_specs=[rows] * 6
            + [
                pl.BlockSpec((None, HEADS // 2, 2, slots), lambda i, *_: (seq, 0, 0, 0)),
                whole((width, width)),
                whole(vectors.shape),
            ]
            + ([whole((width, width)), whole((8, width))] if totals else [])
            + [pl.BlockSpec(memory_space=pl.ANY)] * len(before),
            out_specs=[rows] * 4 + [whole((width, width)), whole((8, width))],
            scratch_shapes=[
                turned, turned, turned, pltpu.VMEM((slots, width), jnp.bfloat16), turned, turned,
            ],
        ),
        out_shape=[
            jax.ShapeDtypeStruct(q.shape, jnp.float32), low, low, low,
            jax.ShapeDtypeStruct((width, width), jnp.float32),
            jax.ShapeDtypeStruct((8, width), jnp.float32),
        ],
        input_output_aliases={len(inputs) + i: i for i in range(len(before))},
        compiler_params=pltpu.CompilerParams(vmem_limit_bytes=VMEM_BYTES),
        cost_estimate=estimate(16),
        name="attend_backward",
    )(*inputs, *before)


def project_grads_kernel(cuts, dp_size, me_ref, x_ref, dq_ref, dk_ref, dv_ref, og_ref, small_ref, *rest):
    xt, held, sems = rest[-3:]
    outs = rest[:-3]
    xt[...] = x_ref[...].T
    held[0] = og_ref[...].astype(jnp.bfloat16)
    started = []

    def emit(which, cut, refs, at):
        pairs = held.shape[2] // cut.width
        columns = [(p * cut.width, p, 0, cut.width) for p in range(pairs)]
        started.extend(
            run_all(
                piece_copies(
                    held.at[which], refs, sems.at[which], me_ref, cut.stages, 0, dp_size,
                    cut.half, at, columns, cut.width,
                )
            )
        )

    if cuts is not None:
        emit(0, cuts[1], outs[2:4], cuts[1].half)
        small = small_copies(
            small_ref, outs[:2], sems.at[4], me_ref, cuts[0].stages, 2 * cuts[0].half, dp_size,
            held.shape[2] // cuts[0].width,
        )
        started.extend(run_all(small))
    for which, ref in ((1, dv_ref), (2, dq_ref), (3, dk_ref)):
        held[which] = dot(xt[...], ref[...]).astype(jnp.bfloat16)
        if cuts is not None:
            cut, refs, at = (
                (cuts[1], outs[2:4], 0) if which == 1 else (cuts[0], outs[:2], (which - 2) * cuts[0].half)
            )
            emit(which, cut, refs, at)
    if cuts is None:
        for out, which in zip(outs, (2, 3, 1, 0)):
            out[...] = held[which]
    wait_all(started)


def project_grads(me, x, dq, dk, dv, og, small, cuts, dp_size):
    total, width = x.shape
    grad = jax.ShapeDtypeStruct((width, width), jnp.bfloat16)
    here = pl.BlockSpec(memory_space=pltpu.VMEM)
    direct = cuts is not None
    copies = 2 * dp_size * (width // cuts[0].width) if direct else 1
    return pl.pallas_call(
        functools.partial(project_grads_kernel, cuts, dp_size),
        in_specs=[SCALARS] + [here] * 6,
        out_specs=[ANYWHERE] * 4 if direct else [here] * 4,
        out_shape=[*cuts[0].shapes(), *cuts[1].shapes()] if direct else [grad] * 4,
        scratch_shapes=[
            pltpu.VMEM((width, total), jnp.bfloat16),
            pltpu.VMEM((4, width, width), jnp.bfloat16),
            pltpu.SemaphoreType.DMA((5, copies)),
        ],
        compiler_params=pltpu.CompilerParams(vmem_limit_bytes=VMEM_BYTES),
        cost_estimate=estimate(8),
        name="project_grads",
    )(me, x, dq, dk, dv, og, small)


def input_grad_kernel(gf_ref, dq_ref, dk_ref, dv_ref, wq_ref, wk_ref, wv_ref, out_ref):
    grad = gf_ref[...] + dot_last(dq_ref[...], wq_ref[...])
    grad = grad + dot_last(dk_ref[...], wk_ref[...])
    grad = grad + dot_last(dv_ref[...], wv_ref[...])
    out_ref[...] = grad.astype(jnp.bfloat16)


def input_grads(gf, dq, dk, dv, wq, wk, wv):
    total, width = dq.shape
    count = min(256, total)
    rows = pl.BlockSpec((count, width), lambda i: (i, 0))
    return pl.pallas_call(
        input_grad_kernel,
        grid=(total // count,),
        in_specs=[rows] * 4 + [whole((width, width))] * 3,
        out_specs=rows,
        out_shape=jax.ShapeDtypeStruct((total, width), jnp.bfloat16),
        compiler_params=pltpu.CompilerParams(vmem_limit_bytes=VMEM_BYTES),
        cost_estimate=estimate(8),
        name="input_grads",
    )(gf, dq, dk, dv, wq, wk, wv)


def after(values, *others):
    return lax.optimization_barrier((values, others))[0]


class Attention:
    def __init__(self, inputs, lengths, weights, vectors):
        self.inputs, self.lengths, self.vectors = inputs, lengths, vectors
        self.weights, self.state, self.back = weights, (), ()
        self.totals = ()

    def forward(self, seq):
        self.state = tuple(
            attend_forward(seq, self.inputs, self.lengths, *self.weights, self.vectors, self.state)
        )

    def backward(self, seq, gm):
        q, k, v, att, lse, first = self.state
        results = attend_backward(
            seq, gm, first, q, k, v, att, lse, self.lengths, self.weights[3], self.vectors,
            self.totals, self.back,
        )
        self.back, self.totals = tuple(results[:4]), tuple(results[4:])


def layer_step(inputs, lengths, upstream, gather, scatter):
    shape = inputs.shape
    flat = (shape[0] * shape[1], shape[2])
    seqs = shape[0]
    wq, wk, wv, wo, bias, hidden, gains, shifts = gather.first()
    vectors = jnp.concatenate([bias, gains, shifts], axis=0).astype(jnp.float32)
    hidden_bias = hidden.astype(jnp.float32)[None]
    attention = Attention(inputs, lengths, (wq, wk, wv, wo), vectors)
    for seq in range(seqs):
        attention.inputs = gather.before(seq, attention.inputs)
        attention.forward(seq)
        attention.state = gather.after(seq, attention.state)
    wi, wf = gather.second()
    first = attention.state[5]
    outputs, act, slope, mid, gs, low, sums_two = feed_forward(
        first, upstream, lengths, wi, wf, hidden_bias, vectors
    )
    me = gather.me
    hid, hidden_sum, *outer_grad = feed_back_outer(me, low, act, slope, wf, scatter.cuts["outer"])
    mid = scatter.outer(outer_grad, mid)
    gm, *inner_grad = feed_back_inner(me, gs, mid, hid, wi, scatter.cuts["inner"])
    gm = scatter.inner(inner_grad, gm)
    for seq in range(seqs):
        attention.backward(seq, gm.reshape(shape))
        attention.back = scatter.step(seq, attention.back)
    gf, dq, dk, dv = attention.back
    output_grad, sums_one = attention.totals
    dq, dk, dv = dq.reshape(flat), dk.reshape(flat), dv.reshape(flat)
    bias_grad = jnp.concatenate([sums_one[3:5], sums_one[2:3], sums_two[2:3]], axis=0)
    gain_grad = jnp.concatenate([sums_one[:1], sums_two[:1]], axis=0)
    shift_grad = jnp.concatenate([sums_one[1:2], sums_two[1:2]], axis=0)
    small = scatter.small((bias_grad, hidden_sum[0], gain_grad, shift_grad))
    packed = small if scatter.cuts["first"] else jnp.zeros((1, 8, 128), jnp.bfloat16)
    results = project_grads(
        me, inputs.reshape(flat), dq, dk, dv, output_grad, packed, scatter.cuts["first"], scatter.dp_size
    )
    gf = scatter.last(results, small, gf)
    input_grad = input_grads(gf.reshape(flat), dq, dk, dv, wq, wk, wv)
    return outputs.reshape(shape), input_grad.reshape(shape), scatter.totals()


def split_up(value, dim, size):
    before, after = (value.shape[:dim], value.shape[dim + 1 :])
    return jnp.moveaxis(value.reshape(*before, size, -1, *after), dim, 0)


def sum_at_owner(value, axis, dim):
    size = lax.axis_size(axis)
    parts = lax.all_to_all(split_up(value, dim, size), axis, 0, 0, tiled=True)
    return jnp.sum(parts.astype(jnp.float32), axis=0)


def side_by_side(arrays, axis, dim, along):
    ends, at = ([], 0)
    for a in arrays[:-1]:
        at += a.shape[along]
        ends.append(at)
    both = jnp.concatenate(arrays, axis=along)
    return tuple(jnp.split(sum_at_owner(both, axis, dim), ends, axis=along))


def gather_forward(shards):
    (
        query_part,
        key_part,
        value_part,
        output_part,
        inner_part,
        outer_part,
        bias_part,
        hidden_part,
        gain_part,
        shift_part,
    ) = shards
    column_full = (
        lax.all_gather(query_part, "fsdp", axis=1, tiled=True),
        lax.all_gather(key_part, "fsdp", axis=1, tiled=True),
        lax.all_gather(value_part, "fsdp", axis=1, tiled=True),
        lax.all_gather(output_part, "fsdp", axis=1, tiled=True),
        lax.all_gather(inner_part, "fsdp", axis=1, tiled=True),
        lax.all_gather(outer_part, "fsdp", axis=1, tiled=True),
    )
    return (
        lax.all_gather(column_full[0], "dp", axis=0, tiled=True),
        lax.all_gather(column_full[1], "dp", axis=0, tiled=True),
        lax.all_gather(column_full[2], "dp", axis=0, tiled=True),
        lax.all_gather(column_full[3], "dp", axis=0, tiled=True),
        lax.all_gather(column_full[4], "dp", axis=0, tiled=True),
        lax.all_gather(column_full[5], "dp", axis=0, tiled=True),
        lax.all_gather(bias_part, "dp", axis=1, tiled=True),
        lax.all_gather(hidden_part, "dp", axis=0, tiled=True),
        lax.all_gather(gain_part, "dp", axis=1, tiled=True),
        lax.all_gather(shift_part, "dp", axis=1, tiled=True),
    )


def reduce_grads(grads):
    (
        query_grad,
        key_grad,
        value_grad,
        output_grad,
        inner_grad,
        outer_grad,
        bias_grad,
        hidden_grad,
        gain_grad,
        shift_grad,
    ) = grads
    bias_grad, hidden_grad, gain_grad, shift_grad = (
        lax.psum(bias_grad.astype(jnp.bfloat16), "fsdp").astype(jnp.float32),
        lax.psum(hidden_grad.astype(jnp.bfloat16), "fsdp").astype(jnp.float32),
        lax.psum(gain_grad.astype(jnp.bfloat16), "fsdp").astype(jnp.float32),
        lax.psum(shift_grad.astype(jnp.bfloat16), "fsdp").astype(jnp.float32),
    )
    narrow = (
        lax.psum_scatter(
            query_grad.astype(jnp.bfloat16), "fsdp", scatter_dimension=1, tiled=True
        ).astype(jnp.float32),
        lax.psum_scatter(
            key_grad.astype(jnp.bfloat16), "fsdp", scatter_dimension=1, tiled=True
        ).astype(jnp.float32),
        lax.psum_scatter(
            value_grad.astype(jnp.bfloat16), "fsdp", scatter_dimension=1, tiled=True
        ).astype(jnp.float32),
        lax.psum_scatter(
            output_grad.astype(jnp.bfloat16), "fsdp", scatter_dimension=1, tiled=True
        ).astype(jnp.float32),
        lax.psum_scatter(
            inner_grad.astype(jnp.bfloat16), "fsdp", scatter_dimension=1, tiled=True
        ).astype(jnp.float32),
        lax.psum_scatter(
            outer_grad.astype(jnp.bfloat16), "fsdp", scatter_dimension=1, tiled=True
        ).astype(jnp.float32),
    )
    return (
        *side_by_side(
            (
                narrow[0].astype(jnp.bfloat16),
                narrow[1].astype(jnp.bfloat16),
                narrow[2].astype(jnp.bfloat16),
                narrow[3].astype(jnp.bfloat16),
                narrow[4].astype(jnp.bfloat16),
            ),
            "dp",
            0,
            1,
        ),
        sum_at_owner(narrow[5].astype(jnp.bfloat16), "dp", 0),
        sum_at_owner(bias_grad.astype(jnp.bfloat16), "dp", 1),
        sum_at_owner(hidden_grad.astype(jnp.bfloat16), "dp", 0),
        *side_by_side(
            (gain_grad.astype(jnp.bfloat16), shift_grad.astype(jnp.bfloat16)), "dp", 1, 0
        ),
    )


def pack_small(bias, hidden, gains, shifts, width):
    columns = bias.shape[-1]
    rows = jnp.concatenate([bias, hidden.reshape(-1, columns), gains, shifts], axis=0)
    return jnp.pad(rows, ((0, SMALL_ROWS - rows.shape[0]), (0, width - columns)))


def unpack_small(packed, columns, hidden_count):
    split = 4 + hidden_count // columns
    lined = packed[:, :, :columns]
    whole = jnp.moveaxis(lined, 0, 1).reshape(packed.shape[1], -1)
    hidden = lined[:, 4:split].reshape(-1)
    return whole[:4], hidden, whole[split : split + 2], whole[split + 2 : split + 4]


def spread_small(bias, hidden, gains, shifts, parts, width):
    columns = bias.shape[-1] // parts

    def cut(v):
        return jnp.moveaxis(v.reshape(v.shape[0], parts, columns), 1, 0)

    rows = jnp.concatenate(
        [cut(bias), hidden.reshape(parts, -1, columns), cut(gains), cut(shifts)], axis=1
    )
    rows = rows.astype(jnp.bfloat16)
    return jnp.pad(rows, ((0, 0), (0, SMALL_ROWS - rows.shape[1]), (0, width - columns)))


class Gather:
    def __init__(self, mesh, shards, me):
        self.mesh, self.shards, self.me = mesh, shards, me
        self.orders = stage_orders(mesh)

    def prepare(self):
        query, key, value, output, inner, outer, bias, hidden, gains, shifts = self.shards
        half = query.shape[0] // 2
        small = pack_small(bias, hidden, gains, shifts, 2 * query.shape[1])

        def both(left, right):
            parts = [left[:half], right[:half], left[half:], right[half:]]
            return jnp.concatenate(parts, axis=0)

        parts = pair_up((both(query, key), both(value, output)))
        self.one = [jnp.concatenate([parts[0], small], axis=0)[None], parts[1][None]]
        self.two = [part[None] for part in pair_up((inner, outer))]

    def send(self, parts, stage):
        return [swap(part, *self.orders[i][stage]) for i, part in enumerate(parts)]

    def join(self, parts, received):
        return [jnp.concatenate(pair, axis=0) for pair in zip(parts, received)]

    def first(self):
        self.prepare()
        count = len(self.orders[0])
        far = sum(1 for axis, bit in self.orders[0] if axis == "dp" and bit > 0)
        for stage in range(count):
            arriving = self.send(self.one, stage)
            if 0 < stage <= far:
                self.two = self.join(self.two, self.send(self.two, stage - 1))
            self.one = self.join(self.one, arriving)
            if stage < far:
                self.two = after(self.two, self.one)
        self.stage = far
        self.two = after(self.two, self.one)
        others = [swap(part, "fsdp", 0) for part in self.one]
        half = self.shards[0].shape[0] // 2
        wq, wk, small = place_part(
            self.mesh, self.one[0], others[0], self.me, self.orders[0], (half, half), True
        )
        wv, wo = place_part(
            self.mesh, self.one[1], others[1], self.me, self.orders[1], (half, half), False
        )
        bias, hidden = self.shards[6:8]
        return (wq, wk, wv, wo, *unpack_small(small, bias.shape[1], hidden.shape[0]))

    def before(self, seq, inputs):
        if self.stage == len(self.orders[0]):
            return inputs
        self.arriving = self.send(self.two, self.stage)
        self.stage += 1
        return after(inputs, self.two)

    def after(self, seq, state):
        if self.arriving is None:
            return state
        arriving = after(self.arriving, state)
        self.two, self.arriving = self.join(self.two, arriving), None
        return state

    def second(self):
        while self.stage < len(self.orders[0]):
            self.two = self.join(self.two, self.send(self.two, self.stage))
            self.stage += 1
        others = [swap(part, "fsdp", 0) for part in self.two]
        half, half_outer = self.shards[4].shape[0] // 2, self.shards[5].shape[0] // 2
        (wi,) = place_part(
            self.mesh, self.two[0], others[0], self.me, self.orders[0], (half,), False
        )
        (wf,) = place_part(
            self.mesh, self.two[1], others[1], self.me, self.orders[1], (half_outer,), False
        )
        return wi, wf


class Part:
    def __init__(self, keep, send, stages):
        self.keep, self.stages = keep, list(stages)
        self.arriving = swap(send, "fsdp", 0)

    def step(self):
        axis, bit = self.stages.pop()
        half = self.keep.shape[0] // 2
        send = total_of(self.keep[half:], self.arriving[half:], jnp.bfloat16)
        arriving = swap(send, axis, bit)
        self.keep = total_of(self.keep[:half], self.arriving[:half], jnp.bfloat16)
        self.arriving = arriving
        return send

    def finish(self):
        while self.stages:
            self.step()
        return total_of(self.keep, self.arriving, jnp.float32)[0]


class Scatter:
    def __init__(self, mesh, shards, me):
        self.shards = shards
        one, two = stage_orders(mesh)
        width = 2 * shards[0].shape[1]
        half, half_outer = shards[0].shape[0] // 2, shards[5].shape[0] // 2
        self.dp_size = mesh.shape["dp"]
        self.cuts = {
            "outer": Cut(two, half_outer, half_outer, width),
            "inner": Cut(one, half, half, 2 * shards[4].shape[1]),
            "first": (Cut(one, half, 2 * half + SMALL_ROWS, width), Cut(two, half, 2 * half, width)),
        }

    def outer(self, grad, passing):
        self.outer_part = Part(*grad, self.cuts["outer"].stages)
        return after(passing, grad)

    def inner(self, grad, passing):
        self.inner_part = Part(*grad, self.cuts["inner"].stages)
        return after(passing, grad, self.outer_part.step())

    def step(self, seq, state):
        if seq == 0:
            self.inner_part.arriving = after(self.inner_part.arriving, state)
            sent = [self.inner_part.step()]
        else:
            self.outer_part.arriving = after(self.outer_part.arriving, state)
            self.inner_part.arriving = after(self.inner_part.arriving, state)
            sent = [self.outer_part.step(), self.inner_part.step()]
        return after(state, sent)

    def small(self, small):
        return spread_small(*small, self.dp_size, self.cuts["first"][0].width)

    def last(self, results, small, passing):
        cuts = self.cuts["first"]
        self.first_part = Part(*results[:2], cuts[0].stages)
        self.second_part = Part(*results[2:], cuts[1].stages)
        late, early = self.early(), [self.first_part, self.second_part]
        for part in late:
            part.arriving = after(part.arriving, results)
        sent = [part.step() for part in late]
        for part in early:
            part.arriving = after(part.arriving, sent)
        sent = [part.step() for part in early]
        return after(passing, sent)

    def early(self):
        return [self.outer_part, self.inner_part]

    def together(self, parts):
        values = after([(part.keep, part.arriving) for part in parts])
        for part, (keep, arriving) in zip(parts, values):
            part.keep, part.arriving = keep, arriving

    def totals(self):
        half, half_outer = self.shards[0].shape[0] // 2, self.shards[5].shape[0] // 2
        columns = self.shards[6].shape[1]
        front, behind = [self.first_part, self.second_part], self.early()
        for part in behind:
            if part.stages:
                part.step()
        done = []
        while any(part.stages for part in front + behind):
            self.together(front)
            for part in front:
                if part.stages:
                    part.step()
            for part in behind:
                part.arriving = after(part.arriving, [p.keep for p in front])
                if part.stages:
                    part.step()
        (outer,) = settle(behind[0].finish(), (half_outer,))
        (inner,) = settle(behind[1].finish(), (half,))
        value, output = settle(front[1].finish(), (half, half))
        total = front[0].finish()
        query, key = settle(total, (half, half))
        rows = total[2 * half :, :columns]
        split = 4 + self.shards[7].shape[0] // columns
        return (
            query, key, value, output, inner, outer,
            rows[:4], rows[4:split].reshape(-1), rows[split : split + 2], rows[split + 2 : split + 4],
        )


class PlainGather:
    def __init__(self, mesh, shards, me):
        self.shards, self.me = shards, me

    def first(self):
        whole_ = gather_forward(self.shards)
        self.rest = whole_[4:6]
        return (*whole_[:4], *whole_[6:])

    def before(self, seq, inputs):
        return inputs

    def after(self, seq, state):
        return state

    def second(self):
        return self.rest


class PlainScatter:
    def __init__(self, mesh, shards, me):
        self.cuts = {"outer": None, "inner": None, "first": None}
        self.dp_size = mesh.shape["dp"]

    def outer(self, grad, passing):
        self.outer_grad = grad[0]
        return passing

    def inner(self, grad, passing):
        self.inner_grad = grad[0]
        return passing

    def step(self, seq, state):
        return state

    def small(self, small):
        return small

    def last(self, results, small, passing):
        self.grads = (*results, self.inner_grad, self.outer_grad, *small)
        return passing

    def totals(self):
        return reduce_grads(self.grads)


def on_device(
    mesh,
    tokens,
    lengths,
    cotangent,
    *shards,
):
    me = jnp.stack([lax.axis_index("dp"), lax.axis_index("fsdp")]).astype(jnp.int32)
    rows = (shards[0].shape[0], shards[5].shape[0])
    direct = fits(mesh, rows, shards[0].shape[1])
    gather = (Gather if direct else PlainGather)(mesh, shards, me)
    scatter = (Scatter if direct else PlainScatter)(mesh, shards, me)
    shape = (-1, *tokens.shape[2:])
    outputs, grad_inputs, totals = layer_step(
        tokens.reshape(shape), lengths.reshape(-1), cotangent.reshape(shape), gather, scatter
    )
    return (outputs.reshape(tokens.shape), grad_inputs.reshape(tokens.shape), *totals)


def solution(mesh):
    placed = (
        P(None, ("dp", "fsdp"), None, None),
        P(None, ("dp", "fsdp")),
        P(None, ("dp", "fsdp"), None, None),
        P("dp", "fsdp"),
        P("dp", "fsdp"),
        P("dp", "fsdp"),
        P("dp", "fsdp"),
        P("dp", "fsdp"),
        P("dp", "fsdp"),
        P(None, "dp"),
        P("dp"),
        P(None, "dp"),
        P(None, "dp"),
    )
    return jax.shard_map(
        functools.partial(on_device, mesh),
        mesh=mesh,
        in_specs=placed,
        out_specs=(
            P(None, ("dp", "fsdp"), None, None),
            P(None, ("dp", "fsdp"), None, None),
            P("dp", "fsdp"),
            P("dp", "fsdp"),
            P("dp", "fsdp"),
            P("dp", "fsdp"),
            P("dp", "fsdp"),
            P("dp", "fsdp"),
            P(None, "dp"),
            P("dp"),
            P(None, "dp"),
            P(None, "dp"),
        ),
        check_vma=False,
    )
```

```python
import functools
import jax
import jax.numpy as jnp
from jax import lax
from jax.experimental import pallas as pl
from jax.experimental.pallas import tpu as pltpu
from jax.sharding import PartitionSpec as P

HEADS = 12


EPSILON = 1e-12
MASKED = -1000000000.0
SMALL_ROWS = 16


def swap(value, axis, bit):
    size = lax.axis_size(axis)
    return lax.ppermute(value, axis, [(i, i ^ (1 << bit)) for i in range(size)])


def stage_orders(mesh):
    dp_bits = mesh.shape["dp"].bit_length() - 1
    fsdp_bits = mesh.shape["fsdp"].bit_length() - 1
    far = [("dp", b) for b in range(dp_bits - 1, 0, -1)]
    across = [("fsdp", b) for b in range(fsdp_bits - 1, 0, -1)]
    near = [("dp", 0)]
    return (far + across + near, far + near + across, across + near + far)


def fits(mesh, rows, width, hidden):
    sizes = (mesh.shape["dp"], mesh.shape["fsdp"])
    powers = all(s >= 2 and s & (s - 1) == 0 for s in sizes)
    return powers and all(r % 32 == 0 for r in rows) and width % 64 == 0 and hidden % 128 == 0 and 32 < rows[0] <= 128


def place_of(stages, dp, fsdp, me_ref):
    index = {"dp": dp ^ me_ref[0], "fsdp": fsdp ^ me_ref[1]}
    place = 0
    for s, (axis, bit) in enumerate(stages):
        place = place + (((index[axis] >> bit) & 1) << s)
    return place


def piece_copies(source, outs, sems, me_ref, stages, first_dp, count_dp, half, span, columns):
    copies = []
    offset, rows, at = span
    for i in range(count_dp):
        dp = first_dp + i
        for flip in range(2):
            fsdp = (me_ref[1] & 1) ^ flip
            row = pl.multiple_of((2 * i + fsdp) * half + offset, 16)
            for start, pair, into, count in columns:
                place = place_of(stages, dp, 2 * pair + fsdp, me_ref)
                copies.append(
                    pltpu.make_async_copy(
                        source.at[pl.ds(row, rows), pl.ds(start, count)],
                        outs[flip].at[place, pl.ds(at, rows), pl.ds(into, count)],
                        sems.at[len(copies)],
                    )
                )
    return copies


class Source:
    def __init__(self, operands, stages=(), spots=(), dp_size=0, small_at=None):
        self.operands, self.stages, self.spots = tuple(operands), stages, spots
        self.dp_size, self.small_at = dp_size, small_at

    def count(self, shape):
        if not self.spots:
            return 1
        return 2 * self.dp_size * max(shape[1] // width * len(spans) for _, width, spans in self.spots)

    def copies(self, which, refs, target, sems, me_ref):
        if not self.spots:
            return [pltpu.make_async_copy(refs[which], target, sems.at[0])]
        half, width, spans = self.spots[which]
        copies = []
        for part, at, offset, rows, column in spans:
            count = self.operands[2 * part].shape[2]
            for dp in range(self.dp_size):
                for flip in range(2):
                    fsdp = (me_ref[1] & 1) ^ flip
                    row = pl.multiple_of((2 * dp + fsdp) * half + offset, 16)
                    for pair in range(target.shape[1] // width):
                        place = place_of(self.stages[part], dp, 2 * pair + fsdp, me_ref)
                        copies.append(
                            pltpu.make_async_copy(
                                refs[2 * part + flip].at[place, pl.ds(at, rows), :],
                                target.at[pl.ds(row, rows), pl.ds(pair * width + column, count)],
                                sems.at[len(copies)],
                            )
                        )
        return copies

    def small_copies(self, refs, target, sems, me_ref):
        copies = []
        for dp in range(self.dp_size):
            place = place_of(self.stages[0], dp, me_ref[1], me_ref)
            source = refs[0].at[place, pl.ds(self.small_at, SMALL_ROWS), :]
            copies.append(pltpu.make_async_copy(source, target.at[dp], sems.at[dp]))
        return copies

    def pick(self, which):
        if not self.spots:
            return Source([self.operands[i] for i in which])
        return Source(self.operands, self.stages, [self.spots[i] for i in which], self.dp_size)


def lay_vectors(small, columns, hidden_count, vec_ref, hb_ref):
    lanes = min(128, small.shape[2])
    width = vec_ref.shape[1]
    parts = small.shape[0]

    def chosen(to, start):
        row = lax.broadcasted_iota(jnp.int32, (lanes, to), 0)
        column = lax.broadcasted_iota(jnp.int32, (lanes, to), 1)
        return ((column - start == row) & (row < columns)).astype(jnp.float32).astype(jnp.bfloat16)

    total = jnp.zeros((SMALL_ROWS, width), jnp.float32)
    for dp in range(parts):
        total = total + dot(small[dp, :, :lanes], chosen(width, dp * columns))
    share = hidden_count // parts
    rows = share // columns
    vec_ref[0:4, :] = total[0:4]
    vec_ref[4:8, :] = total[4 + rows : 8 + rows]
    flat = small[:, :, :lanes].reshape(parts * SMALL_ROWS, lanes)
    spread = [dot(flat, chosen(share, k * columns)) for k in range(rows)]
    for dp in range(parts):
        at = dp * SMALL_ROWS + 4
        hb_ref[:, dp * share : (dp + 1) * share] = sum(
            spread[k][at + k : at + k + 1] for k in range(rows)
        )


def small_copies(source, outs, sems, me_ref, stages, at, dp_size, pairs):
    copies = []
    for dp in range(dp_size):
        for flip in range(2):
            fsdp = (me_ref[1] & 1) ^ flip
            for pair in range(pairs):
                place = place_of(stages, dp, 2 * pair + fsdp, me_ref)
                copies.append(
                    pltpu.make_async_copy(
                        source.at[dp],
                        outs[flip].at[place, pl.ds(at, SMALL_ROWS), :],
                        sems.at[len(copies)],
                    )
                )
    return copies


def run_all(copies):
    for copy in copies:
        copy.start()
    return copies


def wait_all(copies):
    for copy in copies:
        copy.wait()


def total_of(left, right, kind):
    return (left.astype(jnp.float32) + right.astype(jnp.float32)).astype(kind)


def settle(total, rows):
    width = total.shape[-1] // 2
    count = sum(rows)
    second = lax.axis_index("fsdp") & 1
    own = jnp.where(second == 0, total[:count, :width], total[:count, width:])
    away = jnp.where(second == 0, total[:count, width:], total[:count, :width])
    came = swap(away.astype(jnp.bfloat16), "fsdp", 0).astype(jnp.float32)
    first, last = jnp.where(second == 0, own, came), jnp.where(second == 0, came, own)
    outs, at = [], 0
    for half in rows:
        outs.append(jnp.concatenate([first[at : at + half], last[at : at + half]], axis=0))
        at += half
    return outs


def pair_up(shards):
    second = lax.axis_index("fsdp") & 1
    outs = []
    for shard in shards:
        half = shard.shape[0] // 2
        mine = jnp.where(second == 0, shard[:half], shard[half:])
        away = jnp.where(second == 0, shard[half:], shard[:half])
        came = swap(away, "fsdp", 0)
        outs.append(
            jnp.where(
                second == 0,
                jnp.concatenate([mine, came], axis=1),
                jnp.concatenate([came, mine], axis=1),
            )
        )
    return outs


VMEM_BYTES = 56 << 20
FEED_BYTES = 60 << 20


def estimate(micros):
    return pl.CostEstimate(flops=micros * 1000000000, bytes_accessed=micros * 1000000, transcendentals=0)


def dot(left, right):
    return jnp.dot(left, right, preferred_element_type=jnp.float32)


def dot_last(left, right):
    return lax.dot_general(
        left, right, (((1,), (1,)), ((), ())), preferred_element_type=jnp.float32
    )


def dot_first(left, right):
    return lax.dot_general(
        left, right, (((0,), (0,)), ((), ())), preferred_element_type=jnp.float32
    )


def normalize(values):
    centered = values - jnp.mean(values, axis=-1, keepdims=True)
    variance = jnp.mean(centered * centered, axis=-1, keepdims=True)
    factor = lax.rsqrt(variance + EPSILON)
    return (centered * factor, factor)


def norm_back(upward, normed, factor):
    return factor * (
        upward
        - jnp.mean(upward, axis=-1, keepdims=True)
        - normed * jnp.mean(upward * normed, axis=-1, keepdims=True)
    )


def gelu_pair(v):
    size = jnp.abs(v) * 0.7071067811865476
    t = 1.0 / (1.0 + 0.3275911 * size)
    bell = jnp.exp(-size * size)
    poly = t * (
        0.254829592
        + t * (-0.284496736 + t * (1.421413741 + t * (-1.453152027 + t * 1.061405429)))
    )
    tail = 0.5 * poly * bell
    cdf = jnp.where(v >= 0.0, 1.0 - tail, tail)
    return v * cdf, cdf + v * bell * 0.3989422804014327


def three_parts(value):
    high = value.astype(jnp.bfloat16).astype(jnp.float32)
    rest = value - high
    middle = rest.astype(jnp.bfloat16).astype(jnp.float32)
    return high, middle, rest - middle


def head_keys(pair, head, length, with_stats):
    rows, lanes = pair.shape
    lane = lax.broadcasted_iota(jnp.int32, (rows, lanes), 1)
    row = lax.broadcasted_iota(jnp.int32, (rows, lanes), 0)
    start = lanes // 2 if head == 0 else 0
    own = lane < lanes // 2 if head == 0 else lane >= lanes // 2
    hidden = jnp.where((lane == start) & (row >= length), MASKED, 0.0)
    if with_stats:
        hidden = jnp.where((lane > start) & (lane < start + 4), 1.0, hidden)
    return jnp.where(own, pair.astype(jnp.float32), hidden).astype(jnp.bfloat16)


def head_values(pair, head):
    rows, lanes = pair.shape
    lane = lax.broadcasted_iota(jnp.int32, (rows, lanes), 1)
    start = lanes // 2 if head == 0 else 0
    own = lane < lanes // 2 if head == 0 else lane >= lanes // 2
    ones = jnp.where((lane >= start) & (lane < start + 3), 1.0, 0.0)
    return jnp.where(own, pair.astype(jnp.float32), ones).astype(jnp.bfloat16)


def only_head(pair, head):
    lane = lax.broadcasted_iota(jnp.int32, pair.shape, 1)
    own = lane < pair.shape[1] // 2 if head == 0 else lane >= pair.shape[1] // 2
    return jnp.where(own, pair.astype(jnp.float32), 0.0).astype(jnp.bfloat16)


def with_rows(part, head, rows):
    count, width = part.shape
    row = lax.broadcasted_iota(jnp.int32, (count, width), 0)
    extra = jnp.zeros((count, width), jnp.float32)
    for i, value in enumerate(rows):
        extra = jnp.where(row == i, value, extra)
    extra = extra.astype(jnp.bfloat16)
    return jnp.concatenate([part, extra] if head == 0 else [extra, part], axis=0)


def forward_kernel(seq, source, columns, count_in, lengths, me_ref, x_ref, *refs):
    inputs, refs = refs[:count_in], refs[count_in:]
    q_ref, k_ref, v_ref, att_ref, lse_ref, vec_ref, hb_ref = refs[:7]
    qt, vt, ot, weights, sems, small, small_sems = refs[7:]
    length = lengths[seq]
    started = []
    for which in range(3):
        started.append(
            run_all(source.copies(which, inputs, weights.at[which], sems.at[which], me_ref))
        )
    wq_ref, wk_ref, wv_ref = (weights.at[i] for i in range(3))
    if source.spots:
        wait_all(run_all(source.small_copies(inputs, small, small_sems, me_ref)))
        lay_vectors(small[...], columns, hb_ref.shape[1], vec_ref, hb_ref)
    else:
        vec_ref[...] = inputs[-2][...]
        hb_ref[...] = inputs[-1][...]
    for copies in started:
        wait_all(copies)
    x = x_ref[...]
    head_size = x.shape[1] // HEADS
    scale = head_size**-0.5
    queries = (dot(x, wq_ref[...]) + vec_ref[0:1, :]).astype(jnp.bfloat16)
    queries = (queries.astype(jnp.float32) * scale).astype(jnp.bfloat16)
    q_ref[...] = queries
    qt[...] = queries.T
    k_ref[...] = dot(x, wk_ref[...]).astype(jnp.bfloat16)
    values = (dot(x, wv_ref[...]) + vec_ref[1:2, :]).astype(jnp.bfloat16)
    v_ref[...] = values
    vt[...] = values.T

    def one_pair(p, carry):
        base = pl.multiple_of(p * 2 * head_size, 2 * head_size)
        pair = k_ref[:, pl.ds(base, 2 * head_size)]
        for head in range(2):
            at = pl.multiple_of(base + head * head_size, head_size)
            keys = head_keys(pair, head, length, False)
            scores = dot(keys, with_rows(qt[pl.ds(at, head_size), :], head, [1.0]))
            highest = jnp.max(scores, axis=0, keepdims=True)
            exponent = jnp.exp(scores - highest)
            total = jnp.sum(exponent, axis=0, keepdims=True)
            blended = dot(vt[pl.ds(at, head_size), :], exponent.astype(jnp.bfloat16))
            ot[pl.ds(at, head_size), :] = (blended / total).astype(jnp.bfloat16)
            lse_ref[p, head : head + 1, :] = highest + jnp.log(total)
        return carry

    lax.fori_loop(0, HEADS // 2, one_pair, 0)
    att_ref[...] = ot[...].T


def whole(shape):
    return pl.BlockSpec(shape, lambda *_: (0,) * len(shape))


def skip_refs(kernel, first, count, *refs):
    kernel(*refs[:first], *refs[first + count :])


def attend_forward(seq, me, x, lengths, source, vectors, columns, hidden_count, before):
    seqs, slots, width = x.shape
    rows = pl.BlockSpec((None, slots, width), lambda i, *_: (seq, 0, 0))
    low = jax.ShapeDtypeStruct(x.shape, jnp.bfloat16)
    given = (*source.operands, *vectors)
    kernel = functools.partial(forward_kernel, seq, source, columns, len(given))
    known = 3 + len(given)
    small = (max(source.dp_size, 1), SMALL_ROWS, source.spots[0][1] if source.spots else 128)
    return pl.pallas_call(
        functools.partial(skip_refs, kernel, known, len(before)),
        grid_spec=pltpu.PrefetchScalarGridSpec(
            num_scalar_prefetch=2,
            grid=(1,),
            in_specs=[rows]
            + [ANYWHERE] * len(source.operands)
            + [whole(v.shape) for v in vectors]
            + [ANYWHERE] * len(before),
            out_specs=[rows] * 4
            + [
                pl.BlockSpec((None, HEADS // 2, 2, slots), lambda i, *_: (seq, 0, 0, 0)),
                whole((8, width)),
                whole((1, hidden_count)),
            ],
            scratch_shapes=[pltpu.VMEM((width, slots), jnp.bfloat16)] * 3
            + [
                pltpu.VMEM((3, width, width), jnp.bfloat16),
                pltpu.SemaphoreType.DMA((3, source.count((width, width)))),
                pltpu.VMEM(small, jnp.bfloat16),
                pltpu.SemaphoreType.DMA((small[0],)),
            ],
        ),
        out_shape=[low] * 4
        + [
            jax.ShapeDtypeStruct((seqs, HEADS // 2, 2, slots), jnp.float32),
            jax.ShapeDtypeStruct((8, width), jnp.float32),
            jax.ShapeDtypeStruct((1, hidden_count), jnp.float32),
        ],
        input_output_aliases={known + i: i for i in range(len(before))},
        compiler_params=pltpu.CompilerParams(vmem_limit_bytes=VMEM_BYTES),
        cost_estimate=estimate(14),
        name="attend_forward",
    )(lengths, me, x, *given, *before)


def feed_kernel(
    source, cuts, slots, lengths, me_ref, x_ref, att_ref, cot_ref, hb_ref, vec_ref, *refs
):
    count_in = len(source.operands)
    inputs, refs = refs[:count_in], refs[count_in:]
    out_ref, gf_ref, do_ref, hsum_ref, sums_ref = refs[:5]
    (
        wi, wf, wo, act, slope_s, first, mid, mid_t, low_s, held_i, held_o, held_a,
        load_a, load_i, load_o, sems, sems_a,
    ) = refs[-17:]
    grads = refs[5:-17]
    loads = [
        run_all(source.copies(which, inputs, target, sem, me_ref))
        for which, target, sem in ((0, wo, load_a), (1, wi, load_i), (2, wf, load_o))
    ]
    total, width = x_ref.shape
    inner = wi.shape[1]
    tile = min(256, slots)
    piece = min(1024, inner)
    sums_ref[...] = jnp.zeros_like(sums_ref)
    wait_all(loads[0])
    first[...] = x_ref[...].astype(jnp.float32) + dot(att_ref[...], wo[...]) + vec_ref[2:3, :]
    for copies in loads[1:]:
        wait_all(copies)

    def forward(t, carry):
        rows = pl.ds(pl.multiple_of(t * tile, tile), tile)
        normed, _ = normalize(first[rows, :])
        middle = normed * vec_ref[4:5, :] + vec_ref[6:7, :]
        middle_low = middle.astype(jnp.bfloat16)
        mid[rows, :] = middle_low
        second = middle + vec_ref[3:4, :]
        for at in range(0, inner, piece):
            here = slice(at, at + piece)
            hidden = dot(middle_low, wi[:, here]) + hb_ref[:, here]
            active, slope = gelu_pair(hidden)
            active = active.astype(jnp.bfloat16)
            act[rows, here] = active
            slope_s[rows, here] = slope.astype(jnp.bfloat16)
            second = second + dot(active, wf[here, :])
        normed, factor = normalize(second)
        start = t * tile
        slot = start % slots + lax.broadcasted_iota(jnp.int32, (tile, 1), 0)
        mask = (slot < lengths[start // slots]).astype(jnp.float32)
        out_ref[rows, :] = ((normed * vec_ref[5:6, :] + vec_ref[7:8, :]) * mask).astype(jnp.bfloat16)
        upward = cot_ref[rows, :].astype(jnp.float32) * mask
        grad = norm_back(upward * vec_ref[5:6, :], normed, factor)
        gf_ref[rows, :] = grad
        low = grad.astype(jnp.bfloat16)
        low_s[rows, :] = low
        sums_ref[0:1, :] += jnp.sum(upward * normed, axis=0, keepdims=True)
        sums_ref[1:2, :] += jnp.sum(upward, axis=0, keepdims=True)
        sums_ref[2:3, :] += jnp.sum(low.astype(jnp.float32), axis=0, keepdims=True)
        return carry

    lax.fori_loop(0, total // tile, forward, 0)
    mid_t[...] = mid[...].T
    chunk = held_i.shape[2]
    steps = inner // chunk

    def copies(step):
        slot = step % 2
        if cuts is None:
            start = pl.multiple_of(step * chunk, chunk)
            return [
                pltpu.make_async_copy(
                    held_o.at[slot], grads[2].at[pl.ds(start, chunk), :], sems.at[slot, 0]
                ),
                pltpu.make_async_copy(
                    held_i.at[slot], grads[1].at[:, pl.ds(start, chunk)], sems.at[slot, 1]
                ),
            ]
        made, split = [], cuts.split
        blocks = chunk // (2 * split.half_outer)
        for cut, outs, span, columns in cuts.outer(grads, width):
            made += piece_copies(
                held_o.at[slot], outs, sems.at[slot, pl.ds(len(made), 2 * blocks * len(columns))],
                me_ref, cut.stages, step * blocks, blocks, split.half_outer, span, columns,
            )
        for cut, outs, span, columns in cuts.inner(grads, step, chunk):
            made += piece_copies(
                held_i.at[slot], outs, sems.at[slot, pl.ds(len(made), width // split.half)],
                me_ref, cut.stages, 0, width // (2 * split.half), split.half, span, columns,
            )
        return made

    def backward(step, carry):
        here = pl.ds(pl.multiple_of(step * chunk, chunk), chunk)
        low = low_s[...]
        up = dot_last(low, wf[here, :]) * slope_s[:, here].astype(jnp.float32)
        hidden = up.astype(jnp.bfloat16)
        hsum_ref[:, here] = jnp.sum(hidden.astype(jnp.float32), axis=0, keepdims=True)

        @pl.when(step >= 2)
        def _():
            wait_all(copies(step - 2))

        held_o[step % 2] = dot_first(act[:, here], low).astype(jnp.bfloat16)
        held_i[step % 2] = dot(mid_t[...], hidden).astype(jnp.bfloat16)
        run_all(copies(step))
        gf_ref[...] += dot_last(hidden, wi[:, here])
        return carry

    lax.fori_loop(0, steps, backward, 0, unroll=2)

    def finish(t, carry):
        rows = pl.ds(pl.multiple_of(t * tile, tile), tile)
        grad_middle = gf_ref[rows, :]
        normed, factor = normalize(first[rows, :])
        sums_ref[3:4, :] += jnp.sum(grad_middle * normed, axis=0, keepdims=True)
        sums_ref[4:5, :] += jnp.sum(grad_middle, axis=0, keepdims=True)
        grad_first = norm_back(grad_middle * vec_ref[4:5, :], normed, factor)
        gf_ref[rows, :] = grad_first
        branch = grad_first.astype(jnp.bfloat16)
        low_s[rows, :] = branch
        sums_ref[5:6, :] += jnp.sum(branch.astype(jnp.float32), axis=0, keepdims=True)
        do_ref[rows, :] = dot_last(branch, wo[...]).astype(jnp.bfloat16)
        return carry

    lax.fori_loop(0, total // tile, finish, 0)
    held_a[...] = dot_first(att_ref[...], low_s[...]).astype(jnp.bfloat16)
    if cuts is None:
        last = [pltpu.make_async_copy(held_a, grads[0], sems_a.at[0])]
    else:
        cut, outs, span, columns = cuts.output(grads, width)
        half = cuts.split.half
        last = piece_copies(
            held_a, outs, sems_a, me_ref, cut.stages, 0, width // (2 * half), half, span, columns
        )
    run_all(last)
    for step in range(max(0, steps - 2), steps):
        wait_all(copies(step))
    wait_all(last)


class Cut:
    def __init__(self, stages, rows, width):
        self.stages, self.rows, self.width = tuple(stages), rows, width
        self.places = 1 << len(stages)

    def shapes(self):
        return [jax.ShapeDtypeStruct((self.places, self.rows, self.width), jnp.bfloat16)] * 2


class FeedSplit:
    def __init__(self, half, half_outer, width, width_inner):
        self.half, self.half_outer, self.width, self.width_inner = half, half_outer, width, width_inner
        self.groups = width_inner // width
        self.extra = 0
        self.most = max(16, half_outer // 6 * 5 // 16 * 16)
        self.rest = half_outer - self.most
        self.folded = half + self.rest

    def spots(self):
        kept = self.half - self.extra
        folds = [
            (2, self.folded + g * self.extra, kept, self.extra, g * self.width)
            for g in range(self.groups if self.extra else 0)
        ]
        return [
            (self.half, self.width, [(2, 0, 0, self.half, 0)]),
            (self.half, self.width_inner, [(0, 0, 0, kept, 0)] + folds),
            (
                self.half_outer,
                self.width,
                [(1, 0, 0, self.most, 0), (2, self.half, self.most, self.rest, 0)],
            ),
        ]


class FeedCuts:
    def __init__(self, orders, split):
        self.split = split
        rows = (split.half - split.extra, split.most, split.folded + split.groups * split.extra)
        widths = (split.width_inner, split.width, split.width)
        self.cuts = [Cut(*sizes) for sizes in zip(orders, rows, widths)]

    def shapes(self):
        return [shape for cut in self.cuts for shape in cut.shapes()]

    def inner(self, grads, step, chunk):
        split = self.split
        kept = split.half - split.extra
        parts = split.width_inner // chunk
        into = pl.multiple_of(step % parts * chunk, 128)
        listed = [(self.cuts[0], grads[0:2], (0, kept, 0), [(0, step // parts, into, chunk)])]
        for g in range(chunk // split.width if split.extra else 0):
            group = step % parts * (chunk // split.width) + g
            at = pl.multiple_of(split.folded + group * split.extra, 16)
            columns = [(g * split.width, step // parts, 0, split.width)]
            listed.append((self.cuts[2], grads[4:6], (kept, split.extra, at), columns))
        return listed

    def outer(self, grads, width):
        split = self.split
        columns = [(p * split.width, p, 0, split.width) for p in range(width // split.width)]
        listed = [(self.cuts[1], grads[2:4], (0, split.most, 0), columns)]
        if split.rest:
            listed.append((self.cuts[2], grads[4:6], (split.most, split.rest, split.half), columns))
        return listed

    def output(self, grads, width):
        split = self.split
        columns = [(p * split.width, p, 0, split.width) for p in range(width // split.width)]
        return self.cuts[2], grads[4:6], (0, split.half, 0), columns


ANYWHERE = pl.BlockSpec(memory_space=pl.ANY)
SCALARS = pl.BlockSpec(memory_space=pltpu.SMEM)
HERE = pl.BlockSpec(memory_space=pltpu.VMEM)


def feed(me, lengths, x, att, cotangent, hidden_bias, vectors, source, cuts):
    seqs, slots, width = x.shape
    inner = hidden_bias.shape[1]
    total = seqs * slots
    chunk = min(768, inner)
    low = jnp.bfloat16
    if cuts is None:
        shapes = ((width, width), (width, inner), (inner, width))
        grads = [jax.ShapeDtypeStruct(shape, low) for shape in shapes]
        copies, copies_last = 2, 1
    else:
        grads = cuts.shapes()
        split = cuts.split
        pairs = width // split.width
        copies = 2 * (chunk // split.half_outer) * pairs
        copies += width // split.half * (1 + chunk // split.width)
        copies_last = width // split.half * pairs
    return pl.pallas_call(
        functools.partial(feed_kernel, source, cuts, slots),
        in_specs=[SCALARS, SCALARS] + [HERE] * 5 + [ANYWHERE] * len(source.operands),
        out_specs=[HERE] * 5 + [ANYWHERE] * len(grads),
        out_shape=[
            jax.ShapeDtypeStruct((total, width), low),
            jax.ShapeDtypeStruct((total, width), jnp.float32),
            jax.ShapeDtypeStruct((total, width), low),
            jax.ShapeDtypeStruct((1, inner), jnp.float32),
            jax.ShapeDtypeStruct((8, width), jnp.float32),
            *grads,
        ],
        scratch_shapes=[
            pltpu.VMEM((width, inner), low),
            pltpu.VMEM((inner, width), low),
            pltpu.VMEM((width, width), low),
            pltpu.VMEM((total, inner), low),
            pltpu.VMEM((total, inner), low),
            pltpu.VMEM((total, width), jnp.float32),
            pltpu.VMEM((total, width), low),
            pltpu.VMEM((width, total), low),
            pltpu.VMEM((total, width), low),
            pltpu.VMEM((2, width, chunk), low),
            pltpu.VMEM((2, chunk, width), low),
            pltpu.VMEM((width, width), low),
            pltpu.SemaphoreType.DMA((source.pick([0]).count((width, width)),)),
            pltpu.SemaphoreType.DMA((source.pick([1]).count((width, inner)),)),
            pltpu.SemaphoreType.DMA((source.pick([2]).count((inner, width)),)),
            pltpu.SemaphoreType.DMA((2, copies)),
            pltpu.SemaphoreType.DMA((copies_last,)),
        ],
        compiler_params=pltpu.CompilerParams(vmem_limit_bytes=FEED_BYTES),
        cost_estimate=estimate(60),
        name="feed",
    )(
        lengths, me, x.reshape(total, width), att.reshape(total, width),
        cotangent.reshape(total, width), hidden_bias, vectors, *source.operands,
    )


def backward_kernel(
    seq, head_size, lengths, do_ref, q_ref, k_ref, v_ref, att_ref, lse_ref, *rest
):
    dq_ref, dk_ref, dv_ref, qt, kt, at_t, do_t, dq_t = rest
    length = lengths[seq]
    width = q_ref.shape[1]
    scale = head_size**-0.5
    at_t[...] = att_ref[...].T
    do_t[...] = do_ref[...].T
    qt[...] = q_ref[...].T
    kt[...] = k_ref[...].T

    def one_pair(p, carry):
        base = pl.multiple_of(p * 2 * head_size, 2 * head_size)
        here = pl.ds(base, 2 * head_size)
        key_pair, value_pair = k_ref[:, here], v_ref[:, here]
        query_pair, up_pair = q_ref[:, here], do_ref[:, here]
        grad_keys = grad_values = None
        for head in range(2):
            at = pl.multiple_of(base + head * head_size, head_size)
            mine = pl.ds(at, head_size)
            logs = [-part for part in three_parts(lse_ref[p, head : head + 1, :])]
            keys = head_keys(key_pair, head, length, True)
            soft = jnp.exp(dot(keys, with_rows(qt[mine, :], head, [1.0] + logs)))
            up = do_t[mine, :]
            delta = jnp.sum(
                up.astype(jnp.float32) * at_t[mine, :].astype(jnp.float32), axis=0, keepdims=True
            )
            deltas = [-part for part in three_parts(delta)]
            grad_soft = dot(head_values(value_pair, head), with_rows(up, head, deltas))
            scores = (soft * grad_soft).astype(jnp.bfloat16)
            from_values = dot(soft.astype(jnp.bfloat16), only_head(up_pair, head))
            from_keys = dot(scores, only_head(query_pair, head))
            grad_values = from_values if head == 0 else grad_values + from_values
            grad_keys = from_keys if head == 0 else grad_keys + from_keys
            dq_t[mine, :] = (dot(kt[mine, :], scores) * scale).astype(jnp.bfloat16)
        dk_ref[:, here] = grad_keys.astype(jnp.bfloat16)
        dv_ref[:, here] = grad_values.astype(jnp.bfloat16)
        return carry

    lax.fori_loop(0, width // (2 * head_size), one_pair, 0)
    dq_ref[...] = dq_t[...].T


def attend_backward(seq, part, parts, do, q, k, v, att, lse, lengths, before):
    seqs, slots, width = q.shape
    count = width // parts
    pairs = HEADS // 2 // parts
    rows = pl.BlockSpec((None, slots, count), lambda i, *_: (seq, 0, part))
    low = jax.ShapeDtypeStruct(q.shape, jnp.bfloat16)
    inputs = (lengths, do, q, k, v, att, lse)
    kernel = functools.partial(backward_kernel, seq, width // HEADS)
    return pl.pallas_call(
        functools.partial(skip_refs, kernel, len(inputs), len(before)),
        grid_spec=pltpu.PrefetchScalarGridSpec(
            num_scalar_prefetch=1,
            grid=(1,),
            in_specs=[rows] * 5
            + [pl.BlockSpec((None, pairs, 2, slots), lambda i, *_: (seq, part, 0, 0))]
            + [ANYWHERE] * len(before),
            out_specs=[rows] * 3,
            scratch_shapes=[pltpu.VMEM((count, slots), jnp.bfloat16)] * 5,
        ),
        out_shape=[low, low, low],
        input_output_aliases={len(inputs) + i: i for i in range(len(before))},
        compiler_params=pltpu.CompilerParams(vmem_limit_bytes=VMEM_BYTES),
        cost_estimate=estimate(14 // parts),
        name="attend_backward",
    )(*inputs, *before)


def pack_gradients(sums_feed, sums_in, hsum, small, columns):
    parts, _, lanes = small.shape
    lanes = min(128, lanes)
    width, share = sums_feed.shape[1], hsum.shape[1] // parts
    rows = share // columns

    def chosen(count, start):
        row = lax.broadcasted_iota(jnp.int32, (count, lanes), 0)
        column = lax.broadcasted_iota(jnp.int32, (count, lanes), 1)
        return ((row - start == column) & (column < columns)).astype(jnp.float32).astype(jnp.bfloat16)

    small[...] = jnp.zeros_like(small)
    listed = (
        [*sums_in, sums_feed[5:6], sums_feed[2:3]]
        + [jnp.zeros((rows, width), jnp.float32)]
        + [sums_feed[3:4], sums_feed[0:1], sums_feed[4:5], sums_feed[1:2]]
    )
    pad = SMALL_ROWS - 8 - rows
    lined = jnp.concatenate(listed + [jnp.zeros((pad, width), jnp.float32)], axis=0)
    lined = lined.astype(jnp.bfloat16)
    hidden = [hsum[:, dp * share : (dp + 1) * share] for dp in range(parts)]
    hidden = jnp.concatenate(hidden, axis=0).astype(jnp.bfloat16)
    spread = [dot(hidden, chosen(share, k * columns)) for k in range(rows)]
    for dp in range(parts):
        here = dot(lined, chosen(width, dp * columns))
        own = [spread[k][dp : dp + 1] for k in range(rows)]
        here = jnp.concatenate([here[:4]] + own + [here[4 + rows :]], axis=0)
        small[dp, :, 0:lanes] = here.astype(jnp.bfloat16)


def project_grads_kernel(
    cuts, columns, me_ref, x_ref, dq_ref, dk_ref, dv_ref, sums_feed, hsum, *rest
):
    xt, held, small, sems = rest[-4:]
    outs = rest[:-4]
    xt[...] = x_ref[...].T
    started = []
    for which, ref in enumerate((dq_ref, dk_ref, dv_ref)):
        held[which] = dot(xt[...], ref[...]).astype(jnp.bfloat16)
        if cuts is None:
            outs[which][...] = held[which]
            continue
        width, half, third = held.shape[2], (cuts[0].rows + cuts[1].rows - SMALL_ROWS) // 3, 0
        third = cuts[0].rows - SMALL_ROWS - half
        spans = [(0, 0, half, 0)], [(1, 0, half, 0)], [(0, 0, third, half), (1, third, half - third, half)]
        used = 0
        for i, offset, count, at in spans[which]:
            if count == 0:
                continue
            cut = cuts[i]
            ends = [(p * cut.width, p, 0, cut.width) for p in range(width // cut.width)]
            made = piece_copies(
                held.at[which], outs[2 * i : 2 * i + 2],
                sems.at[which, pl.ds(used, width // half * len(ends))],
                me_ref, cut.stages, 0, width // (2 * half), half, (offset, count, at), ends,
            )
            used += len(made)
            started += run_all(made)
    if cuts is not None:
        sums_in = [
            jnp.sum(ref[...].astype(jnp.float32), axis=0, keepdims=True) for ref in (dq_ref, dv_ref)
        ]
        pack_gradients(sums_feed[...], sums_in, hsum[...], small, columns)
        started += run_all(
            small_copies(
                small, outs[:2], sems.at[3], me_ref, cuts[0].stages, cuts[0].rows - SMALL_ROWS, small.shape[0],
                held.shape[2] // cuts[0].width,
            )
        )
    wait_all(started)


def project_grads(me, x, dq, dk, dv, sums, cuts, dp_size, columns):
    total, width = x.shape
    grad = jax.ShapeDtypeStruct((width, width), jnp.bfloat16)
    direct = cuts is not None
    copies = 4 * dp_size * (width // cuts[0].width) if direct else 1
    piece = cuts[0].width if direct else 128
    return pl.pallas_call(
        functools.partial(project_grads_kernel, cuts, columns),
        in_specs=[SCALARS] + [HERE] * 6,
        out_specs=[ANYWHERE] * 4 if direct else [HERE] * 3,
        out_shape=[shape for cut in cuts for shape in cut.shapes()] if direct else [grad] * 3,
        scratch_shapes=[
            pltpu.VMEM((width, total), jnp.bfloat16),
            pltpu.VMEM((3, width, width), jnp.bfloat16),
            pltpu.VMEM((dp_size if direct else 1, SMALL_ROWS, piece), jnp.bfloat16),
            pltpu.SemaphoreType.DMA((4, copies)),
        ],
        compiler_params=pltpu.CompilerParams(vmem_limit_bytes=VMEM_BYTES),
        cost_estimate=estimate(8),
        name="project_grads",
    )(me, x, dq, dk, dv, *sums)


def input_grad_kernel(source, me_ref, gf_ref, dq_ref, dk_ref, dv_ref, *refs):
    inputs, (out_ref, weights, sems) = refs[:-3], refs[-3:]
    started = [
        run_all(source.copies(i, inputs, weights.at[i], sems.at[i], me_ref)) for i in range(3)
    ]
    grad = gf_ref[...]
    for i, ref in enumerate((dq_ref, dk_ref, dv_ref)):
        wait_all(started[i])
        grad = grad + dot_last(ref[...], weights[i])
    out_ref[...] = grad.astype(jnp.bfloat16)


def input_grads(me, gf, dq, dk, dv, source):
    total, width = dq.shape
    return pl.pallas_call(
        functools.partial(input_grad_kernel, source),
        in_specs=[SCALARS] + [HERE] * 4 + [ANYWHERE] * len(source.operands),
        out_specs=HERE,
        out_shape=jax.ShapeDtypeStruct((total, width), jnp.bfloat16),
        scratch_shapes=[
            pltpu.VMEM((3, width, width), jnp.bfloat16),
            pltpu.SemaphoreType.DMA((3, source.count((width, width)))),
        ],
        compiler_params=pltpu.CompilerParams(vmem_limit_bytes=VMEM_BYTES),
        cost_estimate=estimate(8),
        name="input_grads",
    )(me, gf, dq, dk, dv, *source.operands)


def after(values, *others):
    return lax.optimization_barrier((values, others))[0]


def meet(values, parts):
    values, arriving = lax.optimization_barrier((values, [part.arriving for part in parts]))
    for part, value in zip(parts, arriving):
        part.arriving = value
    return values


class Attention:
    def __init__(self, me, inputs, lengths, source, given, columns, hidden_count):
        self.me, self.inputs, self.lengths, self.source = me, inputs, lengths, source
        self.given, self.sizes = given, (columns, hidden_count)
        self.state, self.back = (), ()

    def forward(self, seq):
        *state, self.vectors, self.hidden_bias = attend_forward(
            seq, self.me, self.inputs, self.lengths, self.source, self.given, *self.sizes, self.state
        )
        self.state = tuple(state)

    def backward(self, seq, part, parts, do):
        self.back = tuple(
            attend_backward(seq, part, parts, do, *self.state, self.lengths, self.back)
        )


def layer_step(inputs, lengths, upstream, gather, scatter):
    shape = inputs.shape
    flat = (shape[0] * shape[1], shape[2])
    seqs = shape[0]
    source, given = gather.first()
    bias, hidden = gather.shards[6:8]
    me = gather.me
    columns = bias.shape[1]
    attention = Attention(
        me, inputs, lengths, source, given, columns, hidden.shape[0] * scatter.dp_size
    )
    for seq in range(seqs):
        attention.inputs = gather.before(seq, attention.inputs)
        attention.forward(seq)
        attention.state = gather.after(seq, attention.state)
    outputs, gf, do, hidden_sum, sums_feed, *grads = feed(
        me, lengths, inputs, attention.state[3], upstream, attention.hidden_bias,
        attention.vectors, gather.second(), scatter.feed_cuts,
    )
    parts = 2
    scatter.feed(grads)
    for at in range(seqs * parts):
        attention.backward(at // parts, at % parts, parts, do.reshape(shape))
        attention.back = scatter.step(at, attention.back)
    dq, dk, dv = (grad.reshape(flat) for grad in attention.back)
    sums = (sums_feed, hidden_sum)
    scatter.ends = (dq, dv)
    results = project_grads(
        me, inputs.reshape(flat), dq, dk, dv, sums, scatter.first_cuts, scatter.dp_size, columns
    )
    gf = scatter.last(results, sums, gf)
    input_grad = input_grads(me, gf, dq, dk, dv, source)
    input_grad, totals = scatter.totals(input_grad)
    return outputs.reshape(shape), input_grad.reshape(shape), totals


def split_up(value, dim, size):
    before, after = (value.shape[:dim], value.shape[dim + 1 :])
    return jnp.moveaxis(value.reshape(*before, size, -1, *after), dim, 0)


def sum_at_owner(value, axis, dim):
    size = lax.axis_size(axis)
    parts = lax.all_to_all(split_up(value, dim, size), axis, 0, 0, tiled=True)
    return jnp.sum(parts.astype(jnp.float32), axis=0)


def side_by_side(arrays, axis, dim, along):
    ends, at = ([], 0)
    for a in arrays[:-1]:
        at += a.shape[along]
        ends.append(at)
    both = jnp.concatenate(arrays, axis=along)
    return tuple(jnp.split(sum_at_owner(both, axis, dim), ends, axis=along))


def gather_forward(shards):
    (
        query_part,
        key_part,
        value_part,
        output_part,
        inner_part,
        outer_part,
        bias_part,
        hidden_part,
        gain_part,
        shift_part,
    ) = shards
    column_full = (
        lax.all_gather(query_part, "fsdp", axis=1, tiled=True),
        lax.all_gather(key_part, "fsdp", axis=1, tiled=True),
        lax.all_gather(value_part, "fsdp", axis=1, tiled=True),
        lax.all_gather(output_part, "fsdp", axis=1, tiled=True),
        lax.all_gather(inner_part, "fsdp", axis=1, tiled=True),
        lax.all_gather(outer_part, "fsdp", axis=1, tiled=True),
    )
    return (
        lax.all_gather(column_full[0], "dp", axis=0, tiled=True),
        lax.all_gather(column_full[1], "dp", axis=0, tiled=True),
        lax.all_gather(column_full[2], "dp", axis=0, tiled=True),
        lax.all_gather(column_full[3], "dp", axis=0, tiled=True),
        lax.all_gather(column_full[4], "dp", axis=0, tiled=True),
        lax.all_gather(column_full[5], "dp", axis=0, tiled=True),
        lax.all_gather(bias_part, "dp", axis=1, tiled=True),
        lax.all_gather(hidden_part, "dp", axis=0, tiled=True),
        lax.all_gather(gain_part, "dp", axis=1, tiled=True),
        lax.all_gather(shift_part, "dp", axis=1, tiled=True),
    )


def reduce_grads(grads):
    (
        query_grad,
        key_grad,
        value_grad,
        output_grad,
        inner_grad,
        outer_grad,
        bias_grad,
        hidden_grad,
        gain_grad,
        shift_grad,
    ) = grads
    bias_grad, hidden_grad, gain_grad, shift_grad = (
        lax.psum(bias_grad.astype(jnp.bfloat16), "fsdp").astype(jnp.float32),
        lax.psum(hidden_grad.astype(jnp.bfloat16), "fsdp").astype(jnp.float32),
        lax.psum(gain_grad.astype(jnp.bfloat16), "fsdp").astype(jnp.float32),
        lax.psum(shift_grad.astype(jnp.bfloat16), "fsdp").astype(jnp.float32),
    )
    narrow = (
        lax.psum_scatter(
            query_grad.astype(jnp.bfloat16), "fsdp", scatter_dimension=1, tiled=True
        ).astype(jnp.float32),
        lax.psum_scatter(
            key_grad.astype(jnp.bfloat16), "fsdp", scatter_dimension=1, tiled=True
        ).astype(jnp.float32),
        lax.psum_scatter(
            value_grad.astype(jnp.bfloat16), "fsdp", scatter_dimension=1, tiled=True
        ).astype(jnp.float32),
        lax.psum_scatter(
            output_grad.astype(jnp.bfloat16), "fsdp", scatter_dimension=1, tiled=True
        ).astype(jnp.float32),
        lax.psum_scatter(
            inner_grad.astype(jnp.bfloat16), "fsdp", scatter_dimension=1, tiled=True
        ).astype(jnp.float32),
        lax.psum_scatter(
            outer_grad.astype(jnp.bfloat16), "fsdp", scatter_dimension=1, tiled=True
        ).astype(jnp.float32),
    )
    return (
        *side_by_side(
            (
                narrow[0].astype(jnp.bfloat16),
                narrow[1].astype(jnp.bfloat16),
                narrow[2].astype(jnp.bfloat16),
                narrow[3].astype(jnp.bfloat16),
                narrow[4].astype(jnp.bfloat16),
            ),
            "dp",
            0,
            1,
        ),
        sum_at_owner(narrow[5].astype(jnp.bfloat16), "dp", 0),
        sum_at_owner(bias_grad.astype(jnp.bfloat16), "dp", 1),
        sum_at_owner(hidden_grad.astype(jnp.bfloat16), "dp", 0),
        *side_by_side(
            (gain_grad.astype(jnp.bfloat16), shift_grad.astype(jnp.bfloat16)), "dp", 1, 0
        ),
    )


def pack_small(bias, hidden, gains, shifts, width):
    columns = bias.shape[-1]
    rows = jnp.concatenate([bias, hidden.reshape(-1, columns), gains, shifts], axis=0)
    return jnp.pad(rows, ((0, SMALL_ROWS - rows.shape[0]), (0, width - columns)))


class Gather:
    def __init__(self, mesh, shards, me):
        self.mesh, self.shards, self.me = mesh, shards, me
        self.orders = stage_orders(mesh)

    def prepare(self):
        query, key, value, output, inner, outer, bias, hidden, gains, shifts = self.shards
        half, half_outer = query.shape[0] // 2, outer.shape[0] // 2
        small = pack_small(bias, hidden, gains, shifts, 2 * query.shape[1])

        def both(*arrays):
            halves = [array[: array.shape[0] // 2] for array in arrays]
            halves += [array[array.shape[0] // 2 :] for array in arrays]
            return jnp.concatenate(halves, axis=0)

        one, rest, inner = pair_up((both(query, key, value), both(output, outer), inner))
        self.one = [
            jnp.concatenate([one[:half], small], axis=0)[None],
            one[half : 2 * half][None],
            one[2 * half :][None],
        ]
        split = self.split = FeedSplit(half, half_outer, 2 * query.shape[1], inner.shape[1])
        folded = inner[half - split.extra :].reshape(split.extra, split.groups, split.width)
        folded = folded.swapaxes(0, 1).reshape(split.groups * split.extra, split.width)
        self.two = [
            inner[: half - split.extra][None],
            rest[half : half + split.most][None],
            jnp.concatenate([rest[:half], rest[half + split.most :], folded], axis=0)[None],
        ]

    def send(self, parts, stage):
        return [swap(part, *self.orders[i][stage]) for i, part in enumerate(parts)]

    def join(self, parts, received):
        return [jnp.concatenate(pair, axis=0) for pair in zip(parts, received)]

    def first(self):
        self.prepare()
        count = len(self.orders[0])
        self.stage = 0
        for stage in range(count):
            arriving = self.send(self.one, stage)
            ahead = None
            if stage >= count - 2:
                self.two = after(self.two, self.one)
                ahead = self.send(self.two, self.stage)
                self.stage += 1
            self.one = self.join(self.one, arriving)
            if ahead is not None:
                self.two = self.join(self.two, after(ahead, self.one))
        self.two = after(self.two, self.one)
        others = [swap(part, "fsdp", 0) for part in self.one]
        half, width = self.shards[0].shape[0] // 2, self.one[0].shape[2]
        spots = [(half, width, [(i, 0, 0, half, 0)]) for i in range(3)]
        operands = [array for pair in zip(self.one, others) for array in pair]
        return Source(operands, self.orders, spots, self.mesh.shape["dp"], half), ()

    def before(self, seq, inputs):
        if self.stage == len(self.orders[0]):
            return inputs
        self.arriving = self.send(self.two, self.stage)
        self.stage += 1
        return after(inputs, self.two)

    def after(self, seq, state):
        if self.arriving is None:
            return state
        arriving = after(self.arriving, state)
        self.two, self.arriving = self.join(self.two, arriving), None
        return state

    def second(self):
        while self.stage < len(self.orders[0]):
            self.two = self.join(self.two, self.send(self.two, self.stage))
            self.stage += 1
        others = [swap(part, "fsdp", 0) for part in self.two]
        operands = [array for pair in zip(self.two, others) for array in pair]
        return Source(operands, self.orders, self.split.spots(), self.mesh.shape["dp"])


class Part:
    def __init__(self, keep, send, stages):
        self.keep, self.stages = keep, list(stages)
        self.arriving = swap(send, "fsdp", 0)

    def step(self):
        axis, bit = self.stages.pop()
        half = self.keep.shape[0] // 2
        send = total_of(self.keep[half:], self.arriving[half:], jnp.bfloat16)
        arriving = swap(send, axis, bit)
        self.keep = total_of(self.keep[:half], self.arriving[:half], jnp.bfloat16)
        self.arriving = arriving
        return send

    def finish(self):
        while self.stages:
            self.step()
        return total_of(self.keep, self.arriving, jnp.float32)[0]


class Scatter:
    def __init__(self, mesh, shards, me):
        self.shards = shards
        self.orders = stage_orders(mesh)
        width, width_inner = 2 * shards[0].shape[1], 2 * shards[4].shape[1]
        half, half_outer = shards[0].shape[0] // 2, shards[5].shape[0] // 2
        self.dp_size = mesh.shape["dp"]
        self.split = FeedSplit(half, half_outer, width, width_inner)
        self.feed_cuts = FeedCuts(self.orders, self.split)
        self.third = half // 3 // 16 * 16
        rows = (half + self.third + SMALL_ROWS, 2 * half - self.third)
        self.first_cuts = [Cut(order, r, width) for order, r in zip(self.orders, rows)]

    def feed(self, grads):
        self.behind = [
            Part(*grads[2 * i : 2 * i + 2], cut.stages) for i, cut in enumerate(self.feed_cuts.cuts)
        ]

    def step(self, at, state):
        parts = {0: self.behind, 2: self.behind[2:], 3: self.behind}.get(at, [])
        if not parts:
            return state
        state = meet(state, parts)
        return after(state, [part.step() for part in parts])

    def last(self, results, sums, passing):
        results = meet(results, self.behind)
        self.front = [
            Part(*results[2 * i : 2 * i + 2], cut.stages) for i, cut in enumerate(self.first_cuts)
        ]
        sent = [part.step() for part in self.behind]
        meet((), self.front)
        sent += [part.step() for part in self.front]
        return after(passing, sent)

    def totals(self, passing):
        half, half_outer = self.shards[0].shape[0] // 2, self.shards[5].shape[0] // 2
        columns = self.shards[6].shape[1]
        parts = self.front + self.behind
        passing = meet(passing, parts)
        while any(part.stages for part in parts):
            for part in parts:
                if part.stages:
                    part.step()
            meet((), parts)
        one, two = [part.finish() for part in self.front]
        third = self.third
        inner, outer, rest = [part.finish() for part in self.behind]
        thirds = [one[half : half + third], two[half:]]
        query, key, value = settle(jnp.concatenate([one[:half], two[:half], *thirds]), (half,) * 3)
        split = self.split
        folded = rest[split.folded :].reshape(split.groups, split.extra, split.width)
        folded = folded.swapaxes(0, 1).reshape(split.extra, split.width_inner)
        (inner,) = settle(jnp.concatenate([inner, folded], axis=0), (half,))
        outer = jnp.concatenate([outer, rest[half : split.folded]], axis=0)
        output, outer = settle(jnp.concatenate([rest[:half], outer]), (half, half_outer))
        rows = one[half + third :, :columns]
        split = 4 + self.shards[7].shape[0] // columns
        return passing, (
            query, key, value, output, inner, outer,
            rows[:4], rows[4:split].reshape(-1), rows[split : split + 2], rows[split + 2 : split + 4],
        )


class PlainGather:
    def __init__(self, mesh, shards, me):
        self.shards, self.me = shards, me

    def first(self):
        arrays = gather_forward(self.shards)
        self.rest = arrays[3:6]
        bias, hidden, gains, shifts = arrays[6:]
        vectors = jnp.concatenate([bias, gains, shifts], axis=0).astype(jnp.float32)
        return Source(arrays[:3]), (vectors, hidden.astype(jnp.float32)[None])

    def before(self, seq, inputs):
        return inputs

    def after(self, seq, state):
        return state

    def second(self):
        return Source(self.rest)


class PlainScatter:
    def __init__(self, mesh, shards, me):
        self.feed_cuts = self.first_cuts = None
        self.dp_size = mesh.shape["dp"]

    def feed(self, grads):
        self.grads = grads

    def step(self, at, state):
        return state

    def last(self, results, sums, passing):
        (feed, hidden), (dq, dv) = sums, self.ends
        ends = [jnp.sum(d.astype(jnp.float32), axis=0, keepdims=True) for d in (dq, dv)]
        bias = jnp.concatenate([*ends, feed[5:6], feed[2:3]], axis=0)
        gains = jnp.concatenate([feed[3:4], feed[:1]], axis=0)
        shifts = jnp.concatenate([feed[4:5], feed[1:2]], axis=0)
        self.grads = (*results, *self.grads, bias, hidden[0], gains, shifts)
        return passing

    def totals(self, passing):
        return passing, reduce_grads(self.grads)


def on_device(
    mesh,
    tokens,
    lengths,
    cotangent,
    *shards,
):
    me = jnp.stack([lax.axis_index("dp"), lax.axis_index("fsdp")]).astype(jnp.int32)
    rows = (shards[0].shape[0], shards[5].shape[0])
    direct = fits(mesh, rows, shards[0].shape[1], shards[7].shape[0])
    gather = (Gather if direct else PlainGather)(mesh, shards, me)
    scatter = (Scatter if direct else PlainScatter)(mesh, shards, me)
    shape = (-1, *tokens.shape[2:])
    outputs, grad_inputs, totals = layer_step(
        tokens.reshape(shape), lengths.reshape(-1), cotangent.reshape(shape), gather, scatter
    )
    return (outputs.reshape(tokens.shape), grad_inputs.reshape(tokens.shape), *totals)


def solution(mesh):
    placed = (
        P(None, ("dp", "fsdp"), None, None),
        P(None, ("dp", "fsdp")),
        P(None, ("dp", "fsdp"), None, None),
        P("dp", "fsdp"),
        P("dp", "fsdp"),
        P("dp", "fsdp"),
        P("dp", "fsdp"),
        P("dp", "fsdp"),
        P("dp", "fsdp"),
        P(None, "dp"),
        P("dp"),
        P(None, "dp"),
        P(None, "dp"),
    )
    return jax.shard_map(
        functools.partial(on_device, mesh),
        mesh=mesh,
        in_specs=placed,
        out_specs=(
            P(None, ("dp", "fsdp"), None, None),
            P(None, ("dp", "fsdp"), None, None),
            P("dp", "fsdp"),
            P("dp", "fsdp"),
            P("dp", "fsdp"),
            P("dp", "fsdp"),
            P("dp", "fsdp"),
            P("dp", "fsdp"),
            P(None, "dp"),
            P("dp"),
            P(None, "dp"),
            P(None, "dp"),
        ),
        check_vma=False,
    )
```

```python
import functools
import jax
import jax.numpy as jnp
from jax import lax
from jax.experimental import pallas as pl
from jax.experimental.pallas import tpu as pltpu
from jax.sharding import PartitionSpec as P

HEADS = 12


EPSILON = 1e-12
MASKED = -1000000000.0
SMALL_ROWS = 16


def swap(value, axis, bit):
    size = lax.axis_size(axis)
    return lax.ppermute(value, axis, [(i, i ^ (1 << bit)) for i in range(size)])


def stage_orders(mesh):
    dp_bits = mesh.shape["dp"].bit_length() - 1
    fsdp_bits = mesh.shape["fsdp"].bit_length() - 1
    far = [("dp", b) for b in range(dp_bits - 1, 0, -1)]
    across = [("fsdp", b) for b in range(fsdp_bits - 1, 0, -1)]
    near = [("dp", 0)]
    return (far + across + near, far + near + across, across + near + far)


def far_stages(mesh):
    return mesh.shape["dp"].bit_length() - 2


def third_of(half):
    return half // 3 // 16 * 16


def fits(mesh, rows, width, hidden):
    sizes = (mesh.shape["dp"], mesh.shape["fsdp"])
    powers = all(s >= 2 and s & (s - 1) == 0 for s in sizes)
    return powers and all(r % 32 == 0 for r in rows) and width % 64 == 0 and hidden % 128 == 0 and 96 <= rows[0] <= 128


def place_of(stages, dp, fsdp, me_ref):
    index = {"dp": dp ^ me_ref[0], "fsdp": fsdp ^ me_ref[1]}
    place = 0
    for s, (axis, bit) in enumerate(stages):
        place = place + (((index[axis] >> bit) & 1) << s)
    return place


def piece_copies(source, outs, sems, me_ref, stages, first_dp, count_dp, half, span, columns):
    copies = []
    offset, rows, at = span
    for i in range(count_dp):
        dp = first_dp + i
        for flip in range(2):
            fsdp = (me_ref[1] & 1) ^ flip
            row = pl.multiple_of((2 * i + fsdp) * half + offset, 16)
            for start, pair, into, count in columns:
                place = place_of(stages, dp, 2 * pair + fsdp, me_ref)
                copies.append(
                    pltpu.make_async_copy(
                        source.at[pl.ds(row, rows), pl.ds(start, count)],
                        outs[flip].at[place, pl.ds(at, rows), pl.ds(into, count)],
                        sems.at[len(copies)],
                    )
                )
    return copies


class Source:
    def __init__(self, operands, stages=(), spots=(), dp_size=0, small_at=None):
        self.operands, self.stages, self.spots = tuple(operands), stages, spots
        self.dp_size, self.small_at = dp_size, small_at

    def count(self, shape):
        if not self.spots:
            return 1
        return 2 * self.dp_size * max(shape[1] // width * len(spans) for _, width, spans in self.spots)

    def copies(self, which, refs, target, sems, me_ref):
        if not self.spots:
            return [pltpu.make_async_copy(refs[which], target, sems.at[0])]
        half, width, spans = self.spots[which]
        copies = []
        for part, at, offset, rows, column in spans:
            count = self.operands[2 * part].shape[2]
            for dp in range(self.dp_size):
                for flip in range(2):
                    fsdp = (me_ref[1] & 1) ^ flip
                    row = pl.multiple_of((2 * dp + fsdp) * half + offset, 16)
                    for pair in range(target.shape[1] // width):
                        place = place_of(self.stages[part], dp, 2 * pair + fsdp, me_ref)
                        copies.append(
                            pltpu.make_async_copy(
                                refs[2 * part + flip].at[place, pl.ds(at, rows), :],
                                target.at[pl.ds(row, rows), pl.ds(pair * width + column, count)],
                                sems.at[len(copies)],
                            )
                        )
        return copies

    def small_copies(self, refs, target, sems, me_ref):
        copies = []
        for dp in range(self.dp_size):
            place = place_of(self.stages[0], dp, me_ref[1], me_ref)
            source = refs[0].at[place, pl.ds(self.small_at, SMALL_ROWS), :]
            copies.append(pltpu.make_async_copy(source, target.at[dp], sems.at[dp]))
        return copies

    def pick(self, which):
        if not self.spots:
            return Source([self.operands[i] for i in which])
        return Source(self.operands, self.stages, [self.spots[i] for i in which], self.dp_size)


def lay_vectors(small, columns, hidden_count, vec_ref, hb_ref):
    lanes = min(128, small.shape[2])
    width = vec_ref.shape[1]
    parts = small.shape[0]

    def chosen(to, start):
        row = lax.broadcasted_iota(jnp.int32, (lanes, to), 0)
        column = lax.broadcasted_iota(jnp.int32, (lanes, to), 1)
        return ((column - start == row) & (row < columns)).astype(jnp.float32).astype(jnp.bfloat16)

    total = jnp.zeros((SMALL_ROWS, width), jnp.float32)
    for dp in range(parts):
        total = total + dot(small[dp, :, :lanes], chosen(width, dp * columns))
    share = hidden_count // parts
    rows = share // columns
    vec_ref[0:4, :] = total[0:4]
    vec_ref[4:8, :] = total[4 + rows : 8 + rows]
    flat = small[:, :, :lanes].reshape(parts * SMALL_ROWS, lanes)
    spread = [dot(flat, chosen(share, k * columns)) for k in range(rows)]
    for dp in range(parts):
        at = dp * SMALL_ROWS + 4
        hb_ref[:, dp * share : (dp + 1) * share] = sum(
            spread[k][at + k : at + k + 1] for k in range(rows)
        )


def small_copies(source, outs, sems, me_ref, stages, at, dp_size, pairs):
    copies = []
    for dp in range(dp_size):
        for flip in range(2):
            fsdp = (me_ref[1] & 1) ^ flip
            for pair in range(pairs):
                place = place_of(stages, dp, 2 * pair + fsdp, me_ref)
                copies.append(
                    pltpu.make_async_copy(
                        source.at[dp],
                        outs[flip].at[place, pl.ds(at, SMALL_ROWS), :],
                        sems.at[len(copies)],
                    )
                )
    return copies


def run_all(copies):
    for copy in copies:
        copy.start()
    return copies


def wait_all(copies):
    for copy in copies:
        copy.wait()


def total_of(left, right, kind):
    return (left.astype(jnp.float32) + right.astype(jnp.float32)).astype(kind)


def settle(total, rows):
    width = total.shape[-1] // 2
    count = sum(rows)
    second = lax.axis_index("fsdp") & 1
    own = jnp.where(second == 0, total[:count, :width], total[:count, width:])
    away = jnp.where(second == 0, total[:count, width:], total[:count, :width])
    came = swap(away.astype(jnp.bfloat16), "fsdp", 0).astype(jnp.float32)
    first, last = jnp.where(second == 0, own, came), jnp.where(second == 0, came, own)
    outs, at = [], 0
    for half in rows:
        outs.append(jnp.concatenate([first[at : at + half], last[at : at + half]], axis=0))
        at += half
    return outs


def pair_up(shards):
    second = lax.axis_index("fsdp") & 1
    outs = []
    for shard in shards:
        half = shard.shape[0] // 2
        mine = jnp.where(second == 0, shard[:half], shard[half:])
        away = jnp.where(second == 0, shard[half:], shard[:half])
        came = swap(away, "fsdp", 0)
        outs.append(
            jnp.where(
                second == 0,
                jnp.concatenate([mine, came], axis=1),
                jnp.concatenate([came, mine], axis=1),
            )
        )
    return outs


VMEM_BYTES = 56 << 20
FEED_BYTES = 60 << 20


def estimate(micros):
    return pl.CostEstimate(flops=micros * 1000000000, bytes_accessed=micros * 1000000, transcendentals=0)


def dot(left, right):
    return jnp.dot(left, right, preferred_element_type=jnp.float32)


def dot_last(left, right):
    return lax.dot_general(
        left, right, (((1,), (1,)), ((), ())), preferred_element_type=jnp.float32
    )


def dot_first(left, right):
    return lax.dot_general(
        left, right, (((0,), (0,)), ((), ())), preferred_element_type=jnp.float32
    )


def normalize(values):
    centered = values - jnp.mean(values, axis=-1, keepdims=True)
    variance = jnp.mean(centered * centered, axis=-1, keepdims=True)
    factor = lax.rsqrt(variance + EPSILON)
    return (centered * factor, factor)


def norm_back(upward, normed, factor):
    return factor * (
        upward
        - jnp.mean(upward, axis=-1, keepdims=True)
        - normed * jnp.mean(upward * normed, axis=-1, keepdims=True)
    )


def gelu_pair(v):
    size = jnp.abs(v) * 0.7071067811865476
    t = 1.0 / (1.0 + 0.3275911 * size)
    bell = jnp.exp(-size * size)
    poly = t * (
        0.254829592
        + t * (-0.284496736 + t * (1.421413741 + t * (-1.453152027 + t * 1.061405429)))
    )
    tail = 0.5 * poly * bell
    cdf = jnp.where(v >= 0.0, 1.0 - tail, tail)
    return v * cdf, cdf + v * bell * 0.3989422804014327


def three_parts(value):
    high = value.astype(jnp.bfloat16).astype(jnp.float32)
    rest = value - high
    middle = rest.astype(jnp.bfloat16).astype(jnp.float32)
    return high, middle, rest - middle


def head_keys(pair, head, length, with_stats):
    rows, lanes = pair.shape
    lane = lax.broadcasted_iota(jnp.int32, (rows, lanes), 1)
    row = lax.broadcasted_iota(jnp.int32, (rows, lanes), 0)
    start = lanes // 2 if head == 0 else 0
    own = lane < lanes // 2 if head == 0 else lane >= lanes // 2
    hidden = jnp.where((lane == start) & (row >= length), MASKED, 0.0)
    if with_stats:
        hidden = jnp.where((lane > start) & (lane < start + 4), 1.0, hidden)
    return jnp.where(own, pair.astype(jnp.float32), hidden).astype(jnp.bfloat16)


def head_values(pair, head):
    rows, lanes = pair.shape
    lane = lax.broadcasted_iota(jnp.int32, (rows, lanes), 1)
    start = lanes // 2 if head == 0 else 0
    own = lane < lanes // 2 if head == 0 else lane >= lanes // 2
    ones = jnp.where((lane >= start) & (lane < start + 3), 1.0, 0.0)
    return jnp.where(own, pair.astype(jnp.float32), ones).astype(jnp.bfloat16)


def only_head(pair, head):
    lane = lax.broadcasted_iota(jnp.int32, pair.shape, 1)
    own = lane < pair.shape[1] // 2 if head == 0 else lane >= pair.shape[1] // 2
    return jnp.where(own, pair.astype(jnp.float32), 0.0).astype(jnp.bfloat16)


def with_rows(part, head, rows):
    count, width = part.shape
    row = lax.broadcasted_iota(jnp.int32, (count, width), 0)
    extra = jnp.zeros((count, width), jnp.float32)
    for i, value in enumerate(rows):
        extra = jnp.where(row == i, value, extra)
    extra = extra.astype(jnp.bfloat16)
    return jnp.concatenate([part, extra] if head == 0 else [extra, part], axis=0)


def forward_kernel(seq, source, columns, count_in, lengths, me_ref, x_ref, *refs):
    inputs, refs = refs[:count_in], refs[count_in:]
    q_ref, k_ref, v_ref, att_ref, lse_ref, vec_ref, hb_ref = refs[:7]
    qt, vt, ot, weights, sems, small, small_sems = refs[7:]
    length = lengths[seq]
    started = []
    for which in range(3):
        started.append(
            run_all(source.copies(which, inputs, weights.at[which], sems.at[which], me_ref))
        )
    wq_ref, wk_ref, wv_ref = (weights.at[i] for i in range(3))
    if source.spots:
        wait_all(run_all(source.small_copies(inputs, small, small_sems, me_ref)))
        lay_vectors(small[...], columns, hb_ref.shape[1], vec_ref, hb_ref)
    else:
        vec_ref[...] = inputs[-2][...]
        hb_ref[...] = inputs[-1][...]
    for copies in started:
        wait_all(copies)
    x = x_ref[...]
    head_size = x.shape[1] // HEADS
    scale = head_size**-0.5
    queries = (dot(x, wq_ref[...]) + vec_ref[0:1, :]).astype(jnp.bfloat16)
    queries = (queries.astype(jnp.float32) * scale).astype(jnp.bfloat16)
    q_ref[...] = queries
    qt[...] = queries.T
    k_ref[...] = dot(x, wk_ref[...]).astype(jnp.bfloat16)
    values = (dot(x, wv_ref[...]) + vec_ref[1:2, :]).astype(jnp.bfloat16)
    v_ref[...] = values
    vt[...] = values.T

    def one_pair(p, carry):
        base = pl.multiple_of(p * 2 * head_size, 2 * head_size)
        pair = k_ref[:, pl.ds(base, 2 * head_size)]
        for head in range(2):
            at = pl.multiple_of(base + head * head_size, head_size)
            keys = head_keys(pair, head, length, False)
            scores = dot(keys, with_rows(qt[pl.ds(at, head_size), :], head, [1.0]))
            highest = jnp.max(scores, axis=0, keepdims=True)
            exponent = jnp.exp(scores - highest)
            total = jnp.sum(exponent, axis=0, keepdims=True)
            blended = dot(vt[pl.ds(at, head_size), :], exponent.astype(jnp.bfloat16))
            ot[pl.ds(at, head_size), :] = (blended / total).astype(jnp.bfloat16)
            lse_ref[p, head : head + 1, :] = highest + jnp.log(total)
        return carry

    lax.fori_loop(0, HEADS // 2, one_pair, 0)
    att_ref[...] = ot[...].T


def whole(shape):
    return pl.BlockSpec(shape, lambda *_: (0,) * len(shape))


def skip_refs(kernel, first, count, *refs):
    kernel(*refs[:first], *refs[first + count :])


def attend_forward(seq, me, x, lengths, source, vectors, columns, hidden_count, before):
    seqs, slots, width = x.shape
    rows = pl.BlockSpec((None, slots, width), lambda i, *_: (seq, 0, 0))
    low = jax.ShapeDtypeStruct(x.shape, jnp.bfloat16)
    given = (*source.operands, *vectors)
    kernel = functools.partial(forward_kernel, seq, source, columns, len(given))
    known = 3 + len(given)
    small = (max(source.dp_size, 1), SMALL_ROWS, source.spots[0][1] if source.spots else 128)
    return pl.pallas_call(
        functools.partial(skip_refs, kernel, known, len(before)),
        grid_spec=pltpu.PrefetchScalarGridSpec(
            num_scalar_prefetch=2,
            grid=(1,),
            in_specs=[rows]
            + [ANYWHERE] * len(source.operands)
            + [whole(v.shape) for v in vectors]
            + [ANYWHERE] * len(before),
            out_specs=[rows] * 4
            + [
                pl.BlockSpec((None, HEADS // 2, 2, slots), lambda i, *_: (seq, 0, 0, 0)),
                whole((8, width)),
                whole((1, hidden_count)),
            ],
            scratch_shapes=[pltpu.VMEM((width, slots), jnp.bfloat16)] * 3
            + [
                pltpu.VMEM((3, width, width), jnp.bfloat16),
                pltpu.SemaphoreType.DMA((3, source.count((width, width)))),
                pltpu.VMEM(small, jnp.bfloat16),
                pltpu.SemaphoreType.DMA((small[0],)),
            ],
        ),
        out_shape=[low] * 4
        + [
            jax.ShapeDtypeStruct((seqs, HEADS // 2, 2, slots), jnp.float32),
            jax.ShapeDtypeStruct((8, width), jnp.float32),
            jax.ShapeDtypeStruct((1, hidden_count), jnp.float32),
        ],
        input_output_aliases={known + i: i for i in range(len(before))},
        compiler_params=pltpu.CompilerParams(vmem_limit_bytes=VMEM_BYTES),
        cost_estimate=estimate(14),
        name="attend_forward",
    )(lengths, me, x, *given, *before)


def feed_kernel(
    source, cuts, slots, lengths, me_ref, x_ref, att_ref, cot_ref, hb_ref, vec_ref, *refs
):
    count_in = len(source.operands)
    inputs, refs = refs[:count_in], refs[count_in:]
    out_ref, gf_ref, do_ref, hsum_ref, sums_ref = refs[:5]
    (
        wi, wf, wo, act, slope_s, first, mid, mid_t, low_s, held_i, held_o, held_a,
        load_a, load_i, load_o, sems, sems_a,
    ) = refs[-17:]
    grads = refs[5:-17]
    loads = [
        run_all(source.copies(which, inputs, target, sem, me_ref))
        for which, target, sem in ((0, wo, load_a), (1, wi, load_i), (2, wf, load_o))
    ]
    total, width = x_ref.shape
    inner = wi.shape[1]
    tile = min(256, slots)
    piece = min(512, inner)
    sums_ref[...] = jnp.zeros_like(sums_ref)
    wait_all(loads[0])
    first[...] = x_ref[...].astype(jnp.float32) + dot(att_ref[...], wo[...]) + vec_ref[2:3, :]
    for copies in loads[1:]:
        wait_all(copies)

    def forward(t, carry):
        rows = pl.ds(pl.multiple_of(t * tile, tile), tile)
        normed, _ = normalize(first[rows, :])
        middle = normed * vec_ref[4:5, :] + vec_ref[6:7, :]
        middle_low = middle.astype(jnp.bfloat16)
        mid[rows, :] = middle_low
        second = middle + vec_ref[3:4, :]
        def ahead(at):
            return dot(middle_low, wi[:, at : at + piece]) + hb_ref[:, at : at + piece]

        hidden = ahead(0)
        for at in range(0, inner, piece):
            here = slice(at, at + piece)
            following = ahead(at + piece) if at + piece < inner else None
            active, slope = gelu_pair(hidden)
            active = active.astype(jnp.bfloat16)
            act[rows, here] = active
            slope_s[rows, here] = slope.astype(jnp.bfloat16)
            second = second + dot(active, wf[here, :])
            hidden = following
        normed, factor = normalize(second)
        start = t * tile
        slot = start % slots + lax.broadcasted_iota(jnp.int32, (tile, 1), 0)
        mask = (slot < lengths[start // slots]).astype(jnp.float32)
        out_ref[rows, :] = ((normed * vec_ref[5:6, :] + vec_ref[7:8, :]) * mask).astype(jnp.bfloat16)
        upward = cot_ref[rows, :].astype(jnp.float32) * mask
        grad = norm_back(upward * vec_ref[5:6, :], normed, factor)
        gf_ref[rows, :] = grad
        low = grad.astype(jnp.bfloat16)
        low_s[rows, :] = low
        sums_ref[0:1, :] += jnp.sum(upward * normed, axis=0, keepdims=True)
        sums_ref[1:2, :] += jnp.sum(upward, axis=0, keepdims=True)
        sums_ref[2:3, :] += jnp.sum(low.astype(jnp.float32), axis=0, keepdims=True)
        return carry

    lax.fori_loop(0, total // tile, forward, 0, unroll=2)
    mid_t[...] = mid[...].T
    chunk = held_i.shape[2]
    steps = inner // chunk

    def copies(step):
        slot = step % 2
        if cuts is None:
            start = pl.multiple_of(step * chunk, chunk)
            return [
                pltpu.make_async_copy(
                    held_o.at[slot], grads[2].at[pl.ds(start, chunk), :], sems.at[slot, 0]
                ),
                pltpu.make_async_copy(
                    held_i.at[slot], grads[1].at[:, pl.ds(start, chunk)], sems.at[slot, 1]
                ),
            ]
        made, split = [], cuts.split
        blocks = chunk // (2 * split.half_outer)
        for cut, outs, span, columns in cuts.outer(grads, width):
            made += piece_copies(
                held_o.at[slot], outs, sems.at[slot, pl.ds(len(made), 2 * blocks * len(columns))],
                me_ref, cut.stages, step * blocks, blocks, split.half_outer, span, columns,
            )
        for cut, outs, span, columns in cuts.inner(grads, step, chunk):
            made += piece_copies(
                held_i.at[slot], outs, sems.at[slot, pl.ds(len(made), width // split.half)],
                me_ref, cut.stages, 0, width // (2 * split.half), split.half, span, columns,
            )
        return made

    def backward(step, carry):
        here = pl.ds(pl.multiple_of(step * chunk, chunk), chunk)
        low = low_s[...]
        up = dot_last(low, wf[here, :]) * slope_s[:, here].astype(jnp.float32)
        hidden = up.astype(jnp.bfloat16)
        hsum_ref[:, here] = jnp.sum(hidden.astype(jnp.float32), axis=0, keepdims=True)

        @pl.when(step >= 2)
        def _():
            wait_all(copies(step - 2))

        held_o[step % 2] = dot_first(act[:, here], low).astype(jnp.bfloat16)
        held_i[step % 2] = dot(mid_t[...], hidden).astype(jnp.bfloat16)
        run_all(copies(step))
        gf_ref[...] += dot_last(hidden, wi[:, here])
        return carry

    lax.fori_loop(0, steps, backward, 0, unroll=4)

    def finish(t, carry):
        rows = pl.ds(pl.multiple_of(t * tile, tile), tile)
        grad_middle = gf_ref[rows, :]
        normed, factor = normalize(first[rows, :])
        sums_ref[3:4, :] += jnp.sum(grad_middle * normed, axis=0, keepdims=True)
        sums_ref[4:5, :] += jnp.sum(grad_middle, axis=0, keepdims=True)
        grad_first = norm_back(grad_middle * vec_ref[4:5, :], normed, factor)
        gf_ref[rows, :] = grad_first
        branch = grad_first.astype(jnp.bfloat16)
        low_s[rows, :] = branch
        sums_ref[5:6, :] += jnp.sum(branch.astype(jnp.float32), axis=0, keepdims=True)
        do_ref[rows, :] = dot_last(branch, wo[...]).astype(jnp.bfloat16)
        return carry

    lax.fori_loop(0, total // tile, finish, 0, unroll=4)
    held_a[...] = dot_first(att_ref[...], low_s[...]).astype(jnp.bfloat16)
    if cuts is None:
        last = [pltpu.make_async_copy(held_a, grads[0], sems_a.at[0])]
    else:
        cut, outs, span, columns = cuts.output(grads, width)
        half = cuts.split.half
        last = piece_copies(
            held_a, outs, sems_a, me_ref, cut.stages, 0, width // (2 * half), half, span, columns
        )
    run_all(last)
    for step in range(max(0, steps - 2), steps):
        wait_all(copies(step))
    wait_all(last)


class Cut:
    def __init__(self, stages, rows, width):
        self.stages, self.rows, self.width = tuple(stages), rows, width
        self.places = 1 << len(stages)

    def shapes(self):
        return [jax.ShapeDtypeStruct((self.places, self.rows, self.width), jnp.bfloat16)] * 2


class FeedSplit:
    def __init__(self, half, half_outer, width, width_inner):
        self.half, self.half_outer, self.width, self.width_inner = half, half_outer, width, width_inner
        self.most = max(16, half_outer // 6 * 5 // 16 * 16)
        self.rest = half_outer - self.most
        self.folded = half + self.rest

    def spots(self):
        return [
            (self.half, self.width, [(2, 0, 0, self.half, 0)]),
            (self.half, self.width_inner, [(0, 0, 0, self.half, 0)]),
            (
                self.half_outer,
                self.width,
                [(1, 0, 0, self.most, 0), (2, self.half, self.most, self.rest, 0)],
            ),
        ]


class FeedCuts:
    def __init__(self, orders, split):
        self.split = split
        rows = (split.half, split.most, split.folded)
        widths = (split.width_inner, split.width, split.width)
        self.cuts = [Cut(*sizes) for sizes in zip(orders, rows, widths)]

    def shapes(self):
        return [shape for cut in self.cuts for shape in cut.shapes()]

    def inner(self, grads, step, chunk):
        split = self.split
        parts = split.width_inner // chunk
        into = pl.multiple_of(step % parts * chunk, 128)
        return [(self.cuts[0], grads[0:2], (0, split.half, 0), [(0, step // parts, into, chunk)])]

    def outer(self, grads, width):
        split = self.split
        columns = [(p * split.width, p, 0, split.width) for p in range(width // split.width)]
        listed = [(self.cuts[1], grads[2:4], (0, split.most, 0), columns)]
        if split.rest:
            listed.append((self.cuts[2], grads[4:6], (split.most, split.rest, split.half), columns))
        return listed

    def output(self, grads, width):
        split = self.split
        columns = [(p * split.width, p, 0, split.width) for p in range(width // split.width)]
        return self.cuts[2], grads[4:6], (0, split.half, 0), columns


ANYWHERE = pl.BlockSpec(memory_space=pl.ANY)
SCALARS = pl.BlockSpec(memory_space=pltpu.SMEM)
HERE = pl.BlockSpec(memory_space=pltpu.VMEM)


def feed(me, lengths, x, att, cotangent, hidden_bias, vectors, source, cuts):
    seqs, slots, width = x.shape
    inner = hidden_bias.shape[1]
    total = seqs * slots
    chunk = min(768, inner)
    low = jnp.bfloat16
    if cuts is None:
        shapes = ((width, width), (width, inner), (inner, width))
        grads = [jax.ShapeDtypeStruct(shape, low) for shape in shapes]
        copies, copies_last = 2, 1
    else:
        grads = cuts.shapes()
        split = cuts.split
        pairs = width // split.width
        copies = 2 * (chunk // split.half_outer) * pairs
        copies += width // split.half
        copies_last = width // split.half * pairs
    return pl.pallas_call(
        functools.partial(feed_kernel, source, cuts, slots),
        in_specs=[SCALARS, SCALARS] + [HERE] * 5 + [ANYWHERE] * len(source.operands),
        out_specs=[HERE] * 5 + [ANYWHERE] * len(grads),
        out_shape=[
            jax.ShapeDtypeStruct((total, width), low),
            jax.ShapeDtypeStruct((total, width), jnp.float32),
            jax.ShapeDtypeStruct((total, width), low),
            jax.ShapeDtypeStruct((1, inner), jnp.float32),
            jax.ShapeDtypeStruct((8, width), jnp.float32),
            *grads,
        ],
        scratch_shapes=[
            pltpu.VMEM((width, inner), low),
            pltpu.VMEM((inner, width), low),
            pltpu.VMEM((width, width), low),
            pltpu.VMEM((total, inner), low),
            pltpu.VMEM((total, inner), low),
            pltpu.VMEM((total, width), jnp.float32),
            pltpu.VMEM((total, width), low),
            pltpu.VMEM((width, total), low),
            pltpu.VMEM((total, width), low),
            pltpu.VMEM((2, width, chunk), low),
            pltpu.VMEM((2, chunk, width), low),
            pltpu.VMEM((width, width), low),
            pltpu.SemaphoreType.DMA((source.pick([0]).count((width, width)),)),
            pltpu.SemaphoreType.DMA((source.pick([1]).count((width, inner)),)),
            pltpu.SemaphoreType.DMA((source.pick([2]).count((inner, width)),)),
            pltpu.SemaphoreType.DMA((2, copies)),
            pltpu.SemaphoreType.DMA((copies_last,)),
        ],
        compiler_params=pltpu.CompilerParams(vmem_limit_bytes=FEED_BYTES),
        cost_estimate=estimate(60),
        name="feed",
    )(
        lengths, me, x.reshape(total, width), att.reshape(total, width),
        cotangent.reshape(total, width), hidden_bias, vectors, *source.operands,
    )


def backward_kernel(
    seq, head_size, lengths, do_ref, q_ref, k_ref, v_ref, att_ref, lse_ref, *rest
):
    dq_ref, dk_ref, dv_ref, qt, kt, at_t, do_t, dq_t = rest
    length = lengths[seq]
    width = q_ref.shape[1]
    scale = head_size**-0.5
    at_t[...] = att_ref[...].T
    do_t[...] = do_ref[...].T
    qt[...] = q_ref[...].T
    kt[...] = k_ref[...].T

    def one_pair(p, carry):
        base = pl.multiple_of(p * 2 * head_size, 2 * head_size)
        here = pl.ds(base, 2 * head_size)
        key_pair, value_pair = k_ref[:, here], v_ref[:, here]
        query_pair, up_pair = q_ref[:, here], do_ref[:, here]
        grad_keys = grad_values = None
        for head in range(2):
            at = pl.multiple_of(base + head * head_size, head_size)
            mine = pl.ds(at, head_size)
            logs = [-part for part in three_parts(lse_ref[p, head : head + 1, :])]
            keys = head_keys(key_pair, head, length, True)
            soft = jnp.exp(dot(keys, with_rows(qt[mine, :], head, [1.0] + logs)))
            up = do_t[mine, :]
            delta = jnp.sum(
                up.astype(jnp.float32) * at_t[mine, :].astype(jnp.float32), axis=0, keepdims=True
            )
            deltas = [-part for part in three_parts(delta)]
            grad_soft = dot(head_values(value_pair, head), with_rows(up, head, deltas))
            scores = (soft * grad_soft).astype(jnp.bfloat16)
            from_values = dot(soft.astype(jnp.bfloat16), only_head(up_pair, head))
            from_keys = dot(scores, only_head(query_pair, head))
            grad_values = from_values if head == 0 else grad_values + from_values
            grad_keys = from_keys if head == 0 else grad_keys + from_keys
            dq_t[mine, :] = (dot(kt[mine, :], scores) * scale).astype(jnp.bfloat16)
        dk_ref[:, here] = grad_keys.astype(jnp.bfloat16)
        dv_ref[:, here] = grad_values.astype(jnp.bfloat16)
        return carry

    lax.fori_loop(0, width // (2 * head_size), one_pair, 0)
    dq_ref[...] = dq_t[...].T


def attend_backward(seq, part, parts, do, q, k, v, att, lse, lengths, before):
    seqs, slots, width = q.shape
    count = width // parts
    pairs = HEADS // 2 // parts
    rows = pl.BlockSpec((None, slots, count), lambda i, *_: (seq, 0, part))
    low = jax.ShapeDtypeStruct(q.shape, jnp.bfloat16)
    inputs = (lengths, do, q, k, v, att, lse)
    kernel = functools.partial(backward_kernel, seq, width // HEADS)
    return pl.pallas_call(
        functools.partial(skip_refs, kernel, len(inputs), len(before)),
        grid_spec=pltpu.PrefetchScalarGridSpec(
            num_scalar_prefetch=1,
            grid=(1,),
            in_specs=[rows] * 5
            + [pl.BlockSpec((None, pairs, 2, slots), lambda i, *_: (seq, part, 0, 0))]
            + [ANYWHERE] * len(before),
            out_specs=[rows] * 3,
            scratch_shapes=[pltpu.VMEM((count, slots), jnp.bfloat16)] * 5,
        ),
        out_shape=[low, low, low],
        input_output_aliases={len(inputs) + i: i for i in range(len(before))},
        compiler_params=pltpu.CompilerParams(vmem_limit_bytes=VMEM_BYTES),
        cost_estimate=estimate(14 // parts),
        name="attend_backward",
    )(*inputs, *before)


def pack_gradients(sums_feed, sums_in, hsum, small, columns):
    parts, _, lanes = small.shape
    lanes = min(128, lanes)
    width, share = sums_feed.shape[1], hsum.shape[1] // parts
    rows = share // columns

    def chosen(count, start):
        row = lax.broadcasted_iota(jnp.int32, (count, lanes), 0)
        column = lax.broadcasted_iota(jnp.int32, (count, lanes), 1)
        return ((row - start == column) & (column < columns)).astype(jnp.float32).astype(jnp.bfloat16)

    small[...] = jnp.zeros_like(small)
    listed = (
        [*sums_in, sums_feed[5:6], sums_feed[2:3]]
        + [jnp.zeros((rows, width), jnp.float32)]
        + [sums_feed[3:4], sums_feed[0:1], sums_feed[4:5], sums_feed[1:2]]
    )
    pad = SMALL_ROWS - 8 - rows
    lined = jnp.concatenate(listed + [jnp.zeros((pad, width), jnp.float32)], axis=0)
    lined = lined.astype(jnp.bfloat16)
    hidden = [hsum[:, dp * share : (dp + 1) * share] for dp in range(parts)]
    hidden = jnp.concatenate(hidden, axis=0).astype(jnp.bfloat16)
    spread = [dot(hidden, chosen(share, k * columns)) for k in range(rows)]
    for dp in range(parts):
        here = dot(lined, chosen(width, dp * columns))
        own = [spread[k][dp : dp + 1] for k in range(rows)]
        here = jnp.concatenate([here[:4]] + own + [here[4 + rows :]], axis=0)
        small[dp, :, 0:lanes] = here.astype(jnp.bfloat16)


def project_grads_kernel(
    cuts, columns, me_ref, x_ref, dq_ref, dk_ref, dv_ref, sums_feed, hsum, *rest
):
    xt, held, small, sems = rest[-4:]
    outs = rest[:-4]
    xt[...] = x_ref[...].T
    started = []
    for which, ref in enumerate((dq_ref, dk_ref, dv_ref)):
        held[which] = dot(xt[...], ref[...]).astype(jnp.bfloat16)
        if cuts is None:
            outs[which][...] = held[which]
            continue
        width, half, third = held.shape[2], (cuts[0].rows + cuts[1].rows - SMALL_ROWS) // 3, 0
        third = cuts[0].rows - SMALL_ROWS - half
        spans = [(0, 0, half, 0)], [(1, 0, half, 0)], [(0, 0, third, half), (1, third, half - third, half)]
        used = 0
        for i, offset, count, at in spans[which]:
            if count == 0:
                continue
            cut = cuts[i]
            ends = [(p * cut.width, p, 0, cut.width) for p in range(width // cut.width)]
            made = piece_copies(
                held.at[which], outs[2 * i : 2 * i + 2],
                sems.at[which, pl.ds(used, width // half * len(ends))],
                me_ref, cut.stages, 0, width // (2 * half), half, (offset, count, at), ends,
            )
            used += len(made)
            started += run_all(made)
    if cuts is not None:
        sums_in = [
            jnp.sum(ref[...].astype(jnp.float32), axis=0, keepdims=True) for ref in (dq_ref, dv_ref)
        ]
        pack_gradients(sums_feed[...], sums_in, hsum[...], small, columns)
        started += run_all(
            small_copies(
                small, outs[:2], sems.at[3], me_ref, cuts[0].stages, cuts[0].rows - SMALL_ROWS, small.shape[0],
                held.shape[2] // cuts[0].width,
            )
        )
    wait_all(started)


def project_grads(me, x, dq, dk, dv, sums, cuts, dp_size, columns):
    total, width = x.shape
    grad = jax.ShapeDtypeStruct((width, width), jnp.bfloat16)
    direct = cuts is not None
    copies = 4 * dp_size * (width // cuts[0].width) if direct else 1
    piece = cuts[0].width if direct else 128
    return pl.pallas_call(
        functools.partial(project_grads_kernel, cuts, columns),
        in_specs=[SCALARS] + [HERE] * 6,
        out_specs=[ANYWHERE] * 4 if direct else [HERE] * 3,
        out_shape=[shape for cut in cuts for shape in cut.shapes()] if direct else [grad] * 3,
        scratch_shapes=[
            pltpu.VMEM((width, total), jnp.bfloat16),
            pltpu.VMEM((3, width, width), jnp.bfloat16),
            pltpu.VMEM((dp_size if direct else 1, SMALL_ROWS, piece), jnp.bfloat16),
            pltpu.SemaphoreType.DMA((4, copies)),
        ],
        compiler_params=pltpu.CompilerParams(vmem_limit_bytes=VMEM_BYTES),
        cost_estimate=estimate(8),
        name="project_grads",
    )(me, x, dq, dk, dv, *sums)


def input_grad_kernel(source, me_ref, gf_ref, dq_ref, dk_ref, dv_ref, *refs):
    inputs, (out_ref, weights, sems) = refs[:-3], refs[-3:]
    started = [
        run_all(source.copies(i, inputs, weights.at[i], sems.at[i], me_ref)) for i in range(3)
    ]
    grad = gf_ref[...]
    for i, ref in enumerate((dq_ref, dk_ref, dv_ref)):
        wait_all(started[i])
        grad = grad + dot_last(ref[...], weights[i])
    out_ref[...] = grad.astype(jnp.bfloat16)


def input_grads(me, gf, dq, dk, dv, source):
    total, width = dq.shape
    return pl.pallas_call(
        functools.partial(input_grad_kernel, source),
        in_specs=[SCALARS] + [HERE] * 4 + [ANYWHERE] * len(source.operands),
        out_specs=HERE,
        out_shape=jax.ShapeDtypeStruct((total, width), jnp.bfloat16),
        scratch_shapes=[
            pltpu.VMEM((3, width, width), jnp.bfloat16),
            pltpu.SemaphoreType.DMA((3, source.count((width, width)))),
        ],
        compiler_params=pltpu.CompilerParams(vmem_limit_bytes=VMEM_BYTES),
        cost_estimate=estimate(8),
        name="input_grads",
    )(me, gf, dq, dk, dv, *source.operands)


def after(values, *others):
    return lax.optimization_barrier((values, others))[0]


def meet(values, parts):
    values, arriving = lax.optimization_barrier((values, [part.arriving for part in parts]))
    for part, value in zip(parts, arriving):
        part.arriving = value
    return values


class Attention:
    def __init__(self, me, inputs, lengths, source, given, columns, hidden_count):
        self.me, self.inputs, self.lengths, self.source = me, inputs, lengths, source
        self.given, self.sizes = given, (columns, hidden_count)
        self.state, self.back = (), ()

    def forward(self, seq):
        *state, self.vectors, self.hidden_bias = attend_forward(
            seq, self.me, self.inputs, self.lengths, self.source, self.given, *self.sizes, self.state
        )
        self.state = tuple(state)

    def backward(self, seq, part, parts, do):
        self.back = tuple(
            attend_backward(seq, part, parts, do, *self.state, self.lengths, self.back)
        )


def layer_step(inputs, lengths, upstream, gather, scatter):
    shape = inputs.shape
    flat = (shape[0] * shape[1], shape[2])
    seqs = shape[0]
    source, given = gather.first()
    bias, hidden = gather.shards[6:8]
    me = gather.me
    columns = bias.shape[1]
    attention = Attention(
        me, inputs, lengths, source, given, columns, hidden.shape[0] * scatter.dp_size
    )
    for seq in range(seqs):
        attention.inputs = gather.before(seq, attention.inputs)
        attention.forward(seq)
        attention.state = gather.after(seq, attention.state)
    outputs, gf, do, hidden_sum, sums_feed, *grads = feed(
        me, lengths, inputs, attention.state[3], upstream, attention.hidden_bias,
        attention.vectors, gather.second(), scatter.feed_cuts,
    )
    parts = 2
    scatter.feed(grads)
    for at in range(seqs * parts):
        attention.backward(at // parts, at % parts, parts, do.reshape(shape))
        attention.back = scatter.step(at, attention.back)
    dq, dk, dv = (grad.reshape(flat) for grad in attention.back)
    sums = (sums_feed, hidden_sum)
    scatter.ends = (dq, dv)
    results = project_grads(
        me, inputs.reshape(flat), dq, dk, dv, sums, scatter.first_cuts, scatter.dp_size, columns
    )
    gf = scatter.last(results, sums, gf)
    input_grad = input_grads(me, gf, dq, dk, dv, source)
    input_grad, totals = scatter.totals(input_grad)
    return outputs.reshape(shape), input_grad.reshape(shape), totals


def split_up(value, dim, size):
    before, after = (value.shape[:dim], value.shape[dim + 1 :])
    return jnp.moveaxis(value.reshape(*before, size, -1, *after), dim, 0)


def sum_at_owner(value, axis, dim):
    size = lax.axis_size(axis)
    parts = lax.all_to_all(split_up(value, dim, size), axis, 0, 0, tiled=True)
    return jnp.sum(parts.astype(jnp.float32), axis=0)


def side_by_side(arrays, axis, dim, along):
    ends, at = ([], 0)
    for a in arrays[:-1]:
        at += a.shape[along]
        ends.append(at)
    both = jnp.concatenate(arrays, axis=along)
    return tuple(jnp.split(sum_at_owner(both, axis, dim), ends, axis=along))


def gather_forward(shards):
    (
        query_part,
        key_part,
        value_part,
        output_part,
        inner_part,
        outer_part,
        bias_part,
        hidden_part,
        gain_part,
        shift_part,
    ) = shards
    column_full = (
        lax.all_gather(query_part, "fsdp", axis=1, tiled=True),
        lax.all_gather(key_part, "fsdp", axis=1, tiled=True),
        lax.all_gather(value_part, "fsdp", axis=1, tiled=True),
        lax.all_gather(output_part, "fsdp", axis=1, tiled=True),
        lax.all_gather(inner_part, "fsdp", axis=1, tiled=True),
        lax.all_gather(outer_part, "fsdp", axis=1, tiled=True),
    )
    return (
        lax.all_gather(column_full[0], "dp", axis=0, tiled=True),
        lax.all_gather(column_full[1], "dp", axis=0, tiled=True),
        lax.all_gather(column_full[2], "dp", axis=0, tiled=True),
        lax.all_gather(column_full[3], "dp", axis=0, tiled=True),
        lax.all_gather(column_full[4], "dp", axis=0, tiled=True),
        lax.all_gather(column_full[5], "dp", axis=0, tiled=True),
        lax.all_gather(bias_part, "dp", axis=1, tiled=True),
        lax.all_gather(hidden_part, "dp", axis=0, tiled=True),
        lax.all_gather(gain_part, "dp", axis=1, tiled=True),
        lax.all_gather(shift_part, "dp", axis=1, tiled=True),
    )


def reduce_grads(grads):
    (
        query_grad,
        key_grad,
        value_grad,
        output_grad,
        inner_grad,
        outer_grad,
        bias_grad,
        hidden_grad,
        gain_grad,
        shift_grad,
    ) = grads
    bias_grad, hidden_grad, gain_grad, shift_grad = (
        lax.psum(bias_grad.astype(jnp.bfloat16), "fsdp").astype(jnp.float32),
        lax.psum(hidden_grad.astype(jnp.bfloat16), "fsdp").astype(jnp.float32),
        lax.psum(gain_grad.astype(jnp.bfloat16), "fsdp").astype(jnp.float32),
        lax.psum(shift_grad.astype(jnp.bfloat16), "fsdp").astype(jnp.float32),
    )
    narrow = (
        lax.psum_scatter(
            query_grad.astype(jnp.bfloat16), "fsdp", scatter_dimension=1, tiled=True
        ).astype(jnp.float32),
        lax.psum_scatter(
            key_grad.astype(jnp.bfloat16), "fsdp", scatter_dimension=1, tiled=True
        ).astype(jnp.float32),
        lax.psum_scatter(
            value_grad.astype(jnp.bfloat16), "fsdp", scatter_dimension=1, tiled=True
        ).astype(jnp.float32),
        lax.psum_scatter(
            output_grad.astype(jnp.bfloat16), "fsdp", scatter_dimension=1, tiled=True
        ).astype(jnp.float32),
        lax.psum_scatter(
            inner_grad.astype(jnp.bfloat16), "fsdp", scatter_dimension=1, tiled=True
        ).astype(jnp.float32),
        lax.psum_scatter(
            outer_grad.astype(jnp.bfloat16), "fsdp", scatter_dimension=1, tiled=True
        ).astype(jnp.float32),
    )
    return (
        *side_by_side(
            (
                narrow[0].astype(jnp.bfloat16),
                narrow[1].astype(jnp.bfloat16),
                narrow[2].astype(jnp.bfloat16),
                narrow[3].astype(jnp.bfloat16),
                narrow[4].astype(jnp.bfloat16),
            ),
            "dp",
            0,
            1,
        ),
        sum_at_owner(narrow[5].astype(jnp.bfloat16), "dp", 0),
        sum_at_owner(bias_grad.astype(jnp.bfloat16), "dp", 1),
        sum_at_owner(hidden_grad.astype(jnp.bfloat16), "dp", 0),
        *side_by_side(
            (gain_grad.astype(jnp.bfloat16), shift_grad.astype(jnp.bfloat16)), "dp", 1, 0
        ),
    )


def pack_small(bias, hidden, gains, shifts, width):
    columns = bias.shape[-1]
    rows = jnp.concatenate([bias, hidden.reshape(-1, columns), gains, shifts], axis=0)
    return jnp.pad(rows, ((0, SMALL_ROWS - rows.shape[0]), (0, width - columns)))


class Gather:
    def __init__(self, mesh, shards, me):
        self.mesh, self.shards, self.me = mesh, shards, me
        self.orders = stage_orders(mesh)

    def prepare(self):
        query, key, value, output, inner, outer, bias, hidden, gains, shifts = self.shards
        half, half_outer = query.shape[0] // 2, outer.shape[0] // 2
        small = pack_small(bias, hidden, gains, shifts, 2 * query.shape[1])

        def both(*arrays):
            halves = [array[: array.shape[0] // 2] for array in arrays]
            halves += [array[array.shape[0] // 2 :] for array in arrays]
            return jnp.concatenate(halves, axis=0)

        one, rest, inner = pair_up((both(query, key, value), both(output, outer), inner))
        third = third_of(half)
        self.one = [one[:half], one[2 * half : 2 * half + third], small]
        self.cut_at = sum(part.shape[0] for part in self.one)
        self.one += [one[half : 2 * half], one[2 * half + third :]]
        self.one = [jnp.concatenate(self.one, axis=0)[None]]
        split = self.split = FeedSplit(half, half_outer, 2 * query.shape[1], inner.shape[1])
        self.two = [
            inner[None],
            rest[half : half + split.most][None],
            jnp.concatenate([rest[:half], rest[half + split.most :]], axis=0)[None],
        ]

    def send(self, parts, stage):
        return [swap(part, *self.orders[i][stage]) for i, part in enumerate(parts)]

    def join(self, parts, received):
        return [jnp.concatenate(pair, axis=0) for pair in zip(parts, received)]

    def first(self):
        self.prepare()
        count, far = len(self.orders[0]), far_stages(self.mesh)
        self.stage = 0
        for stage in range(far):
            self.one = self.join(self.one, self.send(self.one, stage))
        joined = self.one[0]
        self.one = [joined[:, : self.cut_at], joined[:, self.cut_at :]]
        for stage in range(far, count):
            arriving = self.send(self.one, stage)
            self.two = after(self.two, self.one)
            ahead = self.send(self.two, self.stage)
            self.stage += 1
            self.one = self.join(self.one, arriving)
            self.two = self.join(self.two, after(ahead, self.one))
        self.two = after(self.two, self.one)
        others = [swap(part, "fsdp", 0) for part in self.one]
        half, width = self.shards[0].shape[0] // 2, self.one[0].shape[2]
        third = third_of(half)
        thirds = [(0, half, 0, third, 0), (1, half, third, half - third, 0)]
        spots = [(half, width, [(0, 0, 0, half, 0)]), (half, width, [(1, 0, 0, half, 0)]), (half, width, thirds)]
        operands = [array for pair in zip(self.one, others) for array in pair]
        return Source(operands, self.orders, spots, self.mesh.shape["dp"], half + third), ()

    def before(self, seq, inputs):
        if self.stage == len(self.orders[0]):
            return inputs
        self.arriving = self.send(self.two, self.stage)
        self.stage += 1
        return after(inputs, self.two)

    def after(self, seq, state):
        if self.arriving is None:
            return state
        arriving = after(self.arriving, state)
        self.two, self.arriving = self.join(self.two, arriving), None
        return state

    def second(self):
        while self.stage < len(self.orders[0]):
            self.two = self.join(self.two, self.send(self.two, self.stage))
            self.stage += 1
        others = [swap(part, "fsdp", 0) for part in self.two]
        operands = [array for pair in zip(self.two, others) for array in pair]
        return Source(operands, self.orders, self.split.spots(), self.mesh.shape["dp"])


class Part:
    def __init__(self, keep, send, stages):
        self.keep, self.stages = keep, list(stages)
        self.arriving = swap(send, "fsdp", 0)

    def step(self):
        axis, bit = self.stages.pop()
        half = self.keep.shape[0] // 2
        send = total_of(self.keep[half:], self.arriving[half:], jnp.bfloat16)
        arriving = swap(send, axis, bit)
        self.keep = total_of(self.keep[:half], self.arriving[:half], jnp.bfloat16)
        self.arriving = arriving
        return send

    def join(self, other):
        both = Part.__new__(Part)
        both.keep = jnp.concatenate([self.keep, other.keep], axis=1)
        both.arriving = jnp.concatenate([self.arriving, other.arriving], axis=1)
        both.stages = list(self.stages)
        return both

    def finish(self):
        while self.stages:
            self.step()
        return total_of(self.keep, self.arriving, jnp.float32)[0]


class Scatter:
    def __init__(self, mesh, shards, me):
        self.shards = shards
        self.orders = stage_orders(mesh)
        width, width_inner = 2 * shards[0].shape[1], 2 * shards[4].shape[1]
        half, half_outer = shards[0].shape[0] // 2, shards[5].shape[0] // 2
        self.dp_size = mesh.shape["dp"]
        self.split = FeedSplit(half, half_outer, width, width_inner)
        self.feed_cuts = FeedCuts(self.orders, self.split)
        self.third = third_of(half)
        self.far = far_stages(mesh)
        rows = (half + self.third + SMALL_ROWS, 2 * half - self.third)
        self.first_cuts = [Cut(order, r, width) for order, r in zip(self.orders, rows)]

    def feed(self, grads):
        self.behind = [
            Part(*grads[2 * i : 2 * i + 2], cut.stages) for i, cut in enumerate(self.feed_cuts.cuts)
        ]

    def step(self, at, state):
        parts = {0: self.behind, 2: self.behind[2:], 3: self.behind[:2]}.get(at, [])
        if not parts:
            return state
        state = meet(state, parts)
        return after(state, [part.step() for part in parts])

    def last(self, results, sums, passing):
        results = meet(results, self.behind)
        self.front = [
            Part(*results[2 * i : 2 * i + 2], cut.stages) for i, cut in enumerate(self.first_cuts)
        ]
        sent = [part.step() for part in self.behind]
        meet((), self.front)
        sent += [part.step() for part in self.front]
        return after(passing, sent)

    def totals(self, passing):
        half, half_outer = self.shards[0].shape[0] // 2, self.shards[5].shape[0] // 2
        columns = self.shards[6].shape[1]
        parts, front = self.front + self.behind, self.front
        passing = meet(passing, parts)
        while len(front[0].stages) > self.far:
            for part in parts:
                if part.stages:
                    part.step()
            meet((), front)
        joint = front[0].join(front[1])
        cut_at = front[0].keep.shape[1]
        if joint.stages:
            joint.step()
        inner, outer, rest = [part.finish() for part in self.behind]
        split = self.split
        outer = jnp.concatenate([outer, rest[half : split.folded]], axis=0)
        settled = settle(jnp.concatenate([rest[:half], outer]), (half, half_outer)) + settle(inner, (half,))
        output, outer, inner = meet(settled, [joint])
        total = joint.finish()
        one, two, third = total[:cut_at], total[cut_at:], self.third
        thirds = [one[half : half + third], two[half:]]
        query, key, value = settle(jnp.concatenate([one[:half], two[:half], *thirds]), (half,) * 3)
        rows = one[half + third :, :columns]
        split = 4 + self.shards[7].shape[0] // columns
        return passing, (
            query, key, value, output, inner, outer,
            rows[:4], rows[4:split].reshape(-1), rows[split : split + 2], rows[split + 2 : split + 4],
        )


class PlainGather:
    def __init__(self, mesh, shards, me):
        self.shards, self.me = shards, me

    def first(self):
        arrays = gather_forward(self.shards)
        self.rest = arrays[3:6]
        bias, hidden, gains, shifts = arrays[6:]
        vectors = jnp.concatenate([bias, gains, shifts], axis=0).astype(jnp.float32)
        return Source(arrays[:3]), (vectors, hidden.astype(jnp.float32)[None])

    def before(self, seq, inputs):
        return inputs

    def after(self, seq, state):
        return state

    def second(self):
        return Source(self.rest)


class PlainScatter:
    def __init__(self, mesh, shards, me):
        self.feed_cuts = self.first_cuts = None
        self.dp_size = mesh.shape["dp"]

    def feed(self, grads):
        self.grads = grads

    def step(self, at, state):
        return state

    def last(self, results, sums, passing):
        (feed, hidden), (dq, dv) = sums, self.ends
        ends = [jnp.sum(d.astype(jnp.float32), axis=0, keepdims=True) for d in (dq, dv)]
        bias = jnp.concatenate([*ends, feed[5:6], feed[2:3]], axis=0)
        gains = jnp.concatenate([feed[3:4], feed[:1]], axis=0)
        shifts = jnp.concatenate([feed[4:5], feed[1:2]], axis=0)
        self.grads = (*results, *self.grads, bias, hidden[0], gains, shifts)
        return passing

    def totals(self, passing):
        return passing, reduce_grads(self.grads)


def on_device(
    mesh,
    tokens,
    lengths,
    cotangent,
    *shards,
):
    me = jnp.stack([lax.axis_index("dp"), lax.axis_index("fsdp")]).astype(jnp.int32)
    rows = (shards[0].shape[0], shards[5].shape[0])
    direct = fits(mesh, rows, shards[0].shape[1], shards[7].shape[0])
    gather = (Gather if direct else PlainGather)(mesh, shards, me)
    scatter = (Scatter if direct else PlainScatter)(mesh, shards, me)
    shape = (-1, *tokens.shape[2:])
    outputs, grad_inputs, totals = layer_step(
        tokens.reshape(shape), lengths.reshape(-1), cotangent.reshape(shape), gather, scatter
    )
    return (outputs.reshape(tokens.shape), grad_inputs.reshape(tokens.shape), *totals)


def solution(mesh):
    placed = (
        P(None, ("dp", "fsdp"), None, None),
        P(None, ("dp", "fsdp")),
        P(None, ("dp", "fsdp"), None, None),
        P("dp", "fsdp"),
        P("dp", "fsdp"),
        P("dp", "fsdp"),
        P("dp", "fsdp"),
        P("dp", "fsdp"),
        P("dp", "fsdp"),
        P(None, "dp"),
        P("dp"),
        P(None, "dp"),
        P(None, "dp"),
    )
    return jax.shard_map(
        functools.partial(on_device, mesh),
        mesh=mesh,
        in_specs=placed,
        out_specs=(
            P(None, ("dp", "fsdp"), None, None),
            P(None, ("dp", "fsdp"), None, None),
            P("dp", "fsdp"),
            P("dp", "fsdp"),
            P("dp", "fsdp"),
            P("dp", "fsdp"),
            P("dp", "fsdp"),
            P("dp", "fsdp"),
            P(None, "dp"),
            P("dp"),
            P(None, "dp"),
            P(None, "dp"),
        ),
        check_vma=False,
    )
```

```python
import functools
import jax
import jax.numpy as jnp
from jax import lax
from jax.experimental import pallas as pl
from jax.experimental.pallas import tpu as pltpu
from jax.sharding import PartitionSpec as P

HEADS = 12


EPSILON = 1e-12
MASKED = -1000000000.0
SMALL_ROWS = 16


def swap(value, axis, bit):
    size = lax.axis_size(axis)
    return lax.ppermute(value, axis, [(i, i ^ (1 << bit)) for i in range(size)])


def stage_orders(mesh):
    dp_bits = mesh.shape["dp"].bit_length() - 1
    fsdp_bits = mesh.shape["fsdp"].bit_length() - 1
    far = [("dp", b) for b in range(dp_bits - 1, 0, -1)]
    across = [("fsdp", b) for b in range(fsdp_bits - 1, 0, -1)]
    near = [("dp", 0)]
    return (far + across + near, far + near + across, across + near + far)


def far_stages(mesh):
    return mesh.shape["dp"].bit_length() - 2


def third_of(half):
    return half // 3 // 16 * 16


def fits(mesh, rows, width, hidden):
    sizes = (mesh.shape["dp"], mesh.shape["fsdp"])
    powers = all(s >= 2 and s & (s - 1) == 0 for s in sizes)
    return powers and all(r % 32 == 0 for r in rows) and width % 64 == 0 and hidden % 128 == 0 and 96 <= rows[0] <= 128


def place_of(stages, dp, fsdp, me_ref):
    index = {"dp": dp ^ me_ref[0], "fsdp": fsdp ^ me_ref[1]}
    place = 0
    for s, (axis, bit) in enumerate(stages):
        place = place + (((index[axis] >> bit) & 1) << s)
    return place


def piece_copies(source, outs, sems, me_ref, stages, first_dp, count_dp, half, span, columns):
    copies = []
    offset, rows, at = span
    for i in range(count_dp):
        dp = first_dp + i
        for flip in range(2):
            fsdp = (me_ref[1] & 1) ^ flip
            row = pl.multiple_of((2 * i + fsdp) * half + offset, 16)
            for start, pair, into, count in columns:
                place = place_of(stages, dp, 2 * pair + fsdp, me_ref)
                copies.append(
                    pltpu.make_async_copy(
                        source.at[pl.ds(row, rows), pl.ds(start, count)],
                        outs[flip].at[place, pl.ds(at, rows), pl.ds(into, count)],
                        sems.at[len(copies)],
                    )
                )
    return copies


class Source:
    def __init__(self, operands, stages=(), spots=(), dp_size=0, small_at=None):
        self.operands, self.stages, self.spots = tuple(operands), stages, spots
        self.dp_size, self.small_at = dp_size, small_at

    def count(self, shape):
        if not self.spots:
            return 1
        return 2 * self.dp_size * max(shape[1] // width * len(spans) for _, width, spans in self.spots)

    def copies(self, which, refs, target, sems, me_ref):
        if not self.spots:
            return [pltpu.make_async_copy(refs[which], target, sems.at[0])]
        half, width, spans = self.spots[which]
        copies = []
        for part, at, offset, rows, column in spans:
            count = self.operands[2 * part].shape[2]
            for dp in range(self.dp_size):
                for flip in range(2):
                    fsdp = (me_ref[1] & 1) ^ flip
                    row = pl.multiple_of((2 * dp + fsdp) * half + offset, 16)
                    for pair in range(target.shape[1] // width):
                        place = place_of(self.stages[part], dp, 2 * pair + fsdp, me_ref)
                        copies.append(
                            pltpu.make_async_copy(
                                refs[2 * part + flip].at[place, pl.ds(at, rows), :],
                                target.at[pl.ds(row, rows), pl.ds(pair * width + column, count)],
                                sems.at[len(copies)],
                            )
                        )
        return copies

    def small_copies(self, refs, target, sems, me_ref):
        copies = []
        for dp in range(self.dp_size):
            place = place_of(self.stages[0], dp, me_ref[1], me_ref)
            source = refs[0].at[place, pl.ds(self.small_at, SMALL_ROWS), :]
            copies.append(pltpu.make_async_copy(source, target.at[dp], sems.at[dp]))
        return copies

    def pick(self, which):
        if not self.spots:
            return Source([self.operands[i] for i in which])
        return Source(self.operands, self.stages, [self.spots[i] for i in which], self.dp_size)


def lay_vectors(small, columns, hidden_count, vec_ref, hb_ref):
    lanes = min(128, small.shape[2])
    width = vec_ref.shape[1]
    parts = small.shape[0]

    def chosen(to, start):
        row = lax.broadcasted_iota(jnp.int32, (lanes, to), 0)
        column = lax.broadcasted_iota(jnp.int32, (lanes, to), 1)
        return ((column - start == row) & (row < columns)).astype(jnp.float32).astype(jnp.bfloat16)

    total = jnp.zeros((SMALL_ROWS, width), jnp.float32)
    for dp in range(parts):
        total = total + dot(small[dp, :, :lanes], chosen(width, dp * columns))
    share = hidden_count // parts
    rows = share // columns
    vec_ref[0:4, :] = total[0:4]
    vec_ref[4:8, :] = total[4 + rows : 8 + rows]
    flat = small[:, :, :lanes].reshape(parts * SMALL_ROWS, lanes)
    spread = [dot(flat, chosen(share, k * columns)) for k in range(rows)]
    for dp in range(parts):
        at = dp * SMALL_ROWS + 4
        hb_ref[:, dp * share : (dp + 1) * share] = sum(
            spread[k][at + k : at + k + 1] for k in range(rows)
        )


def small_copies(source, outs, sems, me_ref, stages, at, dp_size, pairs):
    copies = []
    for dp in range(dp_size):
        for flip in range(2):
            fsdp = (me_ref[1] & 1) ^ flip
            for pair in range(pairs):
                place = place_of(stages, dp, 2 * pair + fsdp, me_ref)
                copies.append(
                    pltpu.make_async_copy(
                        source.at[dp],
                        outs[flip].at[place, pl.ds(at, SMALL_ROWS), :],
                        sems.at[len(copies)],
                    )
                )
    return copies


def run_all(copies):
    for copy in copies:
        copy.start()
    return copies


def wait_all(copies):
    for copy in copies:
        copy.wait()


def total_of(left, right, kind):
    return (left.astype(jnp.float32) + right.astype(jnp.float32)).astype(kind)


def settle(total, rows):
    width = total.shape[-1] // 2
    count = sum(rows)
    second = lax.axis_index("fsdp") & 1
    own = jnp.where(second == 0, total[:count, :width], total[:count, width:])
    away = jnp.where(second == 0, total[:count, width:], total[:count, :width])
    came = swap(away.astype(jnp.bfloat16), "fsdp", 0).astype(jnp.float32)
    first, last = jnp.where(second == 0, own, came), jnp.where(second == 0, came, own)
    outs, at = [], 0
    for half in rows:
        outs.append(jnp.concatenate([first[at : at + half], last[at : at + half]], axis=0))
        at += half
    return outs


def pair_up(shards):
    second = lax.axis_index("fsdp") & 1
    outs = []
    for shard in shards:
        half = shard.shape[0] // 2
        mine = jnp.where(second == 0, shard[:half], shard[half:])
        away = jnp.where(second == 0, shard[half:], shard[:half])
        came = swap(away, "fsdp", 0)
        outs.append(
            jnp.where(
                second == 0,
                jnp.concatenate([mine, came], axis=1),
                jnp.concatenate([came, mine], axis=1),
            )
        )
    return outs


VMEM_BYTES = 56 << 20
FEED_BYTES = 60 << 20


def estimate(micros):
    return pl.CostEstimate(flops=micros * 1000000000, bytes_accessed=micros * 1000000, transcendentals=0)


def dot(left, right):
    return jnp.dot(left, right, preferred_element_type=jnp.float32)


def dot_last(left, right):
    return lax.dot_general(
        left, right, (((1,), (1,)), ((), ())), preferred_element_type=jnp.float32
    )


def dot_first(left, right):
    return lax.dot_general(
        left, right, (((0,), (0,)), ((), ())), preferred_element_type=jnp.float32
    )


def normalize(values):
    centered = values - jnp.mean(values, axis=-1, keepdims=True)
    variance = jnp.mean(centered * centered, axis=-1, keepdims=True)
    factor = lax.rsqrt(variance + EPSILON)
    return (centered * factor, factor)


def norm_back(upward, normed, factor):
    return factor * (
        upward
        - jnp.mean(upward, axis=-1, keepdims=True)
        - normed * jnp.mean(upward * normed, axis=-1, keepdims=True)
    )


def gelu_pair(v):
    size = jnp.abs(v) * 0.7071067811865476
    t = 1.0 / (1.0 + 0.3275911 * size)
    bell = jnp.exp(-size * size)
    poly = t * (
        0.254829592
        + t * (-0.284496736 + t * (1.421413741 + t * (-1.453152027 + t * 1.061405429)))
    )
    tail = 0.5 * poly * bell
    cdf = jnp.where(v >= 0.0, 1.0 - tail, tail)
    return v * cdf, cdf + v * bell * 0.3989422804014327


def three_parts(value):
    high = value.astype(jnp.bfloat16).astype(jnp.float32)
    rest = value - high
    middle = rest.astype(jnp.bfloat16).astype(jnp.float32)
    return high, middle, rest - middle


def head_keys(pair, head, length, with_stats):
    rows, lanes = pair.shape
    lane = lax.broadcasted_iota(jnp.int32, (rows, lanes), 1)
    row = lax.broadcasted_iota(jnp.int32, (rows, lanes), 0)
    start = lanes // 2 if head == 0 else 0
    own = lane < lanes // 2 if head == 0 else lane >= lanes // 2
    hidden = jnp.where((lane == start) & (row >= length), MASKED, 0.0)
    if with_stats:
        hidden = jnp.where((lane > start) & (lane < start + 4), 1.0, hidden)
    return jnp.where(own, pair.astype(jnp.float32), hidden).astype(jnp.bfloat16)


def head_values(pair, head):
    rows, lanes = pair.shape
    lane = lax.broadcasted_iota(jnp.int32, (rows, lanes), 1)
    start = lanes // 2 if head == 0 else 0
    own = lane < lanes // 2 if head == 0 else lane >= lanes // 2
    ones = jnp.where((lane >= start) & (lane < start + 3), 1.0, 0.0)
    return jnp.where(own, pair.astype(jnp.float32), ones).astype(jnp.bfloat16)


def only_head(pair, head):
    lane = lax.broadcasted_iota(jnp.int32, pair.shape, 1)
    own = lane < pair.shape[1] // 2 if head == 0 else lane >= pair.shape[1] // 2
    return jnp.where(own, pair.astype(jnp.float32), 0.0).astype(jnp.bfloat16)


def with_rows(part, head, rows):
    count, width = part.shape
    row = lax.broadcasted_iota(jnp.int32, (count, width), 0)
    extra = jnp.zeros((count, width), jnp.float32)
    for i, value in enumerate(rows):
        extra = jnp.where(row == i, value, extra)
    extra = extra.astype(jnp.bfloat16)
    return jnp.concatenate([part, extra] if head == 0 else [extra, part], axis=0)


def forward_kernel(seq, source, columns, count_in, lengths, me_ref, x_ref, *refs):
    inputs, refs = refs[:count_in], refs[count_in:]
    q_ref, k_ref, v_ref, att_ref, lse_ref, vec_ref, hb_ref = refs[:7]
    qt, vt, ot, weights, sems, small, small_sems = refs[7:]
    length = lengths[seq]
    started = []
    for which in range(3):
        started.append(
            run_all(source.copies(which, inputs, weights.at[which], sems.at[which], me_ref))
        )
    wq_ref, wk_ref, wv_ref = (weights.at[i] for i in range(3))
    if source.spots:
        wait_all(run_all(source.small_copies(inputs, small, small_sems, me_ref)))
        lay_vectors(small[...], columns, hb_ref.shape[1], vec_ref, hb_ref)
    else:
        vec_ref[...] = inputs[-2][...]
        hb_ref[...] = inputs[-1][...]
    x = x_ref[...]
    wait_all(started[0])
    head_size = x.shape[1] // HEADS
    scale = head_size**-0.5
    queries = (dot(x, wq_ref[...]) + vec_ref[0:1, :]).astype(jnp.bfloat16)
    queries = (queries.astype(jnp.float32) * scale).astype(jnp.bfloat16)
    q_ref[...] = queries
    qt[...] = queries.T
    wait_all(started[1])
    k_ref[...] = dot(x, wk_ref[...]).astype(jnp.bfloat16)
    wait_all(started[2])
    values = (dot(x, wv_ref[...]) + vec_ref[1:2, :]).astype(jnp.bfloat16)
    v_ref[...] = values
    vt[...] = values.T

    def one_pair(p, carry):
        base = pl.multiple_of(p * 2 * head_size, 2 * head_size)
        pair = k_ref[:, pl.ds(base, 2 * head_size)]
        for head in range(2):
            at = pl.multiple_of(base + head * head_size, head_size)
            keys = head_keys(pair, head, length, False)
            scores = dot(keys, with_rows(qt[pl.ds(at, head_size), :], head, [1.0]))
            highest = jnp.max(scores, axis=0, keepdims=True)
            exponent = jnp.exp(scores - highest)
            total = jnp.sum(exponent, axis=0, keepdims=True)
            blended = dot(vt[pl.ds(at, head_size), :], exponent.astype(jnp.bfloat16))
            ot[pl.ds(at, head_size), :] = (blended / total).astype(jnp.bfloat16)
            lse_ref[p, head : head + 1, :] = highest + jnp.log(total)
        return carry

    lax.fori_loop(0, HEADS // 2, one_pair, 0, unroll=True)
    att_ref[...] = ot[...].T


def whole(shape):
    return pl.BlockSpec(shape, lambda *_: (0,) * len(shape))


def skip_refs(kernel, first, count, *refs):
    kernel(*refs[:first], *refs[first + count :])


def attend_forward(seq, me, x, lengths, source, vectors, columns, hidden_count, before):
    seqs, slots, width = x.shape
    rows = pl.BlockSpec((None, slots, width), lambda i, *_: (seq, 0, 0))
    low = jax.ShapeDtypeStruct(x.shape, jnp.bfloat16)
    given = (*source.operands, *vectors)
    kernel = functools.partial(forward_kernel, seq, source, columns, len(given))
    known = 3 + len(given)
    small = (max(source.dp_size, 1), SMALL_ROWS, source.spots[0][1] if source.spots else 128)
    return pl.pallas_call(
        functools.partial(skip_refs, kernel, known, len(before)),
        grid_spec=pltpu.PrefetchScalarGridSpec(
            num_scalar_prefetch=2,
            grid=(1,),
            in_specs=[rows]
            + [ANYWHERE] * len(source.operands)
            + [whole(v.shape) for v in vectors]
            + [ANYWHERE] * len(before),
            out_specs=[rows] * 4
            + [
                pl.BlockSpec((None, HEADS // 2, 2, slots), lambda i, *_: (seq, 0, 0, 0)),
                whole((8, width)),
                whole((1, hidden_count)),
            ],
            scratch_shapes=[pltpu.VMEM((width, slots), jnp.bfloat16)] * 3
            + [
                pltpu.VMEM((3, width, width), jnp.bfloat16),
                pltpu.SemaphoreType.DMA((3, source.count((width, width)))),
                pltpu.VMEM(small, jnp.bfloat16),
                pltpu.SemaphoreType.DMA((small[0],)),
            ],
        ),
        out_shape=[low] * 4
        + [
            jax.ShapeDtypeStruct((seqs, HEADS // 2, 2, slots), jnp.float32),
            jax.ShapeDtypeStruct((8, width), jnp.float32),
            jax.ShapeDtypeStruct((1, hidden_count), jnp.float32),
        ],
        input_output_aliases={known + i: i for i in range(len(before))},
        compiler_params=pltpu.CompilerParams(vmem_limit_bytes=VMEM_BYTES),
        cost_estimate=estimate(14),
        name="attend_forward",
    )(lengths, me, x, *given, *before)


def feed_kernel(
    source, cuts, slots, lengths, me_ref, x_ref, att_ref, cot_ref, hb_ref, vec_ref, *refs
):
    count_in = len(source.operands)
    inputs, refs = refs[:count_in], refs[count_in:]
    out_ref, gf_ref, do_ref, hsum_ref, sums_ref = refs[:5]
    (
        wi, wf, wo, act, slope_s, first, mid, mid_t, low_s, held_i, held_o, held_a,
        load_a, load_i, load_o, sems, sems_a,
    ) = refs[-17:]
    grads = refs[5:-17]
    loads = [
        run_all(source.copies(which, inputs, target, sem, me_ref))
        for which, target, sem in ((0, wo, load_a), (1, wi, load_i), (2, wf, load_o))
    ]
    total, width = x_ref.shape
    inner = wi.shape[1]
    tile = min(256, slots)
    piece = min(512, inner)
    sums_ref[...] = jnp.zeros_like(sums_ref)
    wait_all(loads[0])
    first[...] = x_ref[...].astype(jnp.float32) + dot(att_ref[...], wo[...]) + vec_ref[2:3, :]
    for copies in loads[1:]:
        wait_all(copies)

    def forward(t, carry):
        rows = pl.ds(pl.multiple_of(t * tile, tile), tile)
        normed, _ = normalize(first[rows, :])
        middle = normed * vec_ref[4:5, :] + vec_ref[6:7, :]
        middle_low = middle.astype(jnp.bfloat16)
        mid[rows, :] = middle_low
        second = middle + vec_ref[3:4, :]
        def ahead(at):
            return dot(middle_low, wi[:, at : at + piece]) + hb_ref[:, at : at + piece]

        hidden = ahead(0)
        for at in range(0, inner, piece):
            here = slice(at, at + piece)
            following = ahead(at + piece) if at + piece < inner else None
            active, slope = gelu_pair(hidden)
            active = active.astype(jnp.bfloat16)
            act[rows, here] = active
            slope_s[rows, here] = slope.astype(jnp.bfloat16)
            second = second + dot(active, wf[here, :])
            hidden = following
        normed, factor = normalize(second)
        start = t * tile
        slot = start % slots + lax.broadcasted_iota(jnp.int32, (tile, 1), 0)
        mask = (slot < lengths[start // slots]).astype(jnp.float32)
        out_ref[rows, :] = ((normed * vec_ref[5:6, :] + vec_ref[7:8, :]) * mask).astype(jnp.bfloat16)
        upward = cot_ref[rows, :].astype(jnp.float32) * mask
        grad = norm_back(upward * vec_ref[5:6, :], normed, factor)
        gf_ref[rows, :] = grad
        low = grad.astype(jnp.bfloat16)
        low_s[rows, :] = low
        sums_ref[0:1, :] += jnp.sum(upward * normed, axis=0, keepdims=True)
        sums_ref[1:2, :] += jnp.sum(upward, axis=0, keepdims=True)
        sums_ref[2:3, :] += jnp.sum(low.astype(jnp.float32), axis=0, keepdims=True)
        return carry

    lax.fori_loop(0, total // tile, forward, 0, unroll=2)
    mid_t[...] = mid[...].T
    chunk = held_i.shape[2]
    steps = inner // chunk

    def copies(step):
        slot = step % 2
        if cuts is None:
            start = pl.multiple_of(step * chunk, chunk)
            return [
                pltpu.make_async_copy(
                    held_o.at[slot], grads[2].at[pl.ds(start, chunk), :], sems.at[slot, 0]
                ),
                pltpu.make_async_copy(
                    held_i.at[slot], grads[1].at[:, pl.ds(start, chunk)], sems.at[slot, 1]
                ),
            ]
        made, split = [], cuts.split
        blocks = chunk // (2 * split.half_outer)
        for cut, outs, span, columns in cuts.outer(grads, width):
            made += piece_copies(
                held_o.at[slot], outs, sems.at[slot, pl.ds(len(made), 2 * blocks * len(columns))],
                me_ref, cut.stages, step * blocks, blocks, split.half_outer, span, columns,
            )
        for cut, outs, span, columns in cuts.inner(grads, step, chunk):
            made += piece_copies(
                held_i.at[slot], outs, sems.at[slot, pl.ds(len(made), width // split.half)],
                me_ref, cut.stages, 0, width // (2 * split.half), split.half, span, columns,
            )
        return made

    def backward(step, carry):
        here = pl.ds(pl.multiple_of(step * chunk, chunk), chunk)
        low = low_s[...]
        up = dot_last(low, wf[here, :]) * slope_s[:, here].astype(jnp.float32)
        hidden = up.astype(jnp.bfloat16)
        hsum_ref[:, here] = jnp.sum(hidden.astype(jnp.float32), axis=0, keepdims=True)

        @pl.when(step >= 2)
        def _():
            wait_all(copies(step - 2))

        held_o[step % 2] = dot_first(act[:, here], low).astype(jnp.bfloat16)
        held_i[step % 2] = dot(mid_t[...], hidden).astype(jnp.bfloat16)
        run_all(copies(step))
        gf_ref[...] += dot_last(hidden, wi[:, here])
        return carry

    lax.fori_loop(0, steps, backward, 0, unroll=4)

    def finish(t, carry):
        rows = pl.ds(pl.multiple_of(t * tile, tile), tile)
        grad_middle = gf_ref[rows, :]
        normed, factor = normalize(first[rows, :])
        sums_ref[3:4, :] += jnp.sum(grad_middle * normed, axis=0, keepdims=True)
        sums_ref[4:5, :] += jnp.sum(grad_middle, axis=0, keepdims=True)
        grad_first = norm_back(grad_middle * vec_ref[4:5, :], normed, factor)
        gf_ref[rows, :] = grad_first
        branch = grad_first.astype(jnp.bfloat16)
        low_s[rows, :] = branch
        sums_ref[5:6, :] += jnp.sum(branch.astype(jnp.float32), axis=0, keepdims=True)
        do_ref[rows, :] = dot_last(branch, wo[...]).astype(jnp.bfloat16)
        return carry

    lax.fori_loop(0, total // tile, finish, 0, unroll=4)
    held_a[...] = dot_first(att_ref[...], low_s[...]).astype(jnp.bfloat16)
    if cuts is None:
        last = [pltpu.make_async_copy(held_a, grads[0], sems_a.at[0])]
    else:
        cut, outs, span, columns = cuts.output(grads, width)
        half = cuts.split.half
        last = piece_copies(
            held_a, outs, sems_a, me_ref, cut.stages, 0, width // (2 * half), half, span, columns
        )
    run_all(last)
    for step in range(max(0, steps - 2), steps):
        wait_all(copies(step))
    wait_all(last)


class Cut:
    def __init__(self, stages, rows, width):
        self.stages, self.rows, self.width = tuple(stages), rows, width
        self.places = 1 << len(stages)

    def shapes(self):
        return [jax.ShapeDtypeStruct((self.places, self.rows, self.width), jnp.bfloat16)] * 2


class FeedSplit:
    def __init__(self, half, half_outer, width, width_inner):
        self.half, self.half_outer, self.width, self.width_inner = half, half_outer, width, width_inner
        self.most = max(16, half_outer // 6 * 5 // 16 * 16)
        self.rest = half_outer - self.most
        self.folded = half + self.rest

    def spots(self):
        return [
            (self.half, self.width, [(2, 0, 0, self.half, 0)]),
            (self.half, self.width_inner, [(0, 0, 0, self.half, 0)]),
            (
                self.half_outer,
                self.width,
                [(1, 0, 0, self.most, 0), (2, self.half, self.most, self.rest, 0)],
            ),
        ]


class FeedCuts:
    def __init__(self, orders, split):
        self.split = split
        rows = (split.half, split.most, split.folded)
        widths = (split.width_inner, split.width, split.width)
        self.cuts = [Cut(*sizes) for sizes in zip(orders, rows, widths)]

    def shapes(self):
        return [shape for cut in self.cuts for shape in cut.shapes()]

    def inner(self, grads, step, chunk):
        split = self.split
        parts = split.width_inner // chunk
        into = pl.multiple_of(step % parts * chunk, 128)
        return [(self.cuts[0], grads[0:2], (0, split.half, 0), [(0, step // parts, into, chunk)])]

    def outer(self, grads, width):
        split = self.split
        columns = [(p * split.width, p, 0, split.width) for p in range(width // split.width)]
        listed = [(self.cuts[1], grads[2:4], (0, split.most, 0), columns)]
        if split.rest:
            listed.append((self.cuts[2], grads[4:6], (split.most, split.rest, split.half), columns))
        return listed

    def output(self, grads, width):
        split = self.split
        columns = [(p * split.width, p, 0, split.width) for p in range(width // split.width)]
        return self.cuts[2], grads[4:6], (0, split.half, 0), columns


ANYWHERE = pl.BlockSpec(memory_space=pl.ANY)
SCALARS = pl.BlockSpec(memory_space=pltpu.SMEM)
HERE = pl.BlockSpec(memory_space=pltpu.VMEM)


def feed(me, lengths, x, att, cotangent, hidden_bias, vectors, source, cuts):
    seqs, slots, width = x.shape
    inner = hidden_bias.shape[1]
    total = seqs * slots
    chunk = min(768, inner)
    low = jnp.bfloat16
    if cuts is None:
        shapes = ((width, width), (width, inner), (inner, width))
        grads = [jax.ShapeDtypeStruct(shape, low) for shape in shapes]
        copies, copies_last = 2, 1
    else:
        grads = cuts.shapes()
        split = cuts.split
        pairs = width // split.width
        copies = 2 * (chunk // split.half_outer) * pairs
        copies += width // split.half
        copies_last = width // split.half * pairs
    return pl.pallas_call(
        functools.partial(feed_kernel, source, cuts, slots),
        in_specs=[SCALARS, SCALARS] + [HERE] * 5 + [ANYWHERE] * len(source.operands),
        out_specs=[HERE] * 5 + [ANYWHERE] * len(grads),
        out_shape=[
            jax.ShapeDtypeStruct((total, width), low),
            jax.ShapeDtypeStruct((total, width), jnp.float32),
            jax.ShapeDtypeStruct((total, width), low),
            jax.ShapeDtypeStruct((1, inner), jnp.float32),
            jax.ShapeDtypeStruct((8, width), jnp.float32),
            *grads,
        ],
        scratch_shapes=[
            pltpu.VMEM((width, inner), low),
            pltpu.VMEM((inner, width), low),
            pltpu.VMEM((width, width), low),
            pltpu.VMEM((total, inner), low),
            pltpu.VMEM((total, inner), low),
            pltpu.VMEM((total, width), jnp.float32),
            pltpu.VMEM((total, width), low),
            pltpu.VMEM((width, total), low),
            pltpu.VMEM((total, width), low),
            pltpu.VMEM((2, width, chunk), low),
            pltpu.VMEM((2, chunk, width), low),
            pltpu.VMEM((width, width), low),
            pltpu.SemaphoreType.DMA((source.pick([0]).count((width, width)),)),
            pltpu.SemaphoreType.DMA((source.pick([1]).count((width, inner)),)),
            pltpu.SemaphoreType.DMA((source.pick([2]).count((inner, width)),)),
            pltpu.SemaphoreType.DMA((2, copies)),
            pltpu.SemaphoreType.DMA((copies_last,)),
        ],
        compiler_params=pltpu.CompilerParams(vmem_limit_bytes=FEED_BYTES),
        cost_estimate=estimate(60),
        name="feed",
    )(
        lengths, me, x.reshape(total, width), att.reshape(total, width),
        cotangent.reshape(total, width), hidden_bias, vectors, *source.operands,
    )


def backward_kernel(
    seq, head_size, lengths, do_ref, q_ref, k_ref, v_ref, att_ref, lse_ref, *rest
):
    dq_ref, dk_ref, dv_ref, qt, kt, at_t, do_t, dq_t = rest
    length = lengths[seq]
    width = q_ref.shape[1]
    scale = head_size**-0.5
    at_t[...] = att_ref[...].T
    do_t[...] = do_ref[...].T
    qt[...] = q_ref[...].T
    kt[...] = k_ref[...].T

    def one_pair(p, carry):
        base = pl.multiple_of(p * 2 * head_size, 2 * head_size)
        here = pl.ds(base, 2 * head_size)
        key_pair, value_pair = k_ref[:, here], v_ref[:, here]
        query_pair, up_pair = q_ref[:, here], do_ref[:, here]
        grad_keys = grad_values = None
        for head in range(2):
            at = pl.multiple_of(base + head * head_size, head_size)
            mine = pl.ds(at, head_size)
            logs = [-part for part in three_parts(lse_ref[p, head : head + 1, :])]
            keys = head_keys(key_pair, head, length, True)
            soft = jnp.exp(dot(keys, with_rows(qt[mine, :], head, [1.0] + logs)))
            up = do_t[mine, :]
            delta = jnp.sum(
                up.astype(jnp.float32) * at_t[mine, :].astype(jnp.float32), axis=0, keepdims=True
            )
            deltas = [-part for part in three_parts(delta)]
            grad_soft = dot(head_values(value_pair, head), with_rows(up, head, deltas))
            scores = (soft * grad_soft).astype(jnp.bfloat16)
            from_values = dot(soft.astype(jnp.bfloat16), only_head(up_pair, head))
            from_keys = dot(scores, only_head(query_pair, head))
            grad_values = from_values if head == 0 else grad_values + from_values
            grad_keys = from_keys if head == 0 else grad_keys + from_keys
            dq_t[mine, :] = (dot(kt[mine, :], scores) * scale).astype(jnp.bfloat16)
        dk_ref[:, here] = grad_keys.astype(jnp.bfloat16)
        dv_ref[:, here] = grad_values.astype(jnp.bfloat16)
        return carry

    lax.fori_loop(0, width // (2 * head_size), one_pair, 0, unroll=True)
    dq_ref[...] = dq_t[...].T


def attend_backward(seq, part, parts, do, q, k, v, att, lse, lengths, before):
    seqs, slots, width = q.shape
    count = width // parts
    pairs = HEADS // 2 // parts
    rows = pl.BlockSpec((None, slots, count), lambda i, *_: (seq, 0, part))
    low = jax.ShapeDtypeStruct(q.shape, jnp.bfloat16)
    inputs = (lengths, do, q, k, v, att, lse)
    kernel = functools.partial(backward_kernel, seq, width // HEADS)
    return pl.pallas_call(
        functools.partial(skip_refs, kernel, len(inputs), len(before)),
        grid_spec=pltpu.PrefetchScalarGridSpec(
            num_scalar_prefetch=1,
            grid=(1,),
            in_specs=[rows] * 5
            + [pl.BlockSpec((None, pairs, 2, slots), lambda i, *_: (seq, part, 0, 0))]
            + [ANYWHERE] * len(before),
            out_specs=[rows] * 3,
            scratch_shapes=[pltpu.VMEM((count, slots), jnp.bfloat16)] * 5,
        ),
        out_shape=[low, low, low],
        input_output_aliases={len(inputs) + i: i for i in range(len(before))},
        compiler_params=pltpu.CompilerParams(vmem_limit_bytes=VMEM_BYTES),
        cost_estimate=estimate(14 // parts),
        name="attend_backward",
    )(*inputs, *before)


def pack_gradients(sums_feed, sums_in, hsum, small, columns):
    parts, _, lanes = small.shape
    lanes = min(128, lanes)
    width, share = sums_feed.shape[1], hsum.shape[1] // parts
    rows = share // columns

    def chosen(count, start):
        row = lax.broadcasted_iota(jnp.int32, (count, lanes), 0)
        column = lax.broadcasted_iota(jnp.int32, (count, lanes), 1)
        return ((row - start == column) & (column < columns)).astype(jnp.float32).astype(jnp.bfloat16)

    small[...] = jnp.zeros_like(small)
    listed = (
        [*sums_in, sums_feed[5:6], sums_feed[2:3]]
        + [jnp.zeros((rows, width), jnp.float32)]
        + [sums_feed[3:4], sums_feed[0:1], sums_feed[4:5], sums_feed[1:2]]
    )
    pad = SMALL_ROWS - 8 - rows
    lined = jnp.concatenate(listed + [jnp.zeros((pad, width), jnp.float32)], axis=0)
    lined = lined.astype(jnp.bfloat16)
    hidden = [hsum[:, dp * share : (dp + 1) * share] for dp in range(parts)]
    hidden = jnp.concatenate(hidden, axis=0).astype(jnp.bfloat16)
    spread = [dot(hidden, chosen(share, k * columns)) for k in range(rows)]
    for dp in range(parts):
        here = dot(lined, chosen(width, dp * columns))
        own = [spread[k][dp : dp + 1] for k in range(rows)]
        here = jnp.concatenate([here[:4]] + own + [here[4 + rows :]], axis=0)
        small[dp, :, 0:lanes] = here.astype(jnp.bfloat16)


def project_grads_kernel(
    cuts, columns, me_ref, x_ref, dq_ref, dk_ref, dv_ref, sums_feed, hsum, *rest
):
    xt, held, small, sems = rest[-4:]
    outs = rest[:-4]
    xt[...] = x_ref[...].T
    started = []
    for which, ref in enumerate((dq_ref, dk_ref, dv_ref)):
        held[which] = dot(xt[...], ref[...]).astype(jnp.bfloat16)
        if cuts is None:
            outs[which][...] = held[which]
            continue
        width, half, third = held.shape[2], (cuts[0].rows + cuts[1].rows - SMALL_ROWS) // 3, 0
        third = cuts[0].rows - SMALL_ROWS - half
        spans = [(0, 0, half, 0)], [(1, 0, half, 0)], [(0, 0, third, half), (1, third, half - third, half)]
        used = 0
        for i, offset, count, at in spans[which]:
            if count == 0:
                continue
            cut = cuts[i]
            ends = [(p * cut.width, p, 0, cut.width) for p in range(width // cut.width)]
            made = piece_copies(
                held.at[which], outs[2 * i : 2 * i + 2],
                sems.at[which, pl.ds(used, width // half * len(ends))],
                me_ref, cut.stages, 0, width // (2 * half), half, (offset, count, at), ends,
            )
            used += len(made)
            started += run_all(made)
    if cuts is not None:
        sums_in = [
            jnp.sum(ref[...].astype(jnp.float32), axis=0, keepdims=True) for ref in (dq_ref, dv_ref)
        ]
        pack_gradients(sums_feed[...], sums_in, hsum[...], small, columns)
        started += run_all(
            small_copies(
                small, outs[:2], sems.at[3], me_ref, cuts[0].stages, cuts[0].rows - SMALL_ROWS, small.shape[0],
                held.shape[2] // cuts[0].width,
            )
        )
    wait_all(started)


def project_grads(me, x, dq, dk, dv, sums, cuts, dp_size, columns):
    total, width = x.shape
    grad = jax.ShapeDtypeStruct((width, width), jnp.bfloat16)
    direct = cuts is not None
    copies = 4 * dp_size * (width // cuts[0].width) if direct else 1
    piece = cuts[0].width if direct else 128
    return pl.pallas_call(
        functools.partial(project_grads_kernel, cuts, columns),
        in_specs=[SCALARS] + [HERE] * 6,
        out_specs=[ANYWHERE] * 4 if direct else [HERE] * 3,
        out_shape=[shape for cut in cuts for shape in cut.shapes()] if direct else [grad] * 3,
        scratch_shapes=[
            pltpu.VMEM((width, total), jnp.bfloat16),
            pltpu.VMEM((3, width, width), jnp.bfloat16),
            pltpu.VMEM((dp_size if direct else 1, SMALL_ROWS, piece), jnp.bfloat16),
            pltpu.SemaphoreType.DMA((4, copies)),
        ],
        compiler_params=pltpu.CompilerParams(vmem_limit_bytes=VMEM_BYTES),
        cost_estimate=estimate(8),
        name="project_grads",
    )(me, x, dq, dk, dv, *sums)


def input_grad_kernel(source, me_ref, gf_ref, dq_ref, dk_ref, dv_ref, *refs):
    inputs, (out_ref, weights, sems) = refs[:-3], refs[-3:]
    started = [
        run_all(source.copies(i, inputs, weights.at[i], sems.at[i], me_ref)) for i in range(3)
    ]
    grad = gf_ref[...]
    for i, ref in enumerate((dq_ref, dk_ref, dv_ref)):
        wait_all(started[i])
        grad = grad + dot_last(ref[...], weights[i])
    out_ref[...] = grad.astype(jnp.bfloat16)


def input_grads(me, gf, dq, dk, dv, source):
    total, width = dq.shape
    return pl.pallas_call(
        functools.partial(input_grad_kernel, source),
        in_specs=[SCALARS] + [HERE] * 4 + [ANYWHERE] * len(source.operands),
        out_specs=HERE,
        out_shape=jax.ShapeDtypeStruct((total, width), jnp.bfloat16),
        scratch_shapes=[
            pltpu.VMEM((3, width, width), jnp.bfloat16),
            pltpu.SemaphoreType.DMA((3, source.count((width, width)))),
        ],
        compiler_params=pltpu.CompilerParams(vmem_limit_bytes=VMEM_BYTES),
        cost_estimate=estimate(8),
        name="input_grads",
    )(me, gf, dq, dk, dv, *source.operands)


def after(values, *others):
    return lax.optimization_barrier((values, others))[0]


def meet(values, parts):
    values, arriving = lax.optimization_barrier((values, [part.arriving for part in parts]))
    for part, value in zip(parts, arriving):
        part.arriving = value
    return values


class Attention:
    def __init__(self, me, inputs, lengths, source, given, columns, hidden_count):
        self.me, self.inputs, self.lengths, self.source = me, inputs, lengths, source
        self.given, self.sizes = given, (columns, hidden_count)
        self.state, self.back = (), ()

    def forward(self, seq):
        *state, self.vectors, self.hidden_bias = attend_forward(
            seq, self.me, self.inputs, self.lengths, self.source, self.given, *self.sizes, self.state
        )
        self.state = tuple(state)

    def backward(self, seq, part, parts, do):
        self.back = tuple(
            attend_backward(seq, part, parts, do, *self.state, self.lengths, self.back)
        )


def layer_step(inputs, lengths, upstream, gather, scatter):
    shape = inputs.shape
    flat = (shape[0] * shape[1], shape[2])
    seqs = shape[0]
    source, given = gather.first()
    bias, hidden = gather.shards[6:8]
    me = gather.me
    columns = bias.shape[1]
    attention = Attention(
        me, inputs, lengths, source, given, columns, hidden.shape[0] * scatter.dp_size
    )
    for seq in range(seqs):
        attention.inputs = gather.before(seq, attention.inputs)
        attention.forward(seq)
        attention.state = gather.after(seq, attention.state)
    outputs, gf, do, hidden_sum, sums_feed, *grads = feed(
        me, lengths, inputs, attention.state[3], upstream, attention.hidden_bias,
        attention.vectors, gather.second(), scatter.feed_cuts,
    )
    parts = 2
    scatter.feed(grads)
    for at in range(seqs * parts):
        attention.backward(at // parts, at % parts, parts, do.reshape(shape))
        attention.back = scatter.step(at, attention.back)
    dq, dk, dv = (grad.reshape(flat) for grad in attention.back)
    sums = (sums_feed, hidden_sum)
    scatter.ends = (dq, dv)
    results = project_grads(
        me, inputs.reshape(flat), dq, dk, dv, sums, scatter.first_cuts, scatter.dp_size, columns
    )
    gf = scatter.last(results, sums, gf)
    input_grad = input_grads(me, gf, dq, dk, dv, source)
    input_grad, totals = scatter.totals(input_grad)
    return outputs.reshape(shape), input_grad.reshape(shape), totals


def split_up(value, dim, size):
    before, after = (value.shape[:dim], value.shape[dim + 1 :])
    return jnp.moveaxis(value.reshape(*before, size, -1, *after), dim, 0)


def sum_at_owner(value, axis, dim):
    size = lax.axis_size(axis)
    parts = lax.all_to_all(split_up(value, dim, size), axis, 0, 0, tiled=True)
    return jnp.sum(parts.astype(jnp.float32), axis=0)


def side_by_side(arrays, axis, dim, along):
    ends, at = ([], 0)
    for a in arrays[:-1]:
        at += a.shape[along]
        ends.append(at)
    both = jnp.concatenate(arrays, axis=along)
    return tuple(jnp.split(sum_at_owner(both, axis, dim), ends, axis=along))


def gather_forward(shards):
    (
        query_part,
        key_part,
        value_part,
        output_part,
        inner_part,
        outer_part,
        bias_part,
        hidden_part,
        gain_part,
        shift_part,
    ) = shards
    column_full = (
        lax.all_gather(query_part, "fsdp", axis=1, tiled=True),
        lax.all_gather(key_part, "fsdp", axis=1, tiled=True),
        lax.all_gather(value_part, "fsdp", axis=1, tiled=True),
        lax.all_gather(output_part, "fsdp", axis=1, tiled=True),
        lax.all_gather(inner_part, "fsdp", axis=1, tiled=True),
        lax.all_gather(outer_part, "fsdp", axis=1, tiled=True),
    )
    return (
        lax.all_gather(column_full[0], "dp", axis=0, tiled=True),
        lax.all_gather(column_full[1], "dp", axis=0, tiled=True),
        lax.all_gather(column_full[2], "dp", axis=0, tiled=True),
        lax.all_gather(column_full[3], "dp", axis=0, tiled=True),
        lax.all_gather(column_full[4], "dp", axis=0, tiled=True),
        lax.all_gather(column_full[5], "dp", axis=0, tiled=True),
        lax.all_gather(bias_part, "dp", axis=1, tiled=True),
        lax.all_gather(hidden_part, "dp", axis=0, tiled=True),
        lax.all_gather(gain_part, "dp", axis=1, tiled=True),
        lax.all_gather(shift_part, "dp", axis=1, tiled=True),
    )


def reduce_grads(grads):
    (
        query_grad,
        key_grad,
        value_grad,
        output_grad,
        inner_grad,
        outer_grad,
        bias_grad,
        hidden_grad,
        gain_grad,
        shift_grad,
    ) = grads
    bias_grad, hidden_grad, gain_grad, shift_grad = (
        lax.psum(bias_grad.astype(jnp.bfloat16), "fsdp").astype(jnp.float32),
        lax.psum(hidden_grad.astype(jnp.bfloat16), "fsdp").astype(jnp.float32),
        lax.psum(gain_grad.astype(jnp.bfloat16), "fsdp").astype(jnp.float32),
        lax.psum(shift_grad.astype(jnp.bfloat16), "fsdp").astype(jnp.float32),
    )
    narrow = (
        lax.psum_scatter(
            query_grad.astype(jnp.bfloat16), "fsdp", scatter_dimension=1, tiled=True
        ).astype(jnp.float32),
        lax.psum_scatter(
            key_grad.astype(jnp.bfloat16), "fsdp", scatter_dimension=1, tiled=True
        ).astype(jnp.float32),
        lax.psum_scatter(
            value_grad.astype(jnp.bfloat16), "fsdp", scatter_dimension=1, tiled=True
        ).astype(jnp.float32),
        lax.psum_scatter(
            output_grad.astype(jnp.bfloat16), "fsdp", scatter_dimension=1, tiled=True
        ).astype(jnp.float32),
        lax.psum_scatter(
            inner_grad.astype(jnp.bfloat16), "fsdp", scatter_dimension=1, tiled=True
        ).astype(jnp.float32),
        lax.psum_scatter(
            outer_grad.astype(jnp.bfloat16), "fsdp", scatter_dimension=1, tiled=True
        ).astype(jnp.float32),
    )
    return (
        *side_by_side(
            (
                narrow[0].astype(jnp.bfloat16),
                narrow[1].astype(jnp.bfloat16),
                narrow[2].astype(jnp.bfloat16),
                narrow[3].astype(jnp.bfloat16),
                narrow[4].astype(jnp.bfloat16),
            ),
            "dp",
            0,
            1,
        ),
        sum_at_owner(narrow[5].astype(jnp.bfloat16), "dp", 0),
        sum_at_owner(bias_grad.astype(jnp.bfloat16), "dp", 1),
        sum_at_owner(hidden_grad.astype(jnp.bfloat16), "dp", 0),
        *side_by_side(
            (gain_grad.astype(jnp.bfloat16), shift_grad.astype(jnp.bfloat16)), "dp", 1, 0
        ),
    )


def pack_small(bias, hidden, gains, shifts, width):
    columns = bias.shape[-1]
    rows = jnp.concatenate([bias, hidden.reshape(-1, columns), gains, shifts], axis=0)
    return jnp.pad(rows, ((0, SMALL_ROWS - rows.shape[0]), (0, width - columns)))


class Gather:
    def __init__(self, mesh, shards, me):
        self.mesh, self.shards, self.me = mesh, shards, me
        self.orders = stage_orders(mesh)

    def prepare(self):
        query, key, value, output, inner, outer, bias, hidden, gains, shifts = self.shards
        half, half_outer = query.shape[0] // 2, outer.shape[0] // 2
        small = pack_small(bias, hidden, gains, shifts, 2 * query.shape[1])

        def both(*arrays):
            halves = [array[: array.shape[0] // 2] for array in arrays]
            halves += [array[array.shape[0] // 2 :] for array in arrays]
            return jnp.concatenate(halves, axis=0)

        one, rest, inner = pair_up((both(query, key, value), both(output, outer), inner))
        third = third_of(half)
        self.one = [one[:half], one[2 * half : 2 * half + third], small]
        self.cut_at = sum(part.shape[0] for part in self.one)
        self.one += [one[half : 2 * half], one[2 * half + third :]]
        self.one = [jnp.concatenate(self.one, axis=0)[None]]
        split = self.split = FeedSplit(half, half_outer, 2 * query.shape[1], inner.shape[1])
        self.two = [
            inner[None],
            rest[half : half + split.most][None],
            jnp.concatenate([rest[:half], rest[half + split.most :]], axis=0)[None],
        ]

    def send(self, parts, stage):
        return [swap(part, *self.orders[i][stage]) for i, part in enumerate(parts)]

    def join(self, parts, received):
        return [jnp.concatenate(pair, axis=0) for pair in zip(parts, received)]

    def first(self):
        self.prepare()
        count, far = len(self.orders[0]), far_stages(self.mesh)
        self.stage = 0
        for stage in range(far):
            self.one = self.join(self.one, self.send(self.one, stage))
        joined = self.one[0]
        self.one = [joined[:, : self.cut_at], joined[:, self.cut_at :]]
        for stage in range(far, count):
            arriving = self.send(self.one, stage)
            self.two = after(self.two, self.one)
            ahead = self.send(self.two, self.stage)
            self.stage += 1
            self.one = self.join(self.one, arriving)
            self.two = self.join(self.two, after(ahead, self.one))
        self.two = after(self.two, self.one)
        others = [swap(part, "fsdp", 0) for part in self.one]
        half, width = self.shards[0].shape[0] // 2, self.one[0].shape[2]
        third = third_of(half)
        thirds = [(0, half, 0, third, 0), (1, half, third, half - third, 0)]
        spots = [(half, width, [(0, 0, 0, half, 0)]), (half, width, [(1, 0, 0, half, 0)]), (half, width, thirds)]
        operands = [array for pair in zip(self.one, others) for array in pair]
        return Source(operands, self.orders, spots, self.mesh.shape["dp"], half + third), ()

    def before(self, seq, inputs):
        if self.stage == len(self.orders[0]):
            return inputs
        self.arriving = self.send(self.two, self.stage)
        self.stage += 1
        return after(inputs, self.two)

    def after(self, seq, state):
        if self.arriving is None:
            return state
        arriving = after(self.arriving, state)
        self.two, self.arriving = self.join(self.two, arriving), None
        return state

    def second(self):
        while self.stage < len(self.orders[0]):
            self.two = self.join(self.two, self.send(self.two, self.stage))
            self.stage += 1
        others = [swap(part, "fsdp", 0) for part in self.two]
        operands = [array for pair in zip(self.two, others) for array in pair]
        return Source(operands, self.orders, self.split.spots(), self.mesh.shape["dp"])


class Part:
    def __init__(self, keep, send, stages):
        self.keep, self.stages = keep, list(stages)
        self.arriving = swap(send, "fsdp", 0)

    def step(self):
        axis, bit = self.stages.pop()
        half = self.keep.shape[0] // 2
        send = total_of(self.keep[half:], self.arriving[half:], jnp.bfloat16)
        arriving = swap(send, axis, bit)
        self.keep = total_of(self.keep[:half], self.arriving[:half], jnp.bfloat16)
        self.arriving = arriving
        return send

    def join(self, other):
        both = Part.__new__(Part)
        both.keep = jnp.concatenate([self.keep, other.keep], axis=1)
        both.arriving = jnp.concatenate([self.arriving, other.arriving], axis=1)
        both.stages = list(self.stages)
        return both

    def finish(self):
        while self.stages:
            self.step()
        return total_of(self.keep, self.arriving, jnp.float32)[0]


class Scatter:
    def __init__(self, mesh, shards, me):
        self.shards = shards
        self.orders = stage_orders(mesh)
        width, width_inner = 2 * shards[0].shape[1], 2 * shards[4].shape[1]
        half, half_outer = shards[0].shape[0] // 2, shards[5].shape[0] // 2
        self.dp_size = mesh.shape["dp"]
        self.split = FeedSplit(half, half_outer, width, width_inner)
        self.feed_cuts = FeedCuts(self.orders, self.split)
        self.third = third_of(half)
        self.far = far_stages(mesh)
        rows = (half + self.third + SMALL_ROWS, 2 * half - self.third)
        self.first_cuts = [Cut(order, r, width) for order, r in zip(self.orders, rows)]

    def feed(self, grads):
        self.behind = [
            Part(*grads[2 * i : 2 * i + 2], cut.stages) for i, cut in enumerate(self.feed_cuts.cuts)
        ]

    def step(self, at, state):
        parts = {0: self.behind, 2: self.behind[2:], 3: self.behind[:2]}.get(at, [])
        if not parts:
            return state
        state = meet(state, parts)
        return after(state, [part.step() for part in parts])

    def last(self, results, sums, passing):
        results = meet(results, self.behind)
        self.front = [
            Part(*results[2 * i : 2 * i + 2], cut.stages) for i, cut in enumerate(self.first_cuts)
        ]
        sent = [part.step() for part in self.behind]
        meet((), self.front)
        sent += [part.step() for part in self.front]
        return after(passing, sent)

    def totals(self, passing):
        half, half_outer = self.shards[0].shape[0] // 2, self.shards[5].shape[0] // 2
        columns = self.shards[6].shape[1]
        parts, front = self.front + self.behind, self.front
        passing = meet(passing, parts)
        while len(front[0].stages) > self.far:
            sent = [part.step() for part in front]
            for part in self.behind:
                if part.stages:
                    part.arriving = after(part.arriving, sent)
                    part.step()
            meet((), front)
        joint = front[0].join(front[1])
        cut_at = front[0].keep.shape[1]
        sent = [joint.step()] if joint.stages else []
        for part in self.behind:
            part.arriving = after(part.arriving, sent)
        inner, outer, rest = [part.finish() for part in self.behind]
        split = self.split
        outer = jnp.concatenate([outer, rest[half : split.folded]], axis=0)
        settled = settle(jnp.concatenate([rest[:half], outer]), (half, half_outer)) + settle(inner, (half,))
        output, outer, inner = meet(settled, [joint])
        total = joint.finish()
        one, two, third = total[:cut_at], total[cut_at:], self.third
        thirds = [one[half : half + third], two[half:]]
        query, key, value = settle(jnp.concatenate([one[:half], two[:half], *thirds]), (half,) * 3)
        rows = one[half + third :, :columns]
        split = 4 + self.shards[7].shape[0] // columns
        return passing, (
            query, key, value, output, inner, outer,
            rows[:4], rows[4:split].reshape(-1), rows[split : split + 2], rows[split + 2 : split + 4],
        )


class PlainGather:
    def __init__(self, mesh, shards, me):
        self.shards, self.me = shards, me

    def first(self):
        arrays = gather_forward(self.shards)
        self.rest = arrays[3:6]
        bias, hidden, gains, shifts = arrays[6:]
        vectors = jnp.concatenate([bias, gains, shifts], axis=0).astype(jnp.float32)
        return Source(arrays[:3]), (vectors, hidden.astype(jnp.float32)[None])

    def before(self, seq, inputs):
        return inputs

    def after(self, seq, state):
        return state

    def second(self):
        return Source(self.rest)


class PlainScatter:
    def __init__(self, mesh, shards, me):
        self.feed_cuts = self.first_cuts = None
        self.dp_size = mesh.shape["dp"]

    def feed(self, grads):
        self.grads = grads

    def step(self, at, state):
        return state

    def last(self, results, sums, passing):
        (feed, hidden), (dq, dv) = sums, self.ends
        ends = [jnp.sum(d.astype(jnp.float32), axis=0, keepdims=True) for d in (dq, dv)]
        bias = jnp.concatenate([*ends, feed[5:6], feed[2:3]], axis=0)
        gains = jnp.concatenate([feed[3:4], feed[:1]], axis=0)
        shifts = jnp.concatenate([feed[4:5], feed[1:2]], axis=0)
        self.grads = (*results, *self.grads, bias, hidden[0], gains, shifts)
        return passing

    def totals(self, passing):
        return passing, reduce_grads(self.grads)


def on_device(
    mesh,
    tokens,
    lengths,
    cotangent,
    *shards,
):
    me = jnp.stack([lax.axis_index("dp"), lax.axis_index("fsdp")]).astype(jnp.int32)
    rows = (shards[0].shape[0], shards[5].shape[0])
    direct = fits(mesh, rows, shards[0].shape[1], shards[7].shape[0])
    gather = (Gather if direct else PlainGather)(mesh, shards, me)
    scatter = (Scatter if direct else PlainScatter)(mesh, shards, me)
    shape = (-1, *tokens.shape[2:])
    outputs, grad_inputs, totals = layer_step(
        tokens.reshape(shape), lengths.reshape(-1), cotangent.reshape(shape), gather, scatter
    )
    return (outputs.reshape(tokens.shape), grad_inputs.reshape(tokens.shape), *totals)


def solution(mesh):
    placed = (
        P(None, ("dp", "fsdp"), None, None),
        P(None, ("dp", "fsdp")),
        P(None, ("dp", "fsdp"), None, None),
        P("dp", "fsdp"),
        P("dp", "fsdp"),
        P("dp", "fsdp"),
        P("dp", "fsdp"),
        P("dp", "fsdp"),
        P("dp", "fsdp"),
        P(None, "dp"),
        P("dp"),
        P(None, "dp"),
        P(None, "dp"),
    )
    return jax.shard_map(
        functools.partial(on_device, mesh),
        mesh=mesh,
        in_specs=placed,
        out_specs=(
            P(None, ("dp", "fsdp"), None, None),
            P(None, ("dp", "fsdp"), None, None),
            P("dp", "fsdp"),
            P("dp", "fsdp"),
            P("dp", "fsdp"),
            P("dp", "fsdp"),
            P("dp", "fsdp"),
            P("dp", "fsdp"),
            P(None, "dp"),
            P("dp"),
            P(None, "dp"),
            P(None, "dp"),
        ),
        check_vma=False,
    )
```
